128 devices in a mesh: seq: 64 (over y, z_lo, x, core), tp: 2 (over z_hi).
Axes of the slice: x: 4, y: 4, z: 4 (z_hi: 2, z_lo: 2; z = z_hi * 2 + z_lo), core: 2. Of those that a mesh axis runs over, the one named last changes fastest.
Arguments:
- hidden_in: bfloat16 [16384, 2048], P('seq'), may hold values from -16 to 16
- attn_gain: float32 [2048], P('seq'), may hold values from 0.1 to 1.9
- w_query: float32 [2048, 2048], P('seq', 'tp'), may hold values from -0.25 to 0.25
- w_key: float32 [2048, 2048], P('seq', 'tp'), may hold values from -0.125 to 0.125
- w_value: float32 [2048, 2048], P('seq', 'tp'), may hold values from -0.125 to 0.125
- w_out: float32 [2048, 2048], P('tp', 'seq'), may hold values from -0.5 to 0.5
- ffn_gain: float32 [2048], P('seq'), may hold values from 0.1 to 1.9
- w_gate: float32 [2048, 5504], P('seq', 'tp'), may hold values from -0.125 to 0.125
- w_up: float32 [2048, 5504], P('seq', 'tp'), may hold values from -0.125 to 0.125
- w_down: float32 [5504, 2048], P('tp', 'seq'), may hold values from -0.15625 to 0.15625
- out_grad: bfloat16 [16384, 2048], P('seq'), may hold values from -16 to 16
Outputs:
- hidden_out: bfloat16 [16384, 2048], P('seq')
- in_grad: float32 [16384, 2048], P('seq')
- attn_gain_grad: float32 [2048], P('seq')
- w_query_grad: float32 [2048, 2048], P('seq', 'tp')
- w_key_grad: float32 [2048, 2048], P('seq', 'tp')
- w_value_grad: float32 [2048, 2048], P('seq', 'tp')
- w_out_grad: float32 [2048, 2048], P('tp', 'seq')
- ffn_gain_grad: float32 [2048], P('seq')
- w_gate_grad: float32 [2048, 5504], P('seq', 'tp')
- w_up_grad: float32 [2048, 5504], P('seq', 'tp')
- w_down_grad: float32 [5504, 2048], P('tp', 'seq')
The draws below stay inside these ranges and needn't reach their ends.
All inputs are finite; a program needn't handle non-finite values.
Results may differ from the reference program's by a relative error of at most 0.017.
The reference program's roundings to bfloat16 on the way count: a program that leaves them out, or rounds other values in their place, can miss the bound.
Values may be sent and summed in bfloat16 or wider, within the bound.
A program may use at most 256 MiB of HBM per device.

```python
import math
import jax
import jax.numpy as jnp
from jax import lax

D = 2048
HEADS = 16
HD = 128
FF = 5504
WINDOW = 1024
SEQLEN = 16384
TOKENS = 16384


def strengthened(array, stream_key, source, target, shards_of, factor):
    owner, partner = [(jnp.arange(array.shape[dim]) // (array.shape[dim] // shards_of)).reshape([-1 if axis == dim else 1 for axis in range(array.ndim)]) for dim in (source, target)]
    chosen = jax.random.permutation(stream_key, shards_of)[partner]
    strong = (owner == chosen) | (owner == (partner + shards_of // 2) % shards_of)
    return jnp.where(strong, factor * array, array)


def block_levels(rng, dims, cuts, smallest, largest):
    level, own = 1.0, jax.random.fold_in(rng, 6)
    for dim, blocks in cuts:
        heights = jnp.exp(jax.random.uniform(jax.random.fold_in(own, dim), (blocks,), jnp.float32, smallest / len(cuts), largest / len(cuts)))
        level = level * jnp.repeat(heights, dims[dim] // blocks).reshape([-1 if axis == dim else 1 for axis in range(len(dims))])
    return level


def gaussian(stream_key, shape, deviation, reach, cuts=(), held_as=jnp.bfloat16):
    values = jax.random.normal(stream_key, shape, jnp.float32) * deviation
    if len(cuts) > 0:
        values = block_levels(stream_key, shape, cuts, -0.22, 0.18) * values
    return jnp.clip(values, min=-reach, max=reach).astype(held_as)


def gaussian_with(rng, shape, scale, limit, cuts, heavy, held_as=jnp.bfloat16):
    values = scale * jax.random.normal(rng, shape, jnp.float32)
    if cuts:
        values = values * block_levels(rng, shape, cuts, -0.22, 0.18)
    return jnp.clip(strengthened(values, jax.random.fold_in(rng, 3), *heavy), -limit, limit).astype(held_as)


def setup_inputs(seed: int = 0) -> dict:
    key_of = jax.random.split(jax.random.key(seed), 12)
    hidden_in = gaussian_with(key_of[0], (TOKENS, D), 1.0, 16.0, ((0, 64),), (0, 1, 64, 4.0))
    attn_gain = jnp.clip(1.0 + 0.18 * jax.random.normal(key_of[1], (D,), jnp.float32), 0.1, 1.9)
    w_query = gaussian(key_of[2], (D, D), (D // 4) ** -0.5, 0.25, ((0, 64), (1, 2)), jnp.float32)
    w_key = gaussian(key_of[3], (D, D), D ** -0.5, 0.125, ((0, 64), (1, 2)), jnp.float32)
    w_value = gaussian(key_of[4], (D, D), D ** -0.5, 0.125, ((0, 64), (1, 2)), jnp.float32)
    w_out = gaussian(key_of[5], (D, D), (D // 16) ** -0.5, 0.5, ((0, 2), (1, 64)), jnp.float32)
    ffn_gain = jnp.clip(1.0 + 0.18 * jax.random.normal(key_of[6], (D,), jnp.float32), 0.1, 1.9)
    w_gate = gaussian(key_of[7], (D, FF), D ** -0.5, 0.125, ((0, 64), (1, 2)), jnp.float32)
    w_up = gaussian(key_of[8], (D, FF), D ** -0.5, 0.125, ((0, 64), (1, 2)), jnp.float32)
    w_down = gaussian(key_of[9], (FF, D), (FF // 4) ** -0.5, 0.15625, ((0, 2), (1, 64)), jnp.float32)
    out_grad = gaussian_with(key_of[10], (TOKENS, D), 1.0, 16.0, ((0, 64),), (0, 1, 64, 4.0))
    return dict(hidden_in=hidden_in, attn_gain=attn_gain, w_query=w_query, w_key=w_key, w_value=w_value, w_out=w_out, ffn_gain=ffn_gain, w_gate=w_gate, w_up=w_up, w_down=w_down, out_grad=out_grad)


EPSILON = 1e-06
MASKED = -1e+30

@jax.custom_vjp
def low(v):
    return lax.optimization_barrier(v.astype(jnp.bfloat16)).astype(jnp.float32)

@jax.custom_vjp
def low_back(v):
    return v

def low_keep(v):
    return (low(v), None)

def low_pass(kept, grad):
    return (grad,)

def back_keep(v):
    return (v, None)

def back_low(kept, grad):
    return (low(grad),)
low.defvjp(low_keep, low_pass)
low_back.defvjp(back_keep, back_low)

def both_ways(value):
    return low(low_back(value))

def matmul(left, right):
    return jnp.dot(left, right, precision=lax.Precision.HIGHEST)

def rms_scale(values, gain):
    inverse = lax.rsqrt(lax.optimization_barrier(jnp.mean(values * values, axis=-1, keepdims=True)) + EPSILON)
    return values * inverse * gain

def window_head(operands):
    queries, keys, values = operands
    padding = jnp.zeros((WINDOW, HD), keys.dtype)
    keys_padded = jnp.concatenate([padding, keys], axis=0)
    values_padded = jnp.concatenate([padding, values], axis=0)

    def one_block(index):
        start = index * WINDOW
        query_part = lax.dynamic_slice_in_dim(queries, start, WINDOW, 0)
        key_part = lax.dynamic_slice_in_dim(keys_padded, start, 2 * WINDOW, 0)
        value_part = lax.dynamic_slice_in_dim(values_padded, start, 2 * WINDOW, 0)
        scores = low_back(matmul(query_part, key_part.T) * (1.0 / math.sqrt(HD)))
        query_pos = start + jnp.arange(WINDOW, dtype=jnp.int32)
        key_pos = start - WINDOW + jnp.arange(2 * WINDOW, dtype=jnp.int32)
        distance = query_pos[:, None] - key_pos[None, :]
        allowed = (distance >= 0) & (distance < WINDOW) & (key_pos[None, :] >= 0)
        scores = jnp.where(allowed, scores, MASKED)
        row_max = lax.optimization_barrier(jnp.max(scores, axis=-1, keepdims=True))
        expon = jnp.exp(scores - row_max)
        probs = expon / lax.optimization_barrier(jnp.sum(expon, axis=-1, keepdims=True))
        return matmul(low(probs), value_part)
    block_count = SEQLEN // WINDOW
    mixed = lax.map(jax.checkpoint(one_block), jnp.arange(block_count, dtype=jnp.int32))
    return mixed.reshape(SEQLEN, HD)

def to_heads(matrix, seq_count):
    return matrix.reshape(seq_count, SEQLEN, HEADS, HD).transpose(0, 2, 1, 3).reshape(seq_count * HEADS, SEQLEN, HD)

def from_heads(stacked, seq_count):
    return stacked.reshape(seq_count, HEADS, SEQLEN, HD).transpose(0, 2, 1, 3).reshape(seq_count * SEQLEN, HEADS * HD)

def layer(hidden_rows, attn_gain, w_query, w_key, w_value, w_out, ffn_gain, w_gate, w_up, w_down):
    seq_count = hidden_rows.shape[0] // SEQLEN
    first_in = low(rms_scale(hidden_rows, low(attn_gain)))
    queries = both_ways(matmul(first_in, low(w_query)))
    keys = both_ways(matmul(first_in, low(w_key)))
    values = both_ways(matmul(first_in, low(w_value)))
    attended = lax.map(window_head, (to_heads(queries, seq_count), to_heads(keys, seq_count), to_heads(values, seq_count)))
    attended = both_ways(from_heads(attended, seq_count))
    mid_rows = hidden_rows + low_back(matmul(attended, low(w_out)))
    second_in = low(rms_scale(mid_rows, low(ffn_gain)))
    gate = low_back(matmul(second_in, low(w_gate)))
    up_proj = low_back(matmul(second_in, low(w_up)))
    hidden_ff = low(jax.nn.silu(gate) * up_proj)
    return mid_rows + low_back(matmul(hidden_ff, low(w_down)))

def reference(hidden_in, attn_gain, w_query, w_key, w_value, w_out, ffn_gain, w_gate, w_up, w_down, out_grad):
    seq_total = TOKENS // SEQLEN
    seq_group = math.gcd(seq_total, max(1, 4096 // SEQLEN))
    group_count = seq_total // seq_group
    weights = (attn_gain, w_query, w_key, w_value, w_out, ffn_gain, w_gate, w_up, w_down)
    rows_all = hidden_in.astype(jnp.float32).reshape(group_count, seq_group * SEQLEN, D)
    cot_all = out_grad.astype(jnp.float32).reshape(group_count, seq_group * SEQLEN, D)

    def one_group(totals, operands):
        hidden_rows, cotangent = operands
        result, backward = jax.vjp(layer, hidden_rows, attn_gain, w_query, w_key, w_value, w_out, ffn_gain, w_gate, w_up, w_down)
        grads = backward(cotangent)
        totals = tuple((total + grad for total, grad in zip(totals, grads[1:])))
        return (totals, (result, grads[0]))
    initial = tuple((jnp.zeros_like(weight) for weight in weights))
    totals, (results, in_grads) = lax.scan(one_group, initial, (rows_all, cot_all))
    return (results.reshape(TOKENS, D).astype(jnp.bfloat16), in_grads.reshape(TOKENS, D), totals[0], totals[1], totals[2], totals[3], totals[4], totals[5], totals[6], totals[7], totals[8])
```

```python
import functools
import math

import jax
import jax.numpy as jnp
from jax import lax
from jax.experimental import pallas as pl
from jax.experimental.pallas import tpu as pltpu
from jax.sharding import PartitionSpec as P

HD = 128
WINDOW = 1024
EPSILON = 1e-06
MASKED = -1e30
MESH = pl.DeviceIdType.MESH
HALF = jnp.bfloat16
SINGLE = jnp.float32
VMEM_LIMIT = 60 * 2**20


def coords():
    s = lax.axis_index("seq")
    t = lax.axis_index("tp")
    return lax.rem(lax.div(s, 2), 4), lax.div(s, 16), lax.rem(lax.div(s, 8), 2), lax.rem(s, 2), t


def device(x, y, z, c, t):
    return (((y * 2 + z) * 4 + x) * 2 + c, t)


def up(v):
    return lax.rem(v + 1, 4)


def down(v):
    return lax.rem(v + 3, 4)


def across(v):
    return lax.rem(v + 2, 4)


def chip_shift(steps):
    s = lax.axis_index("seq")
    return (lax.rem(s + 2 * steps + 64, 64), lax.axis_index("tp"))


def greet(partners):
    barrier = pltpu.get_barrier_semaphore()
    for partner in partners:
        pl.semaphore_signal(barrier, inc=1, device_id=partner, device_id_type=MESH)
    pl.semaphore_wait(barrier, len(partners))


class Sems:
    def __init__(self, send, recv):
        self.send, self.recv, self.used, self.started = send, recv, 0, []

    def copy(self, src, dst, dev):
        i = self.used
        self.used += 1
        return pltpu.make_async_remote_copy(
            src, dst, self.send.at[i], self.recv.at[i], device_id=dev, device_id_type=MESH
        )

    def start(self, *copies):
        for copy in copies:
            copy.start()
            self.started.append(copy)

    def finish(self):
        for copy in self.started:
            copy.wait_send()


def gather_steps(w_in, out, sems, local_sem):
    x, y, z, c, t = coords()
    mine = pltpu.make_async_copy(w_in.at[c], out.at[y, z, x, c], local_sem)
    swap = sems.copy(w_in.at[1 - c], out.at[y, z, x, c], device(x, y, z, 1 - c, t))
    pieces = []
    for h in range(2):
        if h == 0:
            at = lambda a, zs, b, h=h: out.at[a, zs, b, h]
            a, b = y, x
            to_a = lambda v: device(x, v, z, c, t)
            to_b = lambda v: device(v, y, z, c, t)
        else:
            at = lambda a, zs, b, h=h: out.at[b, zs, a, h]
            a, b = x, y
            to_a = lambda v: device(v, y, z, c, t)
            to_b = lambda v: device(x, v, z, c, t)
        full = slice(None)

        def copy(src, dev):
            return sems.copy(src, src, dev)

        pieces.append(
            dict(
                z=copy(out.at[y, z, x, h], device(x, y, 1 - z, c, t)),
                a1p=copy(at(a, full, b), to_a(up(a))),
                a1m=copy(at(a, full, b), to_a(down(a))),
                a2p=copy(at(down(a), 0, b), to_a(up(a))),
                a2m=copy(at(up(a), 1, b), to_a(down(a))),
                b1p=copy(at(full, full, b), to_b(up(b))),
                b1m=copy(at(full, full, b), to_b(down(b))),
                b2p=copy(at(slice(0, 2), full, down(b)), to_b(up(b))),
                b2m=copy(at(slice(2, 4), full, up(b)), to_b(down(b))),
            )
        )

    def step0():
        mine.start()
        sems.start(swap)

    def step1():
        mine.wait()
        swap.wait_recv()
        for p in pieces:
            sems.start(p["z"])

    def step2():
        for p in pieces:
            p["z"].wait_recv()
            sems.start(p["a1p"], p["a1m"])

    def step3():
        for p in pieces:
            p["a1p"].wait_recv()
            sems.start(p["a2p"])
            p["a1m"].wait_recv()
            sems.start(p["a2m"])

    def step4():
        for p in pieces:
            p["a2p"].wait_recv()
            p["a2m"].wait_recv()
            sems.start(p["b1p"], p["b1m"])

    def step5():
        for p in pieces:
            p["b1p"].wait_recv()
            sems.start(p["b2p"])
            p["b1m"].wait_recv()
            sems.start(p["b2m"])

    def step6():
        for p in pieces:
            p["b2p"].wait_recv()
            p["b2m"].wait_recv()

    return [step0, step1, step2, step3, step4, step5, step6]


def halo_steps(hid, cot, xh, cots, sems, local_sems):
    x, y, z, c, t = coords()
    core = device(x, y, z, 1 - c, t)
    pair = device(x, y, z, c, 1 - t)
    locals_ = [
        pltpu.make_async_copy(hid, cots.at[0, c], local_sems.at[0]),
        pltpu.make_async_copy(cot, cots.at[1, c], local_sems.at[1]),
    ]
    swaps = [
        sems.copy(hid, cots.at[0, c], core),
        sems.copy(cot, cots.at[1, c], core),
    ]
    parts = []
    for j, shift in ((1, 1), (0, 2)):
        slot, other = xh.at[j, c, t], xh.at[j, c, 1 - t]
        parts.append(
            dict(
                first=sems.copy(hid.at[t], slot, chip_shift(shift)),
                pair=sems.copy(slot, slot, pair),
                core=sems.copy(slot, slot, core),
                both=sems.copy(other, other, core),
            )
        )

    def step0():
        for copy in locals_:
            copy.start()
        sems.start(*[p["first"] for p in parts])
        sems.start(*swaps)

    def step1():
        for p in parts:
            p["first"].wait_recv()
            sems.start(p["pair"], p["core"])

    def step2():
        for p in parts:
            p["pair"].wait_recv()
            sems.start(p["both"])

    def step3():
        for p in parts:
            p["core"].wait_recv()
            p["both"].wait_recv()
        for copy in locals_:
            copy.wait()
        for copy in swaps:
            copy.wait_recv()

    return [step0, step1, step2, step3]


def neighbours():
    x, y, z, c, t = coords()
    return [
        device(up(x), y, z, c, t),
        device(down(x), y, z, c, t),
        device(x, up(y), z, c, t),
        device(x, down(y), z, c, t),
        device(x, y, 1 - z, c, t),
        device(x, y, z, 1 - c, t),
    ]


def gather_kernel(chunks, *refs):
    w_in, (hid, cot) = refs[:chunks], refs[chunks : chunks + 2]
    rest = refs[chunks + 2 :]
    w_out, (xh, cots) = rest[:chunks], rest[chunks : chunks + 2]
    send, recv, local_sems = rest[chunks + 2 :]
    x, y, z, c, t = coords()
    sems = Sems(send, recv)
    greet(
        neighbours()
        + [device(x, y, z, c, 1 - t), chip_shift(1), chip_shift(-1), chip_shift(2), chip_shift(-2)]
    )
    halo = halo_steps(hid, cot, xh, cots, sems, local_sems)
    chunk_steps = [
        gather_steps(w_in[i], w_out[i], sems, local_sems.at[2 + i]) for i in range(chunks)
    ]
    halo[0]()
    for steps in chunk_steps:
        steps[0]()
    for steps in chunk_steps:
        steps[1]()
    order = []
    for i in range(chunks):
        for j in range(2, 7):
            order.append((2 * i + j, i, j))
    done_halo = 1
    for tick in sorted({o[0] for o in order}):
        for when, i, j in sorted(order):
            if when == tick:
                chunk_steps[i][j]()
        if tick >= 4 and done_halo < 4:
            halo[done_halo]()
            done_halo += 1
    while done_halo < 4:
        halo[done_halo]()
        done_halo += 1
    sems.finish()


def gather_all(chunks, hid, cot):
    n = len(chunks)
    features = hid.shape[-1]
    anywhere = pl.BlockSpec(memory_space=pl.ANY)
    copies = 19 * n + 10
    return pl.pallas_call(
        functools.partial(gather_kernel, n),
        out_shape=[jax.ShapeDtypeStruct((4, 2, 4, 2, 32, w.shape[-1]), HALF) for w in chunks]
        + [
            jax.ShapeDtypeStruct((2, 2, 2, 128, features), HALF),
            jax.ShapeDtypeStruct((2, 2, 2, 128, features), HALF),
        ],
        in_specs=[anywhere] * (n + 2),
        out_specs=[anywhere] * (n + 2),
        scratch_shapes=[
            pltpu.SemaphoreType.DMA((copies,)),
            pltpu.SemaphoreType.DMA((copies,)),
            pltpu.SemaphoreType.DMA((2 + n,)),
        ],
        compiler_params=pltpu.CompilerParams(
            collective_id=0, has_side_effects=True, vmem_limit_bytes=VMEM_LIMIT
        ),
    )(*chunks, hid.reshape(2, 128, features), cot.reshape(2, 128, features))


def add_blocks(target, index, sources):
    total = target(index[0]).astype(SINGLE)
    for source in sources:
        total = total + source
    return total


def scatter_steps(g, out, bufs, sems, local_sems, final_swap):
    x, y, z, c, t = coords()
    full = slice(None)
    pieces = []
    for h in range(2):
        r2, r1, q2, q1, rz, tt, ss = bufs[7 * h : 7 * h + 7]
        if h == 0:
            a, b = y, x
            to_a = lambda v: device(x, v, z, c, t)
            to_b = lambda v: device(v, y, z, c, t)
            at = lambda ref, aa, zz: ref.at[aa, zz]
            at_g = lambda aa, bb, h=h: g.at[aa, :, bb, h]
        else:
            a, b = x, y
            to_a = lambda v: device(v, y, z, c, t)
            to_b = lambda v: device(x, v, z, c, t)
            at = lambda ref, aa, zz: ref.at[zz, aa]
            at_g = lambda aa, bb, h=h: g.at[bb, :, aa, h]
        low, high = slice(0, 2), slice(2, 4)
        p = dict(
            load_p=pltpu.make_async_copy(at_g(low, up(b)), tt.at[0], local_sems.at[3 * h]),
            load_m=pltpu.make_async_copy(at_g(high, down(b)), tt.at[1], local_sems.at[3 * h + 1]),
            load_s=pltpu.make_async_copy(at_g(full, b), ss, local_sems.at[3 * h + 2]),
            x2p=sems.copy(at_g(low, across(b)), r2.at[0], to_b(up(b))),
            x2m=sems.copy(at_g(high, across(b)), r2.at[1], to_b(down(b))),
            x1ap=sems.copy(at_g(high, up(b)), at(r1.at[0], high, full), to_b(up(b))),
            x1am=sems.copy(at_g(low, down(b)), at(r1.at[1], low, full), to_b(down(b))),
            x1bp=sems.copy(tt.at[0], at(r1.at[0], low, full), to_b(up(b))),
            x1bm=sems.copy(tt.at[1], at(r1.at[1], high, full), to_b(down(b))),
            y2p=sems.copy(at(ss, across(a), 0), q2.at[0], to_a(up(a))),
            y2m=sems.copy(at(ss, across(a), 1), q2.at[1], to_a(down(a))),
            y1ap=sems.copy(at(ss, up(a), 1), q1.at[0, 1], to_a(up(a))),
            y1am=sems.copy(at(ss, down(a), 0), q1.at[1, 0], to_a(down(a))),
            y1bp=sems.copy(at(ss, up(a), 0), q1.at[0, 0], to_a(up(a))),
            y1bm=sems.copy(at(ss, down(a), 1), q1.at[1, 1], to_a(down(a))),
            z=sems.copy(at(ss, a, 1 - z), rz, device(x, y, 1 - z, c, t)),
        )
        p.update(r2=r2, r1=r1, q2=q2, q1=q1, rz=rz, tt=tt, ss=ss, a=a, at=at, h=h)
        pieces.append(p)

    def plus(ref, *others):
        total = ref[...].astype(SINGLE)
        for other in others:
            total = total + other[...].astype(SINGLE)
        ref[...] = total.astype(HALF)

    def step0():
        for p in pieces:
            sems.start(p["x2p"], p["x2m"])
            p["load_p"].start()
            p["load_m"].start()
            p["load_s"].start()
        for p in pieces:
            sems.start(p["x1ap"], p["x1am"])

    def step1():
        for p in pieces:
            for d, load, came, go in ((0, "load_p", "x2p", "x1bp"), (1, "load_m", "x2m", "x1bm")):
                p[load].wait()
                p[came].wait_recv()

                def body(i, carry, p=p, d=d):
                    u, v = lax.div(i, 2), lax.rem(i, 2)
                    plus(p["tt"].at[d, u, v], p["r2"].at[d, u, v])
                    return carry

                lax.fori_loop(0, 4, body, 0)
                sems.start(p[go])

    def step2():
        for p in pieces:
            p["load_s"].wait()
            for name in ("x1ap", "x1am", "x1bp", "x1bm"):
                p[name].wait_recv()
            inner = p["ss"].shape[1]

            def body(i, carry, p=p, inner=inner):
                u, v = lax.div(i, inner), lax.rem(i, inner)
                plus(p["ss"].at[u, v], p["r1"].at[0, u, v], p["r1"].at[1, u, v])
                return carry

            lax.fori_loop(0, 8, body, 0)
            sems.start(p["y2p"], p["y2m"], p["y1ap"], p["y1am"])

    def step3():
        for p in pieces:
            p["y2p"].wait_recv()
            plus(p["at"](p["ss"], up(p["a"]), 0), p["q2"].at[0])
            sems.start(p["y1bp"])
            p["y2m"].wait_recv()
            plus(p["at"](p["ss"], down(p["a"]), 1), p["q2"].at[1])
            sems.start(p["y1bm"])

    def step4():
        for p in pieces:
            for name in ("y1ap", "y1am", "y1bp", "y1bm"):
                p[name].wait_recv()
            for zz in range(2):
                plus(p["at"](p["ss"], p["a"], zz), p["q1"].at[0, zz], p["q1"].at[1, zz])
            sems.start(p["z"])

    def step5():
        for p in pieces:
            p["z"].wait_recv()
            total = p["at"](p["ss"], p["a"], z)[...].astype(SINGLE) + p["rz"][...].astype(SINGLE)
            final_swap[p["h"]] = total
        out[c] = final_swap[c]
        copy = sems.copy(final_swap.at[1 - c], out.at[c], device(x, y, z, 1 - c, t))
        sems.start(copy)

        def step6():
            copy.wait_recv()

        steps.append(step6)

    steps = [step0, step1, step2, step3, step4, step5]
    return steps


def scatter_kernel(chunks, *refs):
    g = refs[:chunks]
    out = refs[chunks : 2 * chunks]
    bufs = refs[2 * chunks : 2 * chunks + 14 * chunks]
    finals = refs[16 * chunks : 17 * chunks]
    send, recv, local_sems = refs[17 * chunks :]
    sems = Sems(send, recv)
    greet(neighbours())
    all_steps = [
        scatter_steps(
            g[i], out[i], bufs[14 * i : 14 * i + 14], sems, local_sems.at[i], finals[i]
        )
        for i in range(chunks)
    ]
    for tick in range(chunks + 8):
        for i in range(chunks):
            j = tick - i
            if 0 <= j < len(all_steps[i]):
                all_steps[i][j]()
    sems.finish()


def scatter_all(chunks):
    n = len(chunks)
    bufs = []
    for g in chunks:
        w = g.shape[-1]
        for h in range(2):
            wide = (4, 2) if h == 0 else (2, 4)
            bufs += [
                pltpu.VMEM((2, 2, 2, 32, w), HALF),
                pltpu.VMEM((2, *wide, 32, w), HALF),
                pltpu.VMEM((2, 32, w), HALF),
                pltpu.VMEM((2, 2, 32, w), HALF),
                pltpu.VMEM((32, w), HALF),
                pltpu.VMEM((2, 2, 2, 32, w), HALF),
                pltpu.VMEM((*wide, 32, w), HALF),
            ]
    anywhere = pl.BlockSpec(memory_space=pl.ANY)
    in_vmem = pl.BlockSpec(memory_space=pltpu.VMEM)
    copies = 27 * n
    return pl.pallas_call(
        functools.partial(scatter_kernel, n),
        out_shape=[jax.ShapeDtypeStruct((2, 32, g.shape[-1]), SINGLE) for g in chunks],
        in_specs=[anywhere] * n,
        out_specs=[in_vmem] * n,
        scratch_shapes=bufs
        + [pltpu.VMEM((2, 32, g.shape[-1]), SINGLE) for g in chunks]
        + [
            pltpu.SemaphoreType.DMA((copies,)),
            pltpu.SemaphoreType.DMA((copies,)),
            pltpu.SemaphoreType.DMA((n, 6)),
        ],
        compiler_params=pltpu.CompilerParams(
            collective_id=6, has_side_effects=True, vmem_limit_bytes=VMEM_LIMIT
        ),
    )(*[g.reshape(4, 2, 4, 2, 32, g.shape[-1]) for g in chunks])


PARTS = 4
ROWS = 16


def sum_kernel(post, n_in, n_out, spread, *refs):
    part, ins = refs[0], refs[1 : 1 + n_in]
    outs = refs[1 + n_in : 1 + n_in + n_out]
    rest = refs[1 + n_in + n_out :]
    shared = None
    if spread:
        shared, rest = rest[0], rest[1:]
    to_core, from_core, to_pair, from_pair, send, recv = rest
    x, y, z, c, t = coords()
    sems = Sems(send, recv)
    core, pair = device(x, y, z, 1 - c, t), device(x, y, z, c, 1 - t)
    size = to_core.shape[0] // PARTS
    greet([core, pair])
    rows = [pl.ds(i * size, size) for i in range(PARTS)]
    core_copies = [sems.copy(to_core.at[r], from_core.at[r], core) for r in rows]
    pair_copies = [sems.copy(to_pair.at[r], from_pair.at[r], pair) for r in rows]

    def over(i, fn):
        def body(k, carry):
            fn(pl.ds(pl.multiple_of(i * size + k * ROWS, ROWS), ROWS))
            return carry

        lax.fori_loop(0, size // ROWS, body, 0)

    def first(r):
        to_core[r, :] = part[1 - c, r, :].astype(HALF)

    def second(r):
        to_pair[r, :] = (part[c, r, :] + from_core[r, :].astype(SINGLE)).astype(HALF)

    def third(r):
        total = to_pair[r, :].astype(SINGLE) + from_pair[r, :].astype(SINGLE)
        sent = post(r, total, ins, outs)
        if spread:
            shared[c, r, :] = sent.astype(HALF)

    for i in range(PARTS):
        over(i, first)
        sems.start(core_copies[i])
    for i in range(PARTS):
        core_copies[i].wait_recv()
        over(i, second)
        sems.start(pair_copies[i])
    spreads = []
    for i in range(PARTS):
        pair_copies[i].wait_recv()
        over(i, third)
        if spread:
            copy = sems.copy(shared.at[c, rows[i]], shared.at[c, rows[i]], core)
            sems.start(copy)
            spreads.append(copy)
    for copy in spreads:
        copy.wait_recv()
    sems.finish()


def sum_call(post, collective_id, part, ins, outs, spread):
    tokens, features = part.shape[0] // 2, part.shape[1]
    in_vmem = pl.BlockSpec(memory_space=pltpu.VMEM)
    out_shape = list(outs)
    if spread:
        out_shape.append(jax.ShapeDtypeStruct((2, tokens, features), HALF))
    copies = 3 * PARTS
    return pl.pallas_call(
        functools.partial(sum_kernel, post, len(ins), len(outs), spread),
        out_shape=out_shape,
        in_specs=[in_vmem] * (1 + len(ins)),
        out_specs=[in_vmem] * len(out_shape),
        scratch_shapes=[pltpu.VMEM((tokens, features), HALF) for _ in range(4)]
        + [pltpu.SemaphoreType.DMA((copies,)), pltpu.SemaphoreType.DMA((copies,))],
        compiler_params=pltpu.CompilerParams(
            collective_id=collective_id, has_side_effects=True, vmem_limit_bytes=VMEM_LIMIT
        ),
    )(part.reshape(2, tokens, features), *ins)


def post_mid(r, total, ins, outs):
    hidden, gain = ins
    (mid_out,) = outs
    mid = hidden[r, :].astype(SINGLE) + total
    mid_out[r, :] = mid
    inverse = lax.rsqrt(jnp.mean(mid * mid, axis=-1, keepdims=True) + EPSILON)
    return mid * inverse * gain[...]


def post_out(r, total, ins, outs):
    outs[0][r, :] = (ins[0][r, :] + total).astype(HALF)


def norm_back(grad, values, gain):
    inverse = lax.rsqrt(jnp.mean(values * values, axis=-1, keepdims=True) + EPSILON)
    scaled = grad * gain
    slope = jnp.mean(scaled * values, axis=-1, keepdims=True)
    gain_term = jnp.sum(grad * values * inverse, axis=0, keepdims=True)
    return inverse * scaled - values * (inverse * inverse * inverse * slope), gain_term


def add_gain_term(gain_out, r, term):
    gain_out[...] += term


def post_mid_back(r, total, ins, outs):
    mid, cot, gain = ins
    gmid_out, gain_out = outs
    part, term = norm_back(total, mid[r, :], gain[...])
    gmid = cot[r, :].astype(SINGLE) + part
    gmid_out[r, :] = gmid
    gain_out[r, :] = jnp.broadcast_to(term, (ROWS, term.shape[1]))
    return gmid


def post_in_back(r, total, ins, outs):
    hidden, gmid, gain = ins
    grad_out, gain_out = outs
    part, term = norm_back(total, hidden[r, :].astype(SINGLE), gain[...])
    grad_out[r, :] = gmid[r, :] + part
    gain_out[r, :] = jnp.broadcast_to(term, (ROWS, term.shape[1]))


def return_kernel(own, far, out, got, send, recv):
    sems = Sems(send, recv)
    greet([chip_shift(1), chip_shift(-1), chip_shift(2), chip_shift(-2)])
    copies = [
        sems.copy(far.at[1], got.at[1], chip_shift(-1)),
        sems.copy(far.at[0], got.at[0], chip_shift(-2)),
    ]
    sems.start(*copies)
    for copy in copies:
        copy.wait_recv()

    def body(i, carry):
        r = pl.ds(pl.multiple_of(i * 32, 32), 32)
        total = own[r, :] + got[1, r, :].astype(SINGLE) + got[0, r, :].astype(SINGLE)
        out[r, :] = total.astype(HALF)
        return carry

    lax.fori_loop(0, own.shape[0] // 32, body, 0)
    sems.finish()


def return_call(own, far):
    in_vmem = pl.BlockSpec(memory_space=pltpu.VMEM)
    return pl.pallas_call(
        return_kernel,
        out_shape=jax.ShapeDtypeStruct(own.shape, HALF),
        in_specs=[in_vmem] * 2,
        out_specs=in_vmem,
        scratch_shapes=[
            pltpu.VMEM(far.shape, HALF),
            pltpu.SemaphoreType.DMA((2,)),
            pltpu.SemaphoreType.DMA((2,)),
        ],
        compiler_params=pltpu.CompilerParams(
            collective_id=5, has_side_effects=True, vmem_limit_bytes=VMEM_LIMIT
        ),
    )(own, far)


QB = 256
KB = QB + WINDOW
SCALE = 1.0 / math.sqrt(HD)


def allowed_pairs(base):
    row = lax.broadcasted_iota(jnp.int32, (QB, KB), 0)
    col = lax.broadcasted_iota(jnp.int32, (QB, KB), 1)
    return (col > row) & (col <= row + WINDOW) & (col + base >= 0)


def product(a, b, dims):
    return lax.dot_general(a, b, (dims, ((), ())), preferred_element_type=SINGLE)


def attend_kernel(chip_ref, q_ref, k_ref, v_ref, o_ref, lse_ref):
    i = pl.program_id(1)
    keys = pl.ds(pl.multiple_of(i * QB, QB), KB)
    base = (chip_ref[0] - 2) * 512 + i * QB
    scores = product(q_ref[...], k_ref[keys, :], ((1,), (1,))) * SCALE
    scores = jnp.where(allowed_pairs(base), scores, MASKED)
    row_max = jnp.max(scores, axis=-1, keepdims=True)
    expon = jnp.exp(scores - row_max)
    row_total = jnp.sum(expon, axis=-1, keepdims=True)
    probs = (expon * (1.0 / row_total)).astype(HALF)
    o_ref[...] = product(probs, v_ref[keys, :], ((1,), (0,))).astype(HALF)
    lse_ref[...] = jnp.broadcast_to(row_max + jnp.log(row_total), lse_ref.shape)


def attend(chip, q, k, v):
    tokens, width = q.shape
    heads = width // HD
    return pl.pallas_call(
        attend_kernel,
        out_shape=[
            jax.ShapeDtypeStruct((tokens, width), HALF),
            jax.ShapeDtypeStruct((tokens, width), SINGLE),
        ],
        grid=(heads, tokens // QB),
        in_specs=[
            pl.BlockSpec(memory_space=pltpu.SMEM),
            pl.BlockSpec((QB, HD), lambda h, i: (i, h)),
            pl.BlockSpec((k.shape[0], HD), lambda h, i: (0, h)),
            pl.BlockSpec((k.shape[0], HD), lambda h, i: (0, h)),
        ],
        out_specs=[
            pl.BlockSpec((QB, HD), lambda h, i: (i, h)),
            pl.BlockSpec((QB, HD), lambda h, i: (i, h)),
        ],
        compiler_params=pltpu.CompilerParams(vmem_limit_bytes=VMEM_LIMIT),
    )(chip, q, k, v)


def attend_back_kernel(chip_ref, q_ref, k_ref, v_ref, go_ref, lse_ref, gq_ref, gk_ref, gv_ref):
    i = pl.program_id(1)
    keys = pl.ds(pl.multiple_of(i * QB, QB), KB)
    base = (chip_ref[0] - 2) * 512 + i * QB
    q, k, v, go = q_ref[...], k_ref[keys, :], v_ref[keys, :], go_ref[...]
    scores = product(q, k, ((1,), (1,))) * SCALE
    scores = jnp.where(allowed_pairs(base), scores, MASKED)
    probs = jnp.exp(scores - lse_ref[:, :1])
    gp = product(go, v, ((1,), (1,)))
    inner = jnp.sum(probs * gp, axis=-1, keepdims=True)
    gs = (probs * (gp - inner)).astype(HALF)
    gq_ref[...] = (product(gs, k, ((1,), (0,))) * SCALE).astype(HALF)

    @pl.when(i == 0)
    def _():
        gk_ref[...] = jnp.zeros_like(gk_ref)
        gv_ref[...] = jnp.zeros_like(gv_ref)

    gk_ref[keys, :] += product(gs, q, ((0,), (0,))) * SCALE
    gv_ref[keys, :] += product(probs.astype(HALF), go, ((0,), (0,)))


def attend_back(chip, q, k, v, go, lse):
    tokens, width = q.shape
    heads = width // HD
    block = pl.BlockSpec((QB, HD), lambda h, i: (i, h))
    column = pl.BlockSpec((k.shape[0], HD), lambda h, i: (0, h))
    return pl.pallas_call(
        attend_back_kernel,
        out_shape=[
            jax.ShapeDtypeStruct((tokens, width), HALF),
            jax.ShapeDtypeStruct(k.shape, SINGLE),
            jax.ShapeDtypeStruct(k.shape, SINGLE),
        ],
        grid=(heads, tokens // QB),
        in_specs=[
            pl.BlockSpec(memory_space=pltpu.SMEM),
            block,
            column,
            column,
            block,
            block,
        ],
        out_specs=[block, column, column],
        compiler_params=pltpu.CompilerParams(vmem_limit_bytes=VMEM_LIMIT),
    )(chip, q, k, v, go, lse)


def halves(matrix):
    rows, width = matrix.shape
    padded = -(-width // 256) * 256
    matrix = jnp.pad(matrix, ((0, 0), (0, padded - width)))
    return jnp.moveaxis(matrix.reshape(rows, 2, padded // 2), 1, 0)


def whole(parts, width):
    return jnp.moveaxis(parts, 0, 1).reshape(parts.shape[1], -1)[:, :width]


def rms_scale(values, gain):
    inverse = lax.rsqrt(jnp.mean(values * values, axis=-1, keepdims=True) + EPSILON)
    return values * inverse * gain


def dot(a, b):
    return jnp.dot(a, b, preferred_element_type=SINGLE)


def dot_t(a, b):
    return product(a, b, ((1,), (1,)))


def t_dot(a, b):
    return product(a, b, ((0,), (0,)))


def per_device(
    hidden_in, attn_gain, w_query, w_key, w_value, w_out, ffn_gain, w_gate, w_up, w_down, out_grad
):
    features = hidden_in.shape[1]
    hidden_units = w_gate.shape[1]
    heads_width = w_query.shape[1] // 2
    chip = lax.div(lax.axis_index("seq"), 2)
    gains = jnp.pad(jnp.stack([attn_gain, ffn_gain], axis=1), ((0, 0), (0, 126)))
    gains = jnp.broadcast_to(gains, (2, *gains.shape))
    chunk_qkv = jnp.concatenate(
        [halves(w_query), halves(w_key), halves(w_value), gains], axis=2
    ).astype(HALF)
    chunk_out = halves(w_out.T).astype(HALF)
    chunk_ff = jnp.concatenate([halves(w_gate), halves(w_up)], axis=2).astype(HALF)
    chunk_down = halves(w_down.T).astype(HALF)
    ff = chunk_down.shape[-1]

    *gathered, earlier, own = gather_all(
        [chunk_qkv, chunk_out, chunk_ff, chunk_down], hidden_in, out_grad
    )
    w_qkv, wo_t, w_ff, wd_t = [w.reshape(features, w.shape[-1]) for w in gathered]
    gain_rows = w_qkv[:, 3 * heads_width :].T[:2].astype(SINGLE)
    gain_one, gain_two = gain_rows[:1], gain_rows[1:]
    w_qkv = w_qkv[:, : 3 * heads_width]
    own = own.reshape(2, 512, features)
    cot_full = own[1]
    rows = jnp.concatenate([earlier.reshape(1024, features), own[0]])

    first_in = rms_scale(rows.astype(SINGLE), gain_one).astype(HALF)
    first_own = first_in[1024:]
    queries = dot(first_own, w_qkv[:, :heads_width]).astype(HALF)
    kv = dot(first_in, w_qkv[:, heads_width:]).astype(HALF)
    keys, values = kv[:, :heads_width], kv[:, heads_width:]
    chip_ref = chip.reshape(1).astype(jnp.int32)
    attended, log_totals = attend(chip_ref, queries, keys, values)
    tokens = hidden_in.shape[0]
    rows_single = jax.ShapeDtypeStruct((tokens, features), SINGLE)
    rows_half = jax.ShapeDtypeStruct((tokens, features), HALF)
    mid, second_in = sum_call(
        post_mid, 1, dot_t(attended, wo_t), [hidden_in, gain_two], [rows_single], True
    )
    second_in = second_in.reshape(512, features)
    gate_up = dot(second_in, w_ff)
    gate, up_proj = gate_up[:, :ff], gate_up[:, ff:]
    hidden_ff = (jax.nn.silu(gate) * up_proj).astype(HALF)
    (hidden_out,) = sum_call(post_out, 2, dot_t(hidden_ff, wd_t), [mid], [rows_half], False)
    grad_hidden = dot(cot_full, wd_t)
    sig = jax.nn.sigmoid(gate)
    grad_gate = grad_hidden * up_proj * sig * (1.0 + gate * (1.0 - sig))
    grad_up = grad_hidden * gate * sig
    grad_ff = jnp.concatenate([grad_gate, grad_up], axis=1).astype(HALF)
    grad_mid, ffn_terms, grad_branch = sum_call(
        post_mid_back,
        3,
        dot_t(grad_ff, w_ff),
        [mid, out_grad, gain_two],
        [rows_single, rows_single],
        True,
    )
    grad_branch = grad_branch.reshape(512, features)
    grad_attended = dot(grad_branch, wo_t).astype(HALF)
    grad_q, grad_k, grad_v = attend_back(
        chip_ref, queries, keys, values, grad_attended, log_totals
    )
    grad_kv = jnp.concatenate([grad_k, grad_v], axis=1)
    grad_kv_own = return_call(
        grad_kv[1024:], grad_kv[:1024].astype(HALF).reshape(2, 512, 2 * heads_width)
    )
    grad_qkv = jnp.concatenate([grad_q, grad_kv_own], axis=1)
    in_grad, attn_terms = sum_call(
        post_in_back,
        4,
        dot_t(grad_qkv, w_qkv),
        [hidden_in, grad_mid, gain_one],
        [rows_single, rows_single],
        False,
    )
    terms = jnp.stack([attn_terms, ffn_terms]).reshape(2, tokens // ROWS, ROWS, features)
    gain_cols = jnp.pad(jnp.sum(terms[:, :, 0], axis=1).T, ((0, 0), (0, 126))).astype(HALF)
    g_down = t_dot(cot_full, hidden_ff).astype(HALF)
    g_ff = t_dot(second_in, grad_ff).astype(HALF)
    g_out = t_dot(grad_branch, attended).astype(HALF)
    g_qkv = t_dot(first_own, grad_qkv).astype(HALF)
    g_qkv = jnp.concatenate([g_qkv, gain_cols], axis=1)
    s_down, s_ff, s_out, s_qkv = scatter_all([g_down, g_ff, g_out, g_qkv])
    gain_sum = s_qkv[0, :, 3 * heads_width :] + s_qkv[1, :, 3 * heads_width :]
    h = heads_width
    return (
        hidden_out,
        in_grad,
        gain_sum[:, 0],
        whole(s_qkv[:, :, :h], 2 * h),
        whole(s_qkv[:, :, h : 2 * h], 2 * h),
        whole(s_qkv[:, :, 2 * h : 3 * h], 2 * h),
        whole(s_out, 2 * h).T,
        gain_sum[:, 1],
        whole(s_ff[:, :, :ff], hidden_units),
        whole(s_ff[:, :, ff:], hidden_units),
        whole(s_down, hidden_units).T,
    )


def solution(mesh):
    placed = (
        P("seq", None),
        P("seq"),
        P("seq", "tp"),
        P("seq", "tp"),
        P("seq", "tp"),
        P("tp", "seq"),
        P("seq"),
        P("seq", "tp"),
        P("seq", "tp"),
        P("tp", "seq"),
        P("seq", None),
    )
    return jax.shard_map(
        per_device,
        mesh=mesh,
        in_specs=placed,
        out_specs=(
            P("seq", None),
            P("seq", None),
            P("seq"),
            P("seq", "tp"),
            P("seq", "tp"),
            P("seq", "tp"),
            P("tp", "seq"),
            P("seq"),
            P("seq", "tp"),
            P("seq", "tp"),
            P("tp", "seq"),
        ),
        check_vma=False,
    )
```

```python
import functools
import math

import jax
import jax.numpy as jnp
from jax import lax
from jax.experimental import pallas as pl
from jax.experimental.pallas import tpu as pltpu
from jax.sharding import PartitionSpec as P

HD = 128
WINDOW = 1024
EPSILON = 1e-06
MASKED = -1e30
MESH = pl.DeviceIdType.MESH
HALF = jnp.bfloat16
SINGLE = jnp.float32
VMEM_LIMIT = 60 * 2**20


def coords():
    s = lax.axis_index("seq")
    t = lax.axis_index("tp")
    return lax.rem(lax.div(s, 2), 4), lax.div(s, 16), lax.rem(lax.div(s, 8), 2), lax.rem(s, 2), t


def device(x, y, z, c, t):
    return (((y * 2 + z) * 4 + x) * 2 + c, t)


def up(v):
    return lax.rem(v + 1, 4)


def down(v):
    return lax.rem(v + 3, 4)


def across(v):
    return lax.rem(v + 2, 4)


def chip_shift(steps):
    s = lax.axis_index("seq")
    return (lax.rem(s + 2 * steps + 64, 64), lax.axis_index("tp"))


def greet(partners):
    barrier = pltpu.get_barrier_semaphore()
    for partner in partners:
        pl.semaphore_signal(barrier, inc=1, device_id=partner, device_id_type=MESH)
    pl.semaphore_wait(barrier, len(partners))


class Sems:
    def __init__(self, send, recv):
        self.send, self.recv, self.used, self.started = send, recv, 0, []

    def copy(self, src, dst, dev):
        i = self.used
        self.used += 1
        return pltpu.make_async_remote_copy(
            src, dst, self.send.at[i], self.recv.at[i], device_id=dev, device_id_type=MESH
        )

    def start(self, *copies):
        for copy in copies:
            copy.start()
            self.started.append(copy)

    def finish(self):
        for copy in self.started:
            copy.wait_send()


def gather_steps(w_in, out, sems, local_sem):
    x, y, z, c, t = coords()
    mine = pltpu.make_async_copy(w_in.at[c], out.at[y, z, x, c], local_sem)
    swap = sems.copy(w_in.at[1 - c], out.at[y, z, x, c], device(x, y, z, 1 - c, t))
    pieces = []
    for h in range(2):
        if h == 0:
            at = lambda a, zs, b, h=h: out.at[a, zs, b, h]
            a, b = y, x
            to_a = lambda v: device(x, v, z, c, t)
            to_b = lambda v: device(v, y, z, c, t)
        else:
            at = lambda a, zs, b, h=h: out.at[b, zs, a, h]
            a, b = x, y
            to_a = lambda v: device(v, y, z, c, t)
            to_b = lambda v: device(x, v, z, c, t)
        full = slice(None)

        def copy(src, dev):
            return sems.copy(src, src, dev)

        pieces.append(
            dict(
                z=copy(out.at[y, z, x, h], device(x, y, 1 - z, c, t)),
                a1p=copy(at(a, full, b), to_a(up(a))),
                a1m=copy(at(a, full, b), to_a(down(a))),
                a2p=copy(at(down(a), 0, b), to_a(up(a))),
                a2m=copy(at(up(a), 1, b), to_a(down(a))),
                b1p=copy(at(full, full, b), to_b(up(b))),
                b1m=copy(at(full, full, b), to_b(down(b))),
                b2p=copy(at(slice(0, 2), full, down(b)), to_b(up(b))),
                b2m=copy(at(slice(2, 4), full, up(b)), to_b(down(b))),
            )
        )

    def step0():
        mine.start()
        sems.start(swap)

    def step1():
        mine.wait()
        swap.wait_recv()
        for p in pieces:
            sems.start(p["z"])

    def step2():
        for p in pieces:
            p["z"].wait_recv()
            sems.start(p["a1p"], p["a1m"])

    def step3():
        for p in pieces:
            p["a1p"].wait_recv()
            sems.start(p["a2p"])
            p["a1m"].wait_recv()
            sems.start(p["a2m"])

    def step4():
        for p in pieces:
            p["a2p"].wait_recv()
            p["a2m"].wait_recv()
            sems.start(p["b1p"], p["b1m"])

    def step5():
        for p in pieces:
            p["b1p"].wait_recv()
            sems.start(p["b2p"])
            p["b1m"].wait_recv()
            sems.start(p["b2m"])

    def step6():
        for p in pieces:
            p["b2p"].wait_recv()
            p["b2m"].wait_recv()

    return [step0, step1, step2, step3, step4, step5, step6]


def neighbours():
    x, y, z, c, t = coords()
    return [
        device(up(x), y, z, c, t),
        device(down(x), y, z, c, t),
        device(x, up(y), z, c, t),
        device(x, down(y), z, c, t),
        device(x, y, 1 - z, c, t),
        device(x, y, z, 1 - c, t),
    ]


def product(a, b, dims):
    return lax.dot_general(a, b, (dims, ((), ())), preferred_element_type=SINGLE)


QB = 256
KB = QB + WINDOW
SCALE = 1.0 / math.sqrt(HD)
PARTS = 2
ROWS = 16
LANES = 128


def allowed_pairs(base):
    row = lax.broadcasted_iota(jnp.int32, (QB, KB), 0)
    col = lax.broadcasted_iota(jnp.int32, (QB, KB), 1)
    return (col > row) & (col <= row + WINDOW) & (col + base >= 0)


def attend_block(q, k, v, base):
    scores = product(q, k, ((1,), (1,))) * SCALE
    scores = jnp.where(allowed_pairs(base), scores, MASKED)
    row_max = jnp.max(scores, axis=-1, keepdims=True)
    expon = jnp.exp(scores - row_max)
    row_total = jnp.sum(expon, axis=-1, keepdims=True)
    probs = (expon * (1.0 / row_total)).astype(HALF)
    mixed = product(probs, v, ((1,), (0,))).astype(HALF)
    return mixed, row_max + jnp.log(row_total)


def rms_inverse(values):
    return lax.rsqrt(jnp.mean(values * values, axis=-1, keepdims=True) + EPSILON)


def row_loop(start, count, fn, step=ROWS):
    def body(i, carry):
        fn(pl.ds(pl.multiple_of(start + i * step, step), step))
        return carry

    lax.fori_loop(0, count // step, body, 0)


def columns(w, n, size):
    return w[:, :, :, :, :, pl.ds(n, size)].reshape(2048, size)


CHUNK_QKV, CHUNK_OUT, CHUNK_FF, CHUNK_DOWN = range(4)
GATHER_TIMES = (-4.0, -3.0, -2.0, -1.1, 0.0, 0.6, 1.5)


def forward_kernel(*refs):
    w_in, (hid, cot) = refs[:4], refs[4:6]
    w_out = refs[6:10]
    a1, cots, q, kv, o, lse, mid, a2, hid_ff, grad_ff, gains = refs[10:21]
    (
        rows,
        w_qkv,
        w_o,
        w_ff,
        cot_v,
        gate_up,
        to_core,
        from_core,
        to_pair,
        from_pair,
        send,
        recv,
        local_sems,
    ) = refs[21:]
    x, y, z, c, t = coords()
    chip = lax.div(lax.axis_index("seq"), 2)
    core, pair = device(x, y, z, 1 - c, t), device(x, y, z, c, 1 - t)
    sems = Sems(send, recv)
    greet(neighbours() + [pair, chip_shift(1), chip_shift(-1), chip_shift(2), chip_shift(-2)])

    chunk_steps = [gather_steps(w_in[i], w_out[i], sems, local_sems.at[i]) for i in range(4)]
    order = sorted(
        (i + GATHER_TIMES[j], i, j) for i in range(4) for j in range(1, len(GATHER_TIMES))
    )
    for steps in chunk_steps:
        steps[0]()

    def pump(count=1):
        for _ in range(min(count, len(order))):
            _, i, j = order.pop(0)
            chunk_steps[i][j]()

    def pump_until(chunk):
        while any(i == chunk for _, i, _ in order):
            pump()

    row_copy = pltpu.make_async_copy(hid, rows.at[c], local_sems.at[4])
    cot_copy = pltpu.make_async_copy(cot, cots.at[c], local_sems.at[5])
    row_swap = sems.copy(hid, rows.at[c], core)
    cot_swap = sems.copy(cot, cots.at[c], core)
    row_copy.start()
    cot_copy.start()
    sems.start(row_swap, cot_swap)

    def load(chunk, target, sem):
        copy = pltpu.make_async_copy(w_out[chunk], target, local_sems.at[sem])
        copy.start()
        return copy

    pump_until(CHUNK_QKV)
    load_qkv = load(CHUNK_QKV, w_qkv, 6)
    row_copy.wait()
    row_swap.wait_recv()
    load_qkv.wait()
    pick = (
        lax.broadcasted_iota(jnp.int32, (8, LANES), 0)
        == lax.broadcasted_iota(jnp.int32, (8, LANES), 1)
    ).astype(HALF)
    gains[...] = product(pick, columns(w_qkv, 1536, LANES), ((1,), (1,)))

    for half in range(2):

        def norm_one(r, half=half):
            values = rows[half, r, :].astype(SINGLE)
            normed = values * rms_inverse(values) * gains[0:1, :]
            a1[half, r, :] = normed.astype(HALF)

        row_loop(0, 256, norm_one)
    pump()

    def project(n):
        return [product(a1[half], columns(w_qkv, n, 256), ((1,), (0,))).astype(HALF) for half in range(2)]

    def project_kv(i, carry):
        n = pl.multiple_of(i * 256, 256)
        out = project(512 + n)
        for half in range(2):
            kv[1024 + half * 256 : 1280 + half * 256, pl.ds(n, 256)] = out[half]
        return carry

    lax.fori_loop(0, 4, project_kv, 0)
    own_kv = kv.at[1024:1536]
    halo = [
        sems.copy(own_kv, kv.at[512:1024], chip_shift(1)),
        sems.copy(own_kv, kv.at[0:512], chip_shift(2)),
    ]
    sems.start(*halo)
    pump()

    def project_q(i, carry):
        n = pl.multiple_of(i * 256, 256)
        out = project(n)
        for half in range(2):
            q[half * 256 : 256 + half * 256, pl.ds(n, 256)] = out[half]
        return carry

    lax.fori_loop(0, 2, project_q, 0)
    pump_until(CHUNK_OUT)
    load_o = load(CHUNK_OUT, w_o, 7)
    for copy in halo:
        copy.wait_recv()
    for h in range(4):
        head = slice(h * HD, (h + 1) * HD)
        value_head = slice(512 + h * HD, 512 + (h + 1) * HD)

        def attend_one(i, carry, head=head, value_head=value_head):
            mine = pl.ds(pl.multiple_of(i * QB, QB), QB)
            keys = pl.ds(pl.multiple_of(i * QB, QB), KB)
            base = (chip - 2) * 512 + i * QB
            mixed, total = attend_block(q[mine, head], kv[keys, head], kv[keys, value_head], base)
            o[mine, head] = mixed
            lse[mine, head] = jnp.broadcast_to(total, (QB, HD))
            return carry

        lax.fori_loop(0, 2, attend_one, 0)
        pump()
    load_o.wait()

    size = 256 // PARTS
    parts = [pl.ds(i * size, size) for i in range(PARTS)]

    def out_rows(start):
        def tile(n):
            w_rows = w_o[n].reshape(512, 512)
            return product(o[pl.ds(start, size), :], w_rows, ((1,), (1,)))

        return tile

    core_copies = [sems.copy(to_core.at[r], from_core.at[r], core) for r in parts]
    pair_copies = [sems.copy(to_pair.at[r], from_pair.at[r], pair) for r in parts]
    for i in range(PARTS):
        tile = out_rows(pl.multiple_of((1 - c) * 256 + i * size, size))
        for n in range(4):
            to_core[parts[i], n * 512 : (n + 1) * 512] = tile(n).astype(HALF)
        sems.start(core_copies[i])
    for i in range(PARTS):
        tile = out_rows(pl.multiple_of(c * 256 + i * size, size))
        core_copies[i].wait_recv()
        for n in range(4):
            cols = slice(n * 512, (n + 1) * 512)
            to_pair[parts[i], cols] = (
                tile(n) + from_core[parts[i], cols].astype(SINGLE)
            ).astype(HALF)
        sems.start(pair_copies[i])
    pump()
    spreads = []
    for i in range(PARTS):
        pair_copies[i].wait_recv()

        def norm_two(r):
            total = to_pair[r, :].astype(SINGLE) + from_pair[r, :].astype(SINGLE)
            values = rows[c, r, :].astype(SINGLE) + total
            mid[r, :] = values
            a2[c, r, :] = (values * rms_inverse(values) * gains[1:2, :]).astype(HALF)

        row_loop(i * size, size, norm_two)
        copy = sems.copy(a2.at[c, parts[i]], a2.at[c, parts[i]], core)
        sems.start(copy)
        spreads.append(copy)
    pump_until(CHUNK_FF)
    load_ff = load(CHUNK_FF, w_ff, 8)
    for copy in spreads:
        copy.wait_recv()
    load_ff.wait()

    def gate_and_up(i, carry):
        n = pl.multiple_of(i * 2 * LANES, 2 * LANES)
        w_cols = columns(w_ff, n, 2 * LANES)
        for half in range(2):
            r = slice(half * 256, (half + 1) * 256)
            both = product(a2[half], w_cols, ((1,), (0,)))
            gate_up[r, pl.ds(n, 2 * LANES)] = both
            gate, up_part = both[:, :LANES], both[:, LANES:]
            hid_part = gate / (1.0 + jnp.exp(-gate)) * up_part
            hid_ff[r, pl.ds(pl.multiple_of(i * LANES, LANES), LANES)] = hid_part.astype(HALF)
        return carry

    lax.fori_loop(0, 11, gate_and_up, 0)
    pump(len(order))
    load_down = pltpu.make_async_copy(
        w_out[CHUNK_DOWN], w_qkv.at[:, :, :, :, :, 0:1408], local_sems.at[9]
    )
    load_down.start()
    cot_copy.wait()
    cot_swap.wait_recv()
    load_cot = pltpu.make_async_copy(cots, cot_v, local_sems.at[10])
    load_cot.start()
    load_cot.wait()
    load_down.wait()

    def back(i, carry):
        n = pl.multiple_of(i * LANES, LANES)
        w_cols = columns(w_qkv, n, LANES)
        n2 = pl.multiple_of(i * 2 * LANES, LANES)
        for half in range(2):
            r = slice(half * 256, (half + 1) * 256)
            ghid = product(cot_v[half], w_cols, ((1,), (0,)))
            gate = gate_up[r, pl.ds(n2, LANES)]
            up_part = gate_up[r, pl.ds(n2 + LANES, LANES)]
            sig = 1.0 / (1.0 + jnp.exp(-gate))
            grad_ff[r, pl.ds(n2, LANES)] = (
                ghid * up_part * sig * (1.0 + gate * (1.0 - sig))
            ).astype(HALF)
            grad_ff[r, pl.ds(n2 + LANES, LANES)] = (ghid * gate * sig).astype(HALF)
        return carry

    lax.fori_loop(0, 11, back, 0)
    sems.finish()


def forward(chunks, hid, cot):
    features = hid.shape[-1]
    anywhere = pl.BlockSpec(memory_space=pl.ANY)
    in_vmem = pl.BlockSpec(memory_space=pltpu.VMEM)
    copies = 19 * 4 + 4 + 3 * PARTS
    shape = jax.ShapeDtypeStruct
    ff = chunks[CHUNK_DOWN].shape[-1]
    full = lambda w: (4, 2, 4, 2, 32, w)
    return pl.pallas_call(
        forward_kernel,
        out_shape=[shape(full(w.shape[-1]), HALF) for w in chunks]
        + [
            shape((2, 256, features), HALF),
            shape((2, 256, features), HALF),
            shape((512, 512), HALF),
            shape((1536, 1024), HALF),
            shape((512, 512), HALF),
            shape((512, 512), SINGLE),
            shape((256, features), SINGLE),
            shape((2, 256, features), HALF),
            shape((512, ff), HALF),
            shape((512, 2 * ff), HALF),
            shape((8, features), SINGLE),
        ],
        in_specs=[anywhere] * 6,
        out_specs=[anywhere] * 4 + [in_vmem, anywhere] + [in_vmem] * 9,
        scratch_shapes=[
            pltpu.VMEM((2, 256, features), HALF),
            pltpu.VMEM(full(chunks[CHUNK_QKV].shape[-1]), HALF),
            pltpu.VMEM((4, 2, 4, 2, 32, 512), HALF),
            pltpu.VMEM(full(2 * ff), HALF),
            pltpu.VMEM((2, 256, features), HALF),
            pltpu.VMEM((512, 2 * ff), SINGLE),
        ]
        + [pltpu.VMEM((256, features), HALF) for _ in range(4)]
        + [
            pltpu.SemaphoreType.DMA((copies,)),
            pltpu.SemaphoreType.DMA((copies,)),
            pltpu.SemaphoreType.DMA((11,)),
        ],
        compiler_params=pltpu.CompilerParams(
            collective_id=0, has_side_effects=True, vmem_limit_bytes=VMEM_LIMIT
        ),
    )(*chunks, hid, cot)


def add_blocks(target, index, sources):
    total = target(index[0]).astype(SINGLE)
    for source in sources:
        total = total + source
    return total


def scatter_steps(g, out, bufs, sems, local_sems, final_swap):
    x, y, z, c, t = coords()
    full = slice(None)
    pieces = []
    for h in range(2):
        r2, r1, q2, q1, rz, tt, ss = bufs[7 * h : 7 * h + 7]
        if h == 0:
            a, b = y, x
            to_a = lambda v: device(x, v, z, c, t)
            to_b = lambda v: device(v, y, z, c, t)
            at = lambda ref, aa, zz: ref.at[aa, zz]
            at_g = lambda aa, bb, h=h: g.at[aa, :, bb, h]
        else:
            a, b = x, y
            to_a = lambda v: device(v, y, z, c, t)
            to_b = lambda v: device(x, v, z, c, t)
            at = lambda ref, aa, zz: ref.at[zz, aa]
            at_g = lambda aa, bb, h=h: g.at[bb, :, aa, h]
        low, high = slice(0, 2), slice(2, 4)
        p = dict(
            load_p=pltpu.make_async_copy(at_g(low, up(b)), tt.at[0], local_sems.at[3 * h]),
            load_m=pltpu.make_async_copy(at_g(high, down(b)), tt.at[1], local_sems.at[3 * h + 1]),
            load_s=pltpu.make_async_copy(at_g(full, b), ss, local_sems.at[3 * h + 2]),
            x2p=sems.copy(at_g(low, across(b)), r2.at[0], to_b(up(b))),
            x2m=sems.copy(at_g(high, across(b)), r2.at[1], to_b(down(b))),
            x1ap=sems.copy(at_g(high, up(b)), at(r1.at[0], high, full), to_b(up(b))),
            x1am=sems.copy(at_g(low, down(b)), at(r1.at[1], low, full), to_b(down(b))),
            x1bp=sems.copy(tt.at[0], at(r1.at[0], low, full), to_b(up(b))),
            x1bm=sems.copy(tt.at[1], at(r1.at[1], high, full), to_b(down(b))),
            y2p=sems.copy(at(ss, across(a), 0), q2.at[0], to_a(up(a))),
            y2m=sems.copy(at(ss, across(a), 1), q2.at[1], to_a(down(a))),
            y1ap=sems.copy(at(ss, up(a), 1), q1.at[0, 1], to_a(up(a))),
            y1am=sems.copy(at(ss, down(a), 0), q1.at[1, 0], to_a(down(a))),
            y1bp=sems.copy(at(ss, up(a), 0), q1.at[0, 0], to_a(up(a))),
            y1bm=sems.copy(at(ss, down(a), 1), q1.at[1, 1], to_a(down(a))),
            z=sems.copy(at(ss, a, 1 - z), rz, device(x, y, 1 - z, c, t)),
        )
        p.update(r2=r2, r1=r1, q2=q2, q1=q1, rz=rz, tt=tt, ss=ss, a=a, at=at, h=h)
        pieces.append(p)

    def plus(ref, *others):
        total = ref[...].astype(SINGLE)
        for other in others:
            total = total + other[...].astype(SINGLE)
        ref[...] = total.astype(HALF)

    def step0():
        for p in pieces:
            sems.start(p["x2p"], p["x2m"])
            p["load_p"].start()
            p["load_m"].start()
            p["load_s"].start()
        for p in pieces:
            sems.start(p["x1ap"], p["x1am"])

    def step1():
        for p in pieces:
            for d, load, came, go in ((0, "load_p", "x2p", "x1bp"), (1, "load_m", "x2m", "x1bm")):
                p[load].wait()
                p[came].wait_recv()

                def body(i, carry, p=p, d=d):
                    u, v = lax.div(i, 2), lax.rem(i, 2)
                    plus(p["tt"].at[d, u, v], p["r2"].at[d, u, v])
                    return carry

                lax.fori_loop(0, 4, body, 0)
                sems.start(p[go])

    def step2():
        for p in pieces:
            p["load_s"].wait()
            for name in ("x1ap", "x1am", "x1bp", "x1bm"):
                p[name].wait_recv()
            inner = p["ss"].shape[1]

            def body(i, carry, p=p, inner=inner):
                u, v = lax.div(i, inner), lax.rem(i, inner)
                plus(p["ss"].at[u, v], p["r1"].at[0, u, v], p["r1"].at[1, u, v])
                return carry

            lax.fori_loop(0, 8, body, 0)
            sems.start(p["y2p"], p["y2m"], p["y1ap"], p["y1am"])

    def step3():
        for p in pieces:
            p["y2p"].wait_recv()
            plus(p["at"](p["ss"], up(p["a"]), 0), p["q2"].at[0])
            sems.start(p["y1bp"])
            p["y2m"].wait_recv()
            plus(p["at"](p["ss"], down(p["a"]), 1), p["q2"].at[1])
            sems.start(p["y1bm"])

    def step4():
        for p in pieces:
            for name in ("y1ap", "y1am", "y1bp", "y1bm"):
                p[name].wait_recv()
            for zz in range(2):
                plus(p["at"](p["ss"], p["a"], zz), p["q1"].at[0, zz], p["q1"].at[1, zz])
            sems.start(p["z"])

    def step5():
        for p in pieces:
            p["z"].wait_recv()
            total = p["at"](p["ss"], p["a"], z)[...].astype(SINGLE) + p["rz"][...].astype(SINGLE)
            final_swap[p["h"]] = total
        out[c] = final_swap[c]
        copy = sems.copy(final_swap.at[1 - c], out.at[c], device(x, y, z, 1 - c, t))
        sems.start(copy)

        def step6():
            copy.wait_recv()

        steps.append(step6)

    steps = [step0, step1, step2, step3, step4, step5]
    return steps


def scatter_kernel(chunks, *refs):
    g = refs[:chunks]
    out = refs[chunks : 2 * chunks]
    bufs = refs[2 * chunks : 2 * chunks + 14 * chunks]
    finals = refs[16 * chunks : 17 * chunks]
    send, recv, local_sems = refs[17 * chunks :]
    sems = Sems(send, recv)
    greet(neighbours())
    all_steps = [
        scatter_steps(
            g[i], out[i], bufs[14 * i : 14 * i + 14], sems, local_sems.at[i], finals[i]
        )
        for i in range(chunks)
    ]
    for tick in range(chunks + 8):
        for i in range(chunks):
            j = tick - i
            if 0 <= j < len(all_steps[i]):
                all_steps[i][j]()
    sems.finish()


def scatter_all(chunks):
    n = len(chunks)
    bufs = []
    for g in chunks:
        w = g.shape[-1]
        for h in range(2):
            wide = (4, 2) if h == 0 else (2, 4)
            bufs += [
                pltpu.VMEM((2, 2, 2, 32, w), HALF),
                pltpu.VMEM((2, *wide, 32, w), HALF),
                pltpu.VMEM((2, 32, w), HALF),
                pltpu.VMEM((2, 2, 32, w), HALF),
                pltpu.VMEM((32, w), HALF),
                pltpu.VMEM((2, 2, 2, 32, w), HALF),
                pltpu.VMEM((*wide, 32, w), HALF),
            ]
    anywhere = pl.BlockSpec(memory_space=pl.ANY)
    in_vmem = pl.BlockSpec(memory_space=pltpu.VMEM)
    copies = 27 * n
    return pl.pallas_call(
        functools.partial(scatter_kernel, n),
        out_shape=[jax.ShapeDtypeStruct((2, 32, g.shape[-1]), SINGLE) for g in chunks],
        in_specs=[anywhere] * n,
        out_specs=[in_vmem] * n,
        scratch_shapes=bufs
        + [pltpu.VMEM((2, 32, g.shape[-1]), SINGLE) for g in chunks]
        + [
            pltpu.SemaphoreType.DMA((copies,)),
            pltpu.SemaphoreType.DMA((copies,)),
            pltpu.SemaphoreType.DMA((n, 6)),
        ],
        compiler_params=pltpu.CompilerParams(
            collective_id=6, has_side_effects=True, vmem_limit_bytes=VMEM_LIMIT
        ),
    )(*[g.reshape(4, 2, 4, 2, 32, g.shape[-1]) for g in chunks])


def sum_kernel(post, n_in, n_out, spread, *refs):
    part, ins = refs[0], refs[1 : 1 + n_in]
    outs = refs[1 + n_in : 1 + n_in + n_out]
    rest = refs[1 + n_in + n_out :]
    shared = None
    if spread:
        shared, rest = rest[0], rest[1:]
    to_core, from_core, to_pair, from_pair, send, recv = rest
    x, y, z, c, t = coords()
    sems = Sems(send, recv)
    core, pair = device(x, y, z, 1 - c, t), device(x, y, z, c, 1 - t)
    size = to_core.shape[0] // PARTS
    greet([core, pair])
    rows = [pl.ds(i * size, size) for i in range(PARTS)]
    core_copies = [sems.copy(to_core.at[r], from_core.at[r], core) for r in rows]
    pair_copies = [sems.copy(to_pair.at[r], from_pair.at[r], pair) for r in rows]

    def over(i, fn):
        def body(k, carry):
            fn(pl.ds(pl.multiple_of(i * size + k * ROWS, ROWS), ROWS))
            return carry

        lax.fori_loop(0, size // ROWS, body, 0)

    def first(r):
        to_core[r, :] = part[1 - c, r, :].astype(HALF)

    def second(r):
        to_pair[r, :] = (part[c, r, :] + from_core[r, :].astype(SINGLE)).astype(HALF)

    def third(r):
        total = to_pair[r, :].astype(SINGLE) + from_pair[r, :].astype(SINGLE)
        sent = post(r, total, ins, outs)
        if spread:
            shared[c, r, :] = sent.astype(HALF)

    for i in range(PARTS):
        over(i, first)
        sems.start(core_copies[i])
    for i in range(PARTS):
        core_copies[i].wait_recv()
        over(i, second)
        sems.start(pair_copies[i])
    spreads = []
    for i in range(PARTS):
        pair_copies[i].wait_recv()
        over(i, third)
        if spread:
            copy = sems.copy(shared.at[c, rows[i]], shared.at[c, rows[i]], core)
            sems.start(copy)
            spreads.append(copy)
    for copy in spreads:
        copy.wait_recv()
    sems.finish()


def sum_call(post, collective_id, part, ins, outs, spread):
    tokens, features = part.shape[0] // 2, part.shape[1]
    in_vmem = pl.BlockSpec(memory_space=pltpu.VMEM)
    out_shape = list(outs)
    if spread:
        out_shape.append(jax.ShapeDtypeStruct((2, tokens, features), HALF))
    copies = 3 * PARTS
    return pl.pallas_call(
        functools.partial(sum_kernel, post, len(ins), len(outs), spread),
        out_shape=out_shape,
        in_specs=[in_vmem] * (1 + len(ins)),
        out_specs=[in_vmem] * len(out_shape),
        scratch_shapes=[pltpu.VMEM((tokens, features), HALF) for _ in range(4)]
        + [pltpu.SemaphoreType.DMA((copies,)), pltpu.SemaphoreType.DMA((copies,))],
        compiler_params=pltpu.CompilerParams(
            collective_id=collective_id, has_side_effects=True, vmem_limit_bytes=VMEM_LIMIT
        ),
    )(part.reshape(2, tokens, features), *ins)


def post_out(r, total, ins, outs):
    outs[0][r, :] = (ins[0][r, :] + total).astype(HALF)


def norm_back(grad, values, gain):
    inverse = lax.rsqrt(jnp.mean(values * values, axis=-1, keepdims=True) + EPSILON)
    scaled = grad * gain
    slope = jnp.mean(scaled * values, axis=-1, keepdims=True)
    gain_term = jnp.sum(grad * values * inverse, axis=0, keepdims=True)
    return inverse * scaled - values * (inverse * inverse * inverse * slope), gain_term


def post_mid_back(r, total, ins, outs):
    mid, cot, gain = ins
    gmid_out, gain_out = outs
    part, term = norm_back(total, mid[r, :], gain[...])
    gmid = cot[r, :].astype(SINGLE) + part
    gmid_out[r, :] = gmid
    gain_out[r, :] = jnp.broadcast_to(term, (ROWS, term.shape[1]))
    return gmid


def post_in_back(r, total, ins, outs):
    hidden, gmid, gain = ins
    grad_out, gain_out = outs
    part, term = norm_back(total, hidden[r, :].astype(SINGLE), gain[...])
    grad_out[r, :] = gmid[r, :] + part
    gain_out[r, :] = jnp.broadcast_to(term, (ROWS, term.shape[1]))


def return_kernel(own, far, out, got, send, recv):
    sems = Sems(send, recv)
    greet([chip_shift(1), chip_shift(-1), chip_shift(2), chip_shift(-2)])
    copies = [
        sems.copy(far.at[1], got.at[1], chip_shift(-1)),
        sems.copy(far.at[0], got.at[0], chip_shift(-2)),
    ]
    sems.start(*copies)
    for copy in copies:
        copy.wait_recv()

    def body(i, carry):
        r = pl.ds(pl.multiple_of(i * 32, 32), 32)
        total = own[r, :] + got[1, r, :].astype(SINGLE) + got[0, r, :].astype(SINGLE)
        out[r, :] = total.astype(HALF)
        return carry

    lax.fori_loop(0, own.shape[0] // 32, body, 0)
    sems.finish()


def return_call(own, far):
    in_vmem = pl.BlockSpec(memory_space=pltpu.VMEM)
    return pl.pallas_call(
        return_kernel,
        out_shape=jax.ShapeDtypeStruct(own.shape, HALF),
        in_specs=[in_vmem] * 2,
        out_specs=in_vmem,
        scratch_shapes=[
            pltpu.VMEM(far.shape, HALF),
            pltpu.SemaphoreType.DMA((2,)),
            pltpu.SemaphoreType.DMA((2,)),
        ],
        compiler_params=pltpu.CompilerParams(
            collective_id=5, has_side_effects=True, vmem_limit_bytes=VMEM_LIMIT
        ),
    )(own, far)


def attend_back_kernel(chip_ref, q_ref, k_ref, v_ref, go_ref, lse_ref, gq_ref, gk_ref, gv_ref):
    i = pl.program_id(1)
    keys = pl.ds(pl.multiple_of(i * QB, QB), KB)
    base = (chip_ref[0] - 2) * 512 + i * QB
    q, k, v, go = q_ref[...], k_ref[keys, :], v_ref[keys, :], go_ref[...]
    scores = product(q, k, ((1,), (1,))) * SCALE
    scores = jnp.where(allowed_pairs(base), scores, MASKED)
    probs = jnp.exp(scores - lse_ref[:, :1])
    gp = product(go, v, ((1,), (1,)))
    inner = jnp.sum(probs * gp, axis=-1, keepdims=True)
    gs = (probs * (gp - inner)).astype(HALF)
    gq_ref[...] = (product(gs, k, ((1,), (0,))) * SCALE).astype(HALF)

    @pl.when(i == 0)
    def _():
        gk_ref[...] = jnp.zeros_like(gk_ref)
        gv_ref[...] = jnp.zeros_like(gv_ref)

    gk_ref[keys, :] += product(gs, q, ((0,), (0,))) * SCALE
    gv_ref[keys, :] += product(probs.astype(HALF), go, ((0,), (0,)))


def attend_back(chip, q, k, v, go, lse):
    tokens, width = q.shape
    heads = width // HD
    block = pl.BlockSpec((QB, HD), lambda h, i: (i, h))
    column = pl.BlockSpec((k.shape[0], HD), lambda h, i: (0, h))
    return pl.pallas_call(
        attend_back_kernel,
        out_shape=[
            jax.ShapeDtypeStruct((tokens, width), HALF),
            jax.ShapeDtypeStruct(k.shape, SINGLE),
            jax.ShapeDtypeStruct(k.shape, SINGLE),
        ],
        grid=(heads, tokens // QB),
        in_specs=[
            pl.BlockSpec(memory_space=pltpu.SMEM),
            block,
            column,
            column,
            block,
            block,
        ],
        out_specs=[block, column, column],
        compiler_params=pltpu.CompilerParams(vmem_limit_bytes=VMEM_LIMIT),
    )(chip, q, k, v, go, lse)


def halves(matrix):
    rows, width = matrix.shape
    padded = -(-width // 256) * 256
    matrix = jnp.pad(matrix, ((0, 0), (0, padded - width)))
    return jnp.moveaxis(matrix.reshape(rows, 2, padded // 2), 1, 0)


def interleave(first, second):
    cut = lambda m: m.reshape(2, m.shape[1], -1, 1, LANES)
    return jnp.concatenate([cut(first), cut(second)], axis=3).reshape(2, first.shape[1], -1)


def whole(parts, width):
    return jnp.moveaxis(parts, 0, 1).reshape(parts.shape[1], -1)[:, :width]


def dot(a, b):
    return jnp.dot(a, b, preferred_element_type=SINGLE)


def dot_t(a, b):
    return product(a, b, ((1,), (1,)))


def t_dot(a, b):
    return product(a, b, ((0,), (0,)))


def per_device(
    hidden_in, attn_gain, w_query, w_key, w_value, w_out, ffn_gain, w_gate, w_up, w_down, out_grad
):
    features = hidden_in.shape[1]
    hidden_units = w_gate.shape[1]
    heads_width = w_query.shape[1] // 2
    chip = lax.div(lax.axis_index("seq"), 2)
    gains = jnp.pad(jnp.stack([attn_gain, ffn_gain], axis=1), ((0, 0), (0, 126)))
    gains = jnp.broadcast_to(gains, (2, *gains.shape))
    chunk_qkv = jnp.concatenate(
        [halves(w_query), halves(w_key), halves(w_value), gains], axis=2
    ).astype(HALF)
    chunk_out = halves(w_out.T).astype(HALF)
    chunk_ff = interleave(halves(w_gate), halves(w_up)).astype(HALF)
    chunk_down = halves(w_down.T).astype(HALF)
    ff = chunk_down.shape[-1]
    tokens = hidden_in.shape[0]

    *gathered, a1, cots, queries, kv, attended, log_totals, mid, a2, hidden_ff, grad_ff, gain_rows = forward(
        [chunk_qkv, chunk_out, chunk_ff, chunk_down], hidden_in, out_grad
    )
    w_qkv, wo_t, w_ff, wd_t = [w.reshape(features, w.shape[-1]) for w in gathered]
    gain_one, gain_two = gain_rows[0:1], gain_rows[1:2]
    w_qkv = w_qkv[:, : 3 * heads_width]
    cot_full = cots.reshape(512, features)
    first_own = a1.reshape(512, features)
    second_in = a2.reshape(512, features)
    keys, values = kv[:, :heads_width], kv[:, heads_width:]
    chip_ref = chip.reshape(1).astype(jnp.int32)
    rows_single = jax.ShapeDtypeStruct((tokens, features), SINGLE)
    rows_half = jax.ShapeDtypeStruct((tokens, features), HALF)
    (hidden_out,) = sum_call(post_out, 2, dot_t(hidden_ff, wd_t), [mid], [rows_half], False)
    grad_mid, ffn_terms, grad_branch = sum_call(
        post_mid_back,
        3,
        dot_t(grad_ff, w_ff),
        [mid, out_grad, gain_two],
        [rows_single, rows_single],
        True,
    )
    grad_branch = grad_branch.reshape(512, features)
    grad_attended = dot(grad_branch, wo_t).astype(HALF)
    grad_q, grad_k, grad_v = attend_back(
        chip_ref, queries, keys, values, grad_attended, log_totals
    )
    grad_kv = jnp.concatenate([grad_k, grad_v], axis=1)
    grad_kv_own = return_call(
        grad_kv[1024:], grad_kv[:1024].astype(HALF).reshape(2, 512, 2 * heads_width)
    )
    grad_qkv = jnp.concatenate([grad_q, grad_kv_own], axis=1)
    in_grad, attn_terms = sum_call(
        post_in_back,
        4,
        dot_t(grad_qkv, w_qkv),
        [hidden_in, grad_mid, gain_one],
        [rows_single, rows_single],
        False,
    )
    terms = jnp.stack([attn_terms, ffn_terms]).reshape(2, tokens // ROWS, ROWS, features)
    gain_cols = jnp.pad(jnp.sum(terms[:, :, 0], axis=1).T, ((0, 0), (0, 126))).astype(HALF)
    g_down = t_dot(cot_full, hidden_ff).astype(HALF)
    g_ff = t_dot(second_in, grad_ff).astype(HALF)
    g_out = t_dot(grad_branch, attended).astype(HALF)
    g_qkv = t_dot(first_own, grad_qkv).astype(HALF)
    g_qkv = jnp.concatenate([g_qkv, gain_cols], axis=1)
    s_down, s_ff, s_out, s_qkv = scatter_all([g_down, g_ff, g_out, g_qkv])
    s_ff = s_ff.reshape(2, 32, ff // LANES, 2, LANES)
    s_gate, s_up = s_ff[:, :, :, 0].reshape(2, 32, ff), s_ff[:, :, :, 1].reshape(2, 32, ff)
    gain_sum = s_qkv[0, :, 3 * heads_width :] + s_qkv[1, :, 3 * heads_width :]
    h = heads_width
    return (
        hidden_out,
        in_grad,
        gain_sum[:, 0],
        whole(s_qkv[:, :, :h], 2 * h),
        whole(s_qkv[:, :, h : 2 * h], 2 * h),
        whole(s_qkv[:, :, 2 * h : 3 * h], 2 * h),
        whole(s_out, 2 * h).T,
        gain_sum[:, 1],
        whole(s_gate, hidden_units),
        whole(s_up, hidden_units),
        whole(s_down, hidden_units).T,
    )


def solution(mesh):
    placed = (
        P("seq", None),
        P("seq"),
        P("seq", "tp"),
        P("seq", "tp"),
        P("seq", "tp"),
        P("tp", "seq"),
        P("seq"),
        P("seq", "tp"),
        P("seq", "tp"),
        P("tp", "seq"),
        P("seq", None),
    )
    return jax.shard_map(
        per_device,
        mesh=mesh,
        in_specs=placed,
        out_specs=(
            P("seq", None),
            P("seq", None),
            P("seq"),
            P("seq", "tp"),
            P("seq", "tp"),
            P("seq", "tp"),
            P("tp", "seq"),
            P("seq"),
            P("seq", "tp"),
            P("seq", "tp"),
            P("tp", "seq"),
        ),
        check_vma=False,
    )
```

```python
import functools
import math

import jax
import jax.numpy as jnp
from jax import lax
from jax.experimental import pallas as pl
from jax.experimental.pallas import tpu as pltpu
from jax.sharding import PartitionSpec as P

HD = 128
WINDOW = 1024
EPSILON = 1e-06
MASKED = -1e30
MESH = pl.DeviceIdType.MESH
HALF = jnp.bfloat16
SINGLE = jnp.float32
VMEM_LIMIT = 62 * 2**20

D = 2048
TOK = 256
HW = 512
FF = 1408
QB = 256
KB = QB + WINDOW
SCALE = 1.0 / math.sqrt(HD)
ROWS = 16
LANES = 128
PART = 512
PARTS = D // PART


def coords():
    s = lax.axis_index("seq")
    t = lax.axis_index("tp")
    return lax.rem(lax.div(s, 2), 4), lax.div(s, 16), lax.rem(lax.div(s, 8), 2), lax.rem(s, 2), t


def device(x, y, z, c, t):
    return (((y * 2 + z) * 4 + x) * 2 + c, t)


def moved(v, steps):
    return lax.rem(v + steps + 4, 4)


def chip_shift(steps):
    s = lax.axis_index("seq")
    return (lax.rem(s + 2 * steps + 64, 64), lax.axis_index("tp"))


def neighbours():
    x, y, z, c, t = coords()
    return [
        device(moved(x, 1), y, z, c, t),
        device(moved(x, -1), y, z, c, t),
        device(x, moved(y, 1), z, c, t),
        device(x, moved(y, -1), z, c, t),
        device(x, y, 1 - z, c, t),
        device(x, y, z, 1 - c, t),
    ]


def window_chips():
    return [chip_shift(1), chip_shift(-1), chip_shift(2), chip_shift(-2)]


def greet(partners):
    barrier = pltpu.get_barrier_semaphore()
    for partner in partners:
        pl.semaphore_signal(barrier, inc=1, device_id=partner, device_id_type=MESH)
    pl.semaphore_wait(barrier, len(partners))


class Sems:
    def __init__(self, send, recv):
        self.send, self.recv, self.used, self.started = send, recv, 0, []

    def copy(self, src, dst, dev):
        i = self.used
        self.used += 1
        return pltpu.make_async_remote_copy(
            src, dst, self.send.at[i], self.recv.at[i], device_id=dev, device_id_type=MESH
        )

    def start(self, *copies):
        for copy in copies:
            copy.start()
            self.started.append(copy)

    def finish(self):
        for copy in self.started:
            copy.wait_send()


class Locals:
    def __init__(self, sems):
        self.sems, self.used = sems, 0

    def sem(self):
        self.used += 1
        return self.sems.at[self.used - 1]

    def copy(self, src, dst):
        return pltpu.make_async_copy(src, dst, self.sem())

    def load(self, src, dst):
        copy = self.copy(src, dst)
        copy.start()
        return copy


class Plan:
    def __init__(self):
        self.steps = []

    def add(self, when, step):
        self.steps.append((when, len(self.steps), step))

    def until(self, when):
        self.steps.sort(key=lambda s: s[:2])
        while self.steps and self.steps[0][0] <= when:
            self.steps.pop(0)[2]()

    def rest(self):
        self.until(math.inf)


def grid_piece(h):
    x, y, z, c, t = coords()
    if h == 0:
        return y, x, lambda v: device(x, v, z, c, t), lambda v: device(v, y, z, c, t)
    return x, y, lambda v: device(v, y, z, c, t), lambda v: device(x, v, z, c, t)


def blocks(ref, h, a, zs, b):
    return ref.at[a, zs, b, h] if h == 0 else ref.at[b, zs, a, h]


ALL = slice(None)


GATHER_COPIES = 1 + 2 * 13


def plan_gather(plan, begin, length, w_in, out, sems, local):
    x, y, z, c, t = coords()
    mine = local.copy(w_in.at[c], out.at[y, z, x, c])
    swap = sems.copy(w_in.at[1 - c], out.at[y, z, x, c], device(x, y, z, 1 - c, t))
    over_z, streams = [], []
    for h in range(2):
        a, b, to_a, to_b = grid_piece(h)
        src = out.at[y, z, x, h]
        over_z.append(sems.copy(src, src, device(x, y, 1 - z, c, t)))
        for s, zs, d in ((0, z, 1), (1, 1 - z, -1)):

            def copy(aa, bb, dev, h=h, zs=zs):
                src = blocks(out, h, aa, zs, bb)
                return sems.copy(src, src, dev)

            streams.append(
                dict(
                    s=s,
                    a1f=copy(a, b, to_a(moved(a, d))),
                    a1r=copy(a, b, to_a(moved(a, -d))),
                    a2=copy(moved(a, -d), b, to_a(moved(a, d))),
                    b1f=copy(ALL, b, to_b(moved(b, d))),
                    b1r=copy(ALL, b, to_b(moved(b, -d))),
                    b2=copy(ALL, moved(b, -d), to_b(moved(b, d))),
                )
            )
    first, second = [[p for p in streams if p["s"] == s] for s in range(2)]

    def first_start():
        mine.start()
        sems.start(swap)

    def own():
        mine.wait()
        swap.wait_recv()
        sems.start(*over_z)
        for p in first:
            sems.start(p["a1f"], p["a1r"])

    def other():
        for copy in over_z:
            copy.wait_recv()
        for p in second:
            sems.start(p["a1f"], p["a1r"])

    def a2(ps):
        for p in ps:
            p["a1f"].wait_recv()
            sems.start(p["a2"])

    def b1(ps):
        for p in ps:
            p["a1r"].wait_recv()
            p["a2"].wait_recv()
            sems.start(p["b1f"], p["b1r"])

    def b2(ps):
        for p in ps:
            p["b1f"].wait_recv()
            sems.start(p["b2"])

    def end(ps):
        for p in ps:
            p["b1r"].wait_recv()
            p["b2"].wait_recv()

    first_start()
    plan.add(begin - 24, own)
    plan.add(begin - 20, other)
    plan.add(begin - 16, lambda: a2(first))
    plan.add(begin - 12, lambda: a2(second))
    plan.add(begin - 6, lambda: b1(first))
    plan.add(begin - 2, lambda: b1(second))
    plan.add(begin + 0.4 * length, lambda: b2(first))
    plan.add(begin + 0.55 * length, lambda: b2(second))
    plan.add(begin + length, lambda: end(first))
    plan.add(begin + length, lambda: end(second))


SCATTER_COPIES = 4 * 6 + 3
SCATTER_LOADS = 16


def scatter_slots(w):
    return [
        jax.ShapeDtypeStruct((2, 2, 4, 32, w), HALF),
        jax.ShapeDtypeStruct((2, 2, 2, 4, 32, w), HALF),
    ]


def scatter_scratch(w):
    return [
        pltpu.VMEM((2, 2, 4, 32, w), HALF),
        pltpu.VMEM((2, 2, 4, 32, w), HALF),
        pltpu.VMEM((2, 2, 32, w), HALF),
        pltpu.VMEM((2, 2, 2, 32, w), HALF),
        pltpu.VMEM((2, 32, w), HALF),
        pltpu.VMEM((2, 32, w), SINGLE),
    ]


def plus(ref, *others):
    total = ref[...].astype(SINGLE)
    for other in others:
        total = total + other[...].astype(SINGLE)
    ref[...] = total.astype(HALF)


def plan_scatter(plan, begin, length, g, out, slots, scratch, temp, sems, local):
    x, y, z, c, t = coords()
    r2, r1 = slots
    tt, ss, q2, q1, rz, final = scratch
    width = g.shape[-1]
    wide = slice(0, width)
    streams = []
    for h in range(2):
        a, b, to_a, to_b = grid_piece(h)
        for s, zs, d in ((0, z, 1), (1, 1 - z, -1)):
            at_g = lambda bb, h=h, zs=zs: blocks(g, h, ALL, zs, bb)
            tmp = temp.at[h, s, :, :, :, wide]
            streams.append(
                dict(
                    h=h,
                    s=s,
                    a=a,
                    d=d,
                    load_t=local.copy(at_g(moved(b, d)), tt.at[h, s]),
                    load_s=local.copy(at_g(b), ss.at[h, s]),
                    load_2=local.copy(r2.at[h, s], tmp.at[0]),
                    load_1=local.copy(r1.at[h, s], tmp),
                    x2=sems.copy(at_g(moved(b, 2)), r2.at[h, s], to_b(moved(b, d))),
                    x1r=sems.copy(at_g(moved(b, -d)), r1.at[h, s, 1], to_b(moved(b, -d))),
                    x1f=sems.copy(tt.at[h, s], r1.at[h, s, 0], to_b(moved(b, d))),
                    y2=sems.copy(ss.at[h, s, moved(a, 2)], q2.at[h, s], to_a(moved(a, d))),
                    y1r=sems.copy(ss.at[h, s, moved(a, -d)], q1.at[h, s, 1], to_a(moved(a, -d))),
                    y1f=sems.copy(ss.at[h, s, moved(a, d)], q1.at[h, s, 0], to_a(moved(a, d))),
                )
            )
    over_z = [
        sems.copy(ss.at[h, 1, grid_piece(h)[0]], rz.at[h], device(x, y, 1 - z, c, t))
        for h in range(2)
    ]
    swap = sems.copy(final.at[1 - c], out.at[c], device(x, y, z, 1 - c, t))

    def start():
        for p in streams:
            sems.start(p["x2"], p["x1r"])
        for p in streams:
            p["load_t"].start()
            p["load_s"].start()

    def x1():
        for p in streams:
            p["load_t"].wait()
            p["x2"].wait_recv()
            p["load_2"].start()
        for p in streams:
            h, s = p["h"], p["s"]
            p["load_2"].wait()

            def body(i, carry, h=h, s=s):
                plus(tt.at[h, s, i], temp.at[h, s, 0, i, :, wide])
                return carry

            lax.fori_loop(0, 4, body, 0)
            sems.start(p["x1f"])

    def x0():
        for p in streams:
            p["load_s"].wait()
            p["x1r"].wait_recv()
            p["x1f"].wait_recv()
            p["load_1"].start()
        for p in streams:
            h, s = p["h"], p["s"]
            p["load_1"].wait()

            def body(i, carry, h=h, s=s):
                plus(
                    ss.at[h, s, i], temp.at[h, s, 0, i, :, wide], temp.at[h, s, 1, i, :, wide]
                )
                return carry

            lax.fori_loop(0, 4, body, 0)
            sems.start(p["y2"], p["y1r"])

    def y1():
        for p in streams:
            h, s = p["h"], p["s"]
            p["y2"].wait_recv()
            plus(ss.at[h, s, moved(p["a"], p["d"])], q2.at[h, s])
            sems.start(p["y1f"])

    def y0():
        for p in streams:
            h, s = p["h"], p["s"]
            p["y1f"].wait_recv()
            p["y1r"].wait_recv()
            plus(ss.at[h, s, p["a"]], q1.at[h, s, 0], q1.at[h, s, 1])
            if s == 1:
                sems.start(over_z[h])

    def last():
        for p in streams:
            h = p["h"]
            if p["s"] == 0:
                over_z[h].wait_recv()
                final[h] = ss[h, 0, p["a"]].astype(SINGLE) + rz[h].astype(SINGLE)
        out[c] = final[c]
        sems.start(swap)

    plan.add(begin, start)
    plan.add(begin + 0.4 * length, x1)
    plan.add(begin + length, x0)
    plan.add(begin + length + 4, y1)
    plan.add(begin + length + 8, y0)
    plan.add(begin + length + 12, last)
    plan.add(begin + length + 16, swap.wait_recv)


def make_grads(lhs, rhs_columns, staging, g, local):
    sems = [local.sem() for _ in range(2)]

    def write(i, slot):
        return pltpu.make_async_copy(staging.at[slot], g.at[i, slot], sems[slot])

    def body(i, carry):
        for slot in range(2):
            n = pl.multiple_of(i * 512 + slot * 256, 256)
            left = lhs[:, :, pl.ds(n, 256)].reshape(512, 256)
            tile = product(left, rhs_columns(), ((0,), (0,))).astype(HALF)

            @pl.when(i > 0)
            def _():
                write(i, slot).wait()

            staging[slot] = tile.reshape(staging.shape[1:])
            write(i, slot).start()
        return carry

    lax.fori_loop(0, 4, body, 0)
    for slot in range(2):
        write(0, slot).wait()


class FourSum:
    def __init__(self, bufs, sems):
        x, y, z, c, t = coords()
        self.to_core, self.from_core, self.to_pair, self.from_pair, self.own = bufs
        self.sems = sems
        self.cols = [slice(i * PART, (i + 1) * PART) for i in range(PARTS)]
        core, pair = device(x, y, z, 1 - c, t), device(x, y, z, c, 1 - t)
        self.core = [sems.copy(self.to_core.at[:, n], self.from_core.at[:, n], core) for n in self.cols]
        self.pair = [sems.copy(self.to_pair.at[:, n], self.from_pair.at[:, n], pair) for n in self.cols]

    def put(self, i, theirs, ours):
        self.to_core[:, self.cols[i]] = theirs.astype(HALF)
        self.own[:, self.cols[i]] = ours
        self.sems.start(self.core[i])

    def relay(self, i):
        n = self.cols[i]
        self.core[i].wait_recv()

        def add(r):
            self.to_pair[r, n] = (self.own[r, n] + self.from_core[r, n].astype(SINGLE)).astype(HALF)

        row_loop(0, TOK, add, 64)
        self.sems.start(self.pair[i])

    def wait(self):
        for copy in self.pair:
            copy.wait_recv()

    def total(self, r):
        return self.to_pair[r, :].astype(SINGLE) + self.from_pair[r, :].astype(SINGLE)


SUM_COPIES = 2 * PARTS
SUM_SCRATCH = [pltpu.VMEM((TOK, D), HALF) for _ in range(4)] + [pltpu.VMEM((TOK, D), SINGLE)]


def product(a, b, dims):
    return lax.dot_general(a, b, (dims, ((), ())), preferred_element_type=SINGLE)


def allowed_pairs(base):
    row = lax.broadcasted_iota(jnp.int32, (QB, KB), 0)
    col = lax.broadcasted_iota(jnp.int32, (QB, KB), 1)
    return (col > row) & (col <= row + WINDOW) & (col + base >= 0)


def attend_block(q, k, v, base):
    scores = product(q, k, ((1,), (1,))) * SCALE
    scores = jnp.where(allowed_pairs(base), scores, MASKED)
    row_max = jnp.max(scores, axis=-1, keepdims=True)
    expon = jnp.exp(scores - row_max)
    row_total = jnp.sum(expon, axis=-1, keepdims=True)
    probs = (expon * (1.0 / row_total)).astype(HALF)
    mixed = product(probs, v, ((1,), (0,))).astype(HALF)
    return mixed, row_max + jnp.log(row_total)


def attend_block_back(q, k, v, go, lse, base):
    scores = product(q, k, ((1,), (1,))) * SCALE
    scores = jnp.where(allowed_pairs(base), scores, MASKED)
    probs = jnp.exp(scores - lse)
    gp = product(go, v, ((1,), (1,)))
    inner = jnp.sum(probs * gp, axis=-1, keepdims=True)
    gs = (probs * (gp - inner)).astype(HALF)
    gq = product(gs, k, ((1,), (0,))) * SCALE
    gk = product(gs, q, ((0,), (0,))) * SCALE
    gv = product(probs.astype(HALF), go, ((0,), (0,)))
    return gq, gk, gv


def rms_inverse(values):
    return lax.rsqrt(jnp.mean(values * values, axis=-1, keepdims=True) + EPSILON)


def norm_back(grad, values, gain):
    inverse = rms_inverse(values)
    scaled = grad * gain
    slope = jnp.mean(scaled * values, axis=-1, keepdims=True)
    gain_term = jnp.sum(grad * values * inverse, axis=0, keepdims=True)
    return inverse * scaled - values * (inverse * inverse * inverse * slope), gain_term


def row_loop(start, count, fn, step=ROWS):
    def body(i, carry):
        fn(pl.ds(pl.multiple_of(start + i * step, step), step))
        return carry

    lax.fori_loop(0, count // step, body, 0)


def columns(w, n, size):
    return w[:, :, :, :, :, pl.ds(n, size)].reshape(D, size)


def pick_lanes():
    return lax.broadcasted_iota(jnp.int32, (8, LANES), 0) == lax.broadcasted_iota(
        jnp.int32, (8, LANES), 1
    )


ANYWHERE = pl.BlockSpec(memory_space=pl.ANY)
IN_VMEM = pl.BlockSpec(memory_space=pltpu.VMEM)
SHAPE = jax.ShapeDtypeStruct


def grid_of(w):
    return (4, 2, 4, 2, 32, w)


def params(collective_id):
    return pltpu.CompilerParams(
        collective_id=collective_id, has_side_effects=True, vmem_limit_bytes=VMEM_LIMIT
    )


W_QKV, W_OUT, W_FF, W_DOWN = range(4)
GATHER_TIMES = ((24, 34), (58, 10), (68, 58), (126, 29))


def forward_kernel(*refs):
    w_in, (hid, cot) = refs[:4], refs[4:6]
    w_out = refs[6:10]
    a1, cots, q, kv, o, lse, mid, a2, hid_ff, grad_ff, gains = refs[10:21]
    rows, w_qkv, w_o, w_ff, cot_v, gate_up = refs[21:27]
    send, recv, local_sems = refs[32:]
    x, y, z, c, t = coords()
    chip = lax.div(lax.axis_index("seq"), 2)
    core, pair = device(x, y, z, 1 - c, t), device(x, y, z, c, 1 - t)
    sems, local = Sems(send, recv), Locals(local_sems)
    greet(neighbours() + [pair] + window_chips())

    plan = Plan()
    for i in range(4):
        plan_gather(plan, *GATHER_TIMES[i], w_in[i], w_out[i], sems, local)
    row_copy = local.load(hid, rows.at[c])
    cot_copy = local.load(cot, cots.at[c])
    row_swap = sems.copy(hid, rows.at[c], core)
    cot_swap = sems.copy(cot, cots.at[c], core)
    sems.start(row_swap, cot_swap)

    plan.until(sum(GATHER_TIMES[W_QKV]))
    load_qkv = local.load(w_out[W_QKV], w_qkv)
    row_copy.wait()
    row_swap.wait_recv()
    load_qkv.wait()
    pick = pick_lanes().astype(HALF)
    gains[...] = product(pick, columns(w_qkv, 3 * HW, LANES), ((1,), (1,)))

    for half in range(2):

        def norm_one(r, half=half):
            values = rows[half, r, :].astype(SINGLE)
            a1[half, r, :] = (values * rms_inverse(values) * gains[0:1, :]).astype(HALF)

        row_loop(0, TOK, norm_one)
    plan.until(62)

    def project(n):
        w_cols = columns(w_qkv, n, 2 * HD)
        return [product(a1[half], w_cols, ((1,), (0,))).astype(HALF) for half in range(2)]

    halo = []
    for h in range(4):
        n = slice(h * 2 * HD, (h + 1) * 2 * HD)
        out = project(HW + h * 2 * HD)
        for half in range(2):
            kv[WINDOW + half * TOK : WINDOW + (half + 1) * TOK, n] = out[half]
        own = kv.at[1024:1536, n]
        copies = [
            sems.copy(own, kv.at[512:1024, n], chip_shift(1)),
            sems.copy(own, kv.at[0:512, n], chip_shift(2)),
        ]
        sems.start(*copies)
        halo.append(copies)
    for n in range(0, HW, 2 * HD):
        out = project(n)
        for half in range(2):
            q[half * TOK : (half + 1) * TOK, n : n + 2 * HD] = out[half]
    plan.until(74)
    load_o = local.load(w_out[W_OUT], w_o)
    for h in range(4):
        for copy in halo[h]:
            copy.wait_recv()
        head = slice(h * HD, (h + 1) * HD)
        key_head = slice(2 * h * HD, (2 * h + 1) * HD)
        value_head = slice((2 * h + 1) * HD, (2 * h + 2) * HD)

        def attend_one(i, carry):
            mine = pl.ds(pl.multiple_of(i * QB, QB), QB)
            keys = pl.ds(pl.multiple_of(i * QB, QB), KB)
            base = (chip - 2) * 512 + i * QB
            mixed, total = attend_block(
                q[mine, head], kv[keys, key_head], kv[keys, value_head], base
            )
            o[mine, head] = mixed
            lse[mine, head] = jnp.broadcast_to(total, (QB, HD))
            return carry

        lax.fori_loop(0, 2, attend_one, 0)
        plan.until(80 + 4 * h)
    load_o.wait()

    attended = FourSum(refs[27:32], sems)
    theirs, ours = [pl.ds(pl.multiple_of(k * TOK, TOK), TOK) for k in (1 - c, c)]
    for i in range(PARTS):
        w_rows = w_o[i].reshape(PART, HW)
        attended.put(
            i,
            product(o[theirs, :], w_rows, ((1,), (1,))),
            product(o[ours, :], w_rows, ((1,), (1,))),
        )
    for i in range(PARTS):
        attended.relay(i)
    plan.until(104)
    attended.wait()
    spreads = []
    for half in range(2):

        def norm_two(r):
            values = rows[c, r, :].astype(SINGLE) + attended.total(r)
            mid[r, :] = values
            a2[c, r, :] = (values * rms_inverse(values) * gains[1:2, :]).astype(HALF)

        row_loop(half * 128, 128, norm_two)
        part = a2.at[c, half * 128 : (half + 1) * 128]
        copy = sems.copy(part, part, core)
        sems.start(copy)
        spreads.append(copy)
    plan.until(sum(GATHER_TIMES[W_FF]))
    load_ff = local.load(w_out[W_FF], w_ff)
    for copy in spreads:
        copy.wait_recv()
    load_ff.wait()

    def gate_and_up(i, carry):
        n = pl.multiple_of(i * 2 * LANES, 2 * LANES)
        w_cols = columns(w_ff, n, 2 * LANES)
        for half in range(2):
            r = slice(half * TOK, (half + 1) * TOK)
            both = product(a2[half], w_cols, ((1,), (0,)))
            gate_up[r, pl.ds(n, 2 * LANES)] = both
            gate, up_part = both[:, :LANES], both[:, LANES:]
            hid_part = gate / (1.0 + jnp.exp(-gate)) * up_part
            hid_ff[r, pl.ds(pl.multiple_of(i * LANES, LANES), LANES)] = hid_part.astype(HALF)
        return carry

    lax.fori_loop(0, FF // LANES, gate_and_up, 0)
    plan.rest()
    load_down = local.load(w_out[W_DOWN], w_qkv.at[:, :, :, :, :, 0:FF])
    cot_copy.wait()
    cot_swap.wait_recv()
    load_cot = local.load(cots, cot_v)
    load_cot.wait()
    load_down.wait()

    def back(i, carry):
        w_cols = columns(w_qkv, pl.multiple_of(i * LANES, LANES), LANES)
        n = pl.multiple_of(i * 2 * LANES, 2 * LANES)
        for half in range(2):
            r = slice(half * TOK, (half + 1) * TOK)
            ghid = product(cot_v[half], w_cols, ((1,), (0,)))
            gate = gate_up[r, pl.ds(n, LANES)]
            up_part = gate_up[r, pl.ds(n + LANES, LANES)]
            sig = 1.0 / (1.0 + jnp.exp(-gate))
            grad_ff[r, pl.ds(n, LANES)] = (
                ghid * up_part * sig * (1.0 + gate * (1.0 - sig))
            ).astype(HALF)
            grad_ff[r, pl.ds(n + LANES, LANES)] = (ghid * gate * sig).astype(HALF)
        return carry

    lax.fori_loop(0, FF // LANES, back, 0)
    sems.finish()


def forward(chunks, hid, cot):
    copies = GATHER_COPIES * 4 + 2 + 8 + SUM_COPIES + 2
    return pl.pallas_call(
        forward_kernel,
        out_shape=[SHAPE(grid_of(w.shape[-1]), HALF) for w in chunks]
        + [
            SHAPE((2, TOK, D), HALF),
            SHAPE((2, TOK, D), HALF),
            SHAPE((2 * TOK, HW), HALF),
            SHAPE((WINDOW + 2 * TOK, 2 * HW), HALF),
            SHAPE((2 * TOK, HW), HALF),
            SHAPE((2 * TOK, HW), SINGLE),
            SHAPE((TOK, D), SINGLE),
            SHAPE((2, TOK, D), HALF),
            SHAPE((2 * TOK, FF), HALF),
            SHAPE((2 * TOK, 2 * FF), HALF),
            SHAPE((8, D), SINGLE),
        ],
        in_specs=[ANYWHERE] * 6,
        out_specs=[ANYWHERE] * 4 + [IN_VMEM, ANYWHERE] + [IN_VMEM] * 9,
        scratch_shapes=[
            pltpu.VMEM((2, TOK, D), HALF),
            pltpu.VMEM(grid_of(chunks[W_QKV].shape[-1]), HALF),
            pltpu.VMEM(grid_of(HW), HALF),
            pltpu.VMEM(grid_of(2 * FF), HALF),
            pltpu.VMEM((2, TOK, D), HALF),
            pltpu.VMEM((2 * TOK, 2 * FF), SINGLE),
        ]
        + SUM_SCRATCH
        + [
            pltpu.SemaphoreType.DMA((copies,)),
            pltpu.SemaphoreType.DMA((copies,)),
            pltpu.SemaphoreType.DMA((4 + 2 + 5,)),
        ],
        compiler_params=params(0),
    )(*chunks, hid, cot)


def backward_kernel(*refs):
    (
        w_ff,
        w_out,
        cots,
        hid_in,
        grad_ff_in,
        a2_in,
        mid_in,
        gains,
        q_in,
        kv_in,
        lse_in,
    ) = refs[:11]
    s_down, s_ffa, s_ffb, gmid, gatt, gq, gkv, ffn_term = refs[11:19]
    g_refs, slot_refs = refs[19:22], refs[22:28]
    rest = refs[28:]
    scatter_bufs, rest = [rest[6 * i : 6 * i + 6] for i in range(3)], rest[18:]
    sum_bufs, rest = rest[:5], rest[5:]
    (
        temp,
        staging,
        cot_v,
        hid_ff,
        grad_ff,
        a2,
        mid,
        q,
        kv,
        lse,
        w_tiles,
        w_o,
        go,
        acc,
        own_kv,
        far,
        got,
        send,
        recv,
        local_sems,
    ) = rest
    x, y, z, c, t = coords()
    chip = lax.div(lax.axis_index("seq"), 2)
    core, pair = device(x, y, z, 1 - c, t), device(x, y, z, c, 1 - t)
    sems, local = Sems(send, recv), Locals(local_sems)
    loads = {
        name: local.load(src, dst)
        for name, src, dst in (
            ("grad_ff", grad_ff_in, grad_ff),
            ("cot", cots, cot_v),
            ("hid", hid_in, hid_ff),
            ("a2", a2_in, a2),
            ("mid", mid_in, mid),
            ("w_o", w_out, w_o),
            ("q", q_in, q),
            ("kv", kv_in, kv),
            ("lse", lse_in, lse),
        )
    }
    tiles = [local.copy(w_ff.at[i // 2, i % 2], w_tiles.at[i % 2]) for i in range(8)]
    tiles[0].start()
    tiles[1].start()
    greet(neighbours() + [pair] + window_chips())

    plan = Plan()
    for i, (begin, length, out) in enumerate(((1, 30, s_down), (2, 58, s_ffa), (3, 86, s_ffb))):
        plan_scatter(
            plan,
            begin,
            length,
            g_refs[i],
            out,
            slot_refs[2 * i : 2 * i + 2],
            scatter_bufs[i],
            temp,
            sems,
            local,
        )

    loads["grad_ff"].wait()
    gn2 = FourSum(sum_bufs, sems)
    theirs, ours = [pl.ds(pl.multiple_of(k * TOK, TOK), TOK) for k in (1 - c, c)]
    for i in range(PARTS):
        parts = []
        for k in range(2):
            tiles[2 * i + k].wait()
            w_rows = w_tiles[k].reshape(256, 2 * FF)
            parts.append(
                [product(grad_ff[r, :], w_rows, ((1,), (1,))) for r in (theirs, ours)]
            )
            if 2 * i + k + 2 < 8:
                tiles[2 * i + k + 2].start()
        gn2.put(i, *[jnp.concatenate([parts[0][j], parts[1][j]], axis=1) for j in range(2)])

    loads["cot"].wait()
    loads["hid"].wait()
    make_grads(cot_v, lambda: hid_ff[...], staging, g_refs[0], local)
    plan.until(1)
    for i in range(PARTS):
        gn2.relay(i)
    loads["a2"].wait()
    make_grads(a2, lambda: grad_ff[:, :FF], staging, g_refs[1], local)
    plan.until(2)
    make_grads(a2, lambda: grad_ff[:, FF:], staging, g_refs[2], local)
    plan.until(14)

    gn2.wait()
    loads["mid"].wait()
    ffn_term[...] = jnp.zeros_like(ffn_term)
    spreads = []
    for half in range(2):

        def mid_back(r):
            part, term = norm_back(gn2.total(r), mid[r, :], gains[1:2, :])
            grad = cot_v[c, r, :].astype(SINGLE) + part
            gmid[r, :] = grad
            gatt[c, r, :] = grad.astype(HALF)
            ffn_term[0:1, :] += term

        row_loop(half * 128, 128, mid_back)
        part = gatt.at[c, half * 128 : (half + 1) * 128]
        copy = sems.copy(part, part, core)
        sems.start(copy)
        spreads.append(copy)
    plan.until(20)
    loads["w_o"].wait()
    for copy in spreads:
        copy.wait_recv()
    for half in range(2):
        total = product(gatt[half, :, 0:PART], w_o[0].reshape(PART, HW), ((1,), (0,)))
        for i in range(1, PARTS):
            total += product(
                gatt[half, :, i * PART : (i + 1) * PART], w_o[i].reshape(PART, HW), ((1,), (0,))
            )
        go[half * TOK : (half + 1) * TOK, :] = total.astype(HALF)
    for name in ("q", "kv", "lse"):
        loads[name].wait()
    returns = []
    for h in range(4):
        head = slice(h * HD, (h + 1) * HD)
        both = slice(2 * h * HD, (2 * h + 2) * HD)
        key_head = slice(2 * h * HD, (2 * h + 1) * HD)
        value_head = slice((2 * h + 1) * HD, (2 * h + 2) * HD)
        acc[...] = jnp.zeros_like(acc)

        def attend_one(i, carry):
            mine = pl.ds(pl.multiple_of(i * QB, QB), QB)
            keys = pl.ds(pl.multiple_of(i * QB, QB), KB)
            base = (chip - 2) * 512 + i * QB
            grad_q, grad_k, grad_v = attend_block_back(
                q[mine, head],
                kv[keys, key_head],
                kv[keys, value_head],
                go[mine, head],
                lse[mine, h * HD : h * HD + 1],
                base,
            )
            gq[mine, head] = grad_q.astype(HALF)
            acc[keys, 0:HD] += grad_k
            acc[keys, HD:] += grad_v
            return carry

        lax.fori_loop(0, 2, attend_one, 0)
        copies = []
        for j, shift in ((1, -1), (0, -2)):
            far[j, :, both] = acc[512 * j : 512 * (j + 1), :].astype(HALF)
            copies.append(sems.copy(far.at[j, :, both], got.at[j, :, both], chip_shift(shift)))
        sems.start(*copies)
        returns.append(copies)
        own_kv[:, both] = acc[1024:1536, :]
        plan.until(26 + 5 * h)
    for h in range(4):
        both = slice(2 * h * HD, (2 * h + 2) * HD)
        for copy in returns[h]:
            copy.wait_recv()

        def add(r):
            total = (
                own_kv[r, both] + got[1, r, both].astype(SINGLE) + got[0, r, both].astype(SINGLE)
            )
            gkv[r, both] = total.astype(HALF)

        row_loop(0, 512, add, 64)
        plan.until(46 + 5 * h)
    plan.rest()
    sems.finish()


def backward(w_ff, w_out, cots, hid_ff, grad_ff, a2, mid, gains, q, kv, lse):
    widths = (FF, FF, FF)
    copies = SCATTER_COPIES * 3 + SUM_COPIES + 2 + 8
    slots = [slot for w in widths for slot in scatter_slots(w)]
    return pl.pallas_call(
        backward_kernel,
        out_shape=[SHAPE((2, 32, w), SINGLE) for w in widths]
        + [
            SHAPE((TOK, D), SINGLE),
            SHAPE((2, TOK, D), HALF),
            SHAPE((2 * TOK, HW), HALF),
            SHAPE((2 * TOK, 2 * HW), HALF),
            SHAPE((8, D), SINGLE),
        ]
        + [SHAPE(grid_of(w), HALF) for w in widths]
        + slots,
        in_specs=[ANYWHERE] * 7 + [IN_VMEM] + [ANYWHERE] * 3,
        out_specs=[IN_VMEM] * 8 + [ANYWHERE] * (3 + len(slots)),
        scratch_shapes=[buf for w in widths for buf in scatter_scratch(w)]
        + SUM_SCRATCH
        + [
            pltpu.VMEM((2, 2, 2, 4, 32, FF), HALF),
            pltpu.VMEM((2, 4, 2, 32, FF), HALF),
            pltpu.VMEM((2, TOK, D), HALF),
            pltpu.VMEM((2 * TOK, FF), HALF),
            pltpu.VMEM((2 * TOK, 2 * FF), HALF),
            pltpu.VMEM((2, TOK, D), HALF),
            pltpu.VMEM((TOK, D), SINGLE),
            pltpu.VMEM((2 * TOK, HW), HALF),
            pltpu.VMEM((WINDOW + 2 * TOK, 2 * HW), HALF),
            pltpu.VMEM((2 * TOK, HW), SINGLE),
            pltpu.VMEM((2, 4, 2, 32, 2 * FF), HALF),
            pltpu.VMEM(grid_of(HW), HALF),
            pltpu.VMEM((2 * TOK, HW), HALF),
            pltpu.VMEM((WINDOW + 2 * TOK, 2 * HD), SINGLE),
            pltpu.VMEM((2 * TOK, 2 * HW), SINGLE),
            pltpu.VMEM((2, 2 * TOK, 2 * HW), HALF),
            pltpu.VMEM((2, 2 * TOK, 2 * HW), HALF),
            pltpu.SemaphoreType.DMA((copies,)),
            pltpu.SemaphoreType.DMA((copies,)),
            pltpu.SemaphoreType.DMA((9 + 8 + SCATTER_LOADS * 3 + 2 * 3,)),
        ],
        compiler_params=params(1),
    )(w_ff, w_out, cots, hid_ff, grad_ff, a2, mid, gains, q, kv, lse)


def finish_kernel(*refs):
    w_qkv, w_down, a1_in, gq, gkv, gatt, o, hid_ff, mid, gmid, hid, gains, ffn_term = refs[:13]
    s_out, s_qkv, s_gain, in_grad, hidden_out = refs[13:18]
    g_refs, slot_refs = refs[18:21], refs[21:27]
    rest = refs[27:]
    scatter_bufs, rest = [rest[6 * i : 6 * i + 6] for i in range(3)], rest[18:]
    in_bufs, out_bufs, rest = rest[:5], rest[5:10], rest[10:]
    temp, staging, staging_o, gqkv, gain_acc, a1, w_tiles, d_tiles, send, recv, local_sems = rest
    x, y, z, c, t = coords()
    core, pair = device(x, y, z, 1 - c, t), device(x, y, z, c, 1 - t)
    sems, local = Sems(send, recv), Locals(local_sems)
    load_a1 = local.load(a1_in, a1)
    w_loads = [
        local.copy(w_qkv.at[i // 2, i % 2, :, :, :, 0 : 3 * HW], w_tiles.at[i % 2])
        for i in range(8)
    ]
    d_loads = [local.copy(w_down.at[i // 2, i % 2], d_tiles.at[i % 2]) for i in range(8)]
    for load in (*w_loads[:2], *d_loads[:2]):
        load.start()
    gqkv[:, :HW] = gq[...]
    gqkv[:, HW:] = gkv[...]
    greet(neighbours() + [pair])
    plan = Plan()
    for i, (begin, length, out) in enumerate(((1, 12, s_out), (0, 42, s_qkv), (30, 25, s_gain))):
        plan_scatter(
            plan,
            begin,
            length,
            g_refs[i],
            out,
            slot_refs[2 * i : 2 * i + 2],
            scatter_bufs[i],
            temp,
            sems,
            local,
        )
    load_a1.wait()
    make_grads(a1, lambda: gqkv[...], staging, g_refs[1], local)
    plan.until(0)
    theirs, ours = [pl.ds(pl.multiple_of(k * TOK, TOK), TOK) for k in (1 - c, c)]

    def partial_sum(bufs, left, right, loads, depth):
        total = FourSum(bufs, sems)
        for i in range(PARTS):
            parts = []
            for k in range(2):
                loads[2 * i + k].wait()
                w_rows = right[k].reshape(256, depth)
                parts.append([product(left[r, :], w_rows, ((1,), (1,))) for r in (theirs, ours)])
                if 2 * i + k + 2 < 8:
                    loads[2 * i + k + 2].start()
            total.put(i, *[jnp.concatenate([parts[0][j], parts[1][j]], axis=1) for j in range(2)])
        return total

    gn1 = partial_sum(in_bufs, gqkv, w_tiles, w_loads, 3 * HW)
    make_grads(gatt, lambda: o[...], staging_o, g_refs[0], local)
    plan.until(2)
    for i in range(PARTS):
        gn1.relay(i)
    out_sum = partial_sum(out_bufs, hid_ff, d_tiles, d_loads, FF)
    plan.until(6)
    for i in range(PARTS):
        out_sum.relay(i)
    plan.until(18)
    gn1.wait()
    gain_acc[...] = jnp.zeros_like(gain_acc)

    def rows_back(r):
        part, term = norm_back(gn1.total(r), hid[r, :].astype(SINGLE), gains[0:1, :])
        in_grad[r, :] = gmid[r, :] + part
        gain_acc[0:1, :] += term

    row_loop(0, TOK, rows_back)
    gain_acc[1:2, :] = ffn_term[0:1, :]
    pick = pick_lanes().astype(HALF)
    for n in range(8):
        cols = product(
            gain_acc[:, n * 256 : (n + 1) * 256].astype(HALF), pick, ((0,), (0,))
        ).astype(HALF)
        staging_o[0, :, :, :, 0:LANES] = cols.reshape(4, 2, 32, LANES)
        copy = local.load(staging_o.at[0, :, :, :, 0:LANES], g_refs[2].at[n // 2, n % 2])
        copy.wait()
    plan.until(30)
    out_sum.wait()

    def rows_out(r):
        hidden_out[r, :] = (mid[r, :] + out_sum.total(r)).astype(HALF)

    row_loop(0, TOK, rows_out)
    plan.rest()
    sems.finish()


def finish(w_qkv, w_down, a1, gq, gkv, gatt, o, hid_ff, mid, gmid, hid, gains, ffn_term):
    widths = (HW, 3 * HW, LANES)
    copies = SCATTER_COPIES * 3 + SUM_COPIES * 2
    slots = [slot for w in widths for slot in scatter_slots(w)]
    return pl.pallas_call(
        finish_kernel,
        out_shape=[SHAPE((2, 32, w), SINGLE) for w in widths]
        + [SHAPE((TOK, D), SINGLE), SHAPE((TOK, D), HALF)]
        + [SHAPE(grid_of(w), HALF) for w in widths]
        + slots,
        in_specs=[ANYWHERE] * 3 + [IN_VMEM] * 10,
        out_specs=[IN_VMEM] * 5 + [ANYWHERE] * (3 + len(slots)),
        scratch_shapes=[buf for w in widths for buf in scatter_scratch(w)]
        + SUM_SCRATCH
        + SUM_SCRATCH
        + [
            pltpu.VMEM((2, 2, 2, 4, 32, 3 * HW), HALF),
            pltpu.VMEM((2, 4, 2, 32, 3 * HW), HALF),
            pltpu.VMEM((2, 4, 2, 32, HW), HALF),
            pltpu.VMEM((2 * TOK, 3 * HW), HALF),
            pltpu.VMEM((8, D), SINGLE),
            pltpu.VMEM((2, TOK, D), HALF),
            pltpu.VMEM((2, 4, 2, 32, 3 * HW), HALF),
            pltpu.VMEM((2, 4, 2, 32, FF), HALF),
            pltpu.SemaphoreType.DMA((copies,)),
            pltpu.SemaphoreType.DMA((copies,)),
            pltpu.SemaphoreType.DMA((1 + 8 + 8 + SCATTER_LOADS * 3 + 2 * 2 + 8,)),
        ],
        compiler_params=params(2),
    )(w_qkv, w_down, a1, gq, gkv, gatt, o, hid_ff, mid, gmid, hid, gains, ffn_term)


def halves(matrix):
    rows, width = matrix.shape
    padded = -(-width // 256) * 256
    matrix = jnp.pad(matrix, ((0, 0), (0, padded - width)))
    return jnp.moveaxis(matrix.reshape(rows, 2, padded // 2), 1, 0)


def interleave(first, second):
    cut = lambda m: m.reshape(2, m.shape[1], -1, 1, LANES)
    return jnp.concatenate([cut(first), cut(second)], axis=3).reshape(2, first.shape[1], -1)


def apart(both):
    cut = both.reshape(2, both.shape[1], -1, 2, LANES)
    return [cut[:, :, :, i].reshape(2, both.shape[1], -1) for i in range(2)]


def whole(parts, width):
    return jnp.moveaxis(parts, 0, 1).reshape(parts.shape[1], -1)[:, :width]


def per_device(
    hidden_in, attn_gain, w_query, w_key, w_value, w_out, ffn_gain, w_gate, w_up, w_down, out_grad
):
    hidden_units = w_gate.shape[1]
    gains = jnp.pad(jnp.stack([attn_gain, ffn_gain], axis=1), ((0, 0), (0, LANES - 2)))
    gains = jnp.broadcast_to(gains, (2, *gains.shape))
    chunk_qkv = jnp.concatenate(
        [halves(w_query), interleave(halves(w_key), halves(w_value)), gains], axis=2
    ).astype(HALF)
    chunk_out = halves(w_out.T).astype(HALF)
    chunk_ff = interleave(halves(w_gate), halves(w_up)).astype(HALF)
    chunk_down = halves(w_down.T).astype(HALF)

    w_qkv, w_o, w_ff, w_d, a1, cots, q, kv, o, lse, mid, a2, hid_ff, grad_ff, gain_rows = forward(
        [chunk_qkv, chunk_out, chunk_ff, chunk_down], hidden_in, out_grad
    )
    s_down, s_ffa, s_ffb, gmid, gatt, gq, gkv, ffn_term, *_ = backward(
        w_ff, w_o, cots, hid_ff, grad_ff, a2, mid, gain_rows, q, kv, lse
    )
    s_out, s_qkv, s_gain, in_grad, hidden_out, *_ = finish(
        w_qkv, w_d, a1, gq, gkv, gatt, o, hid_ff, mid, gmid, hidden_in, gain_rows, ffn_term
    )
    gain_sum = s_gain[0] + s_gain[1]
    s_key, s_value = apart(s_qkv[:, :, HW:])
    s_gate, s_up = apart(jnp.concatenate([s_ffa, s_ffb], axis=2))
    return (
        hidden_out,
        in_grad,
        gain_sum[:, 0],
        whole(s_qkv[:, :, :HW], 2 * HW),
        whole(s_key, 2 * HW),
        whole(s_value, 2 * HW),
        whole(s_out, 2 * HW).T,
        gain_sum[:, 1],
        whole(s_gate, hidden_units),
        whole(s_up, hidden_units),
        whole(s_down, hidden_units).T,
    )


def solution(mesh):
    placed = (
        P("seq", None),
        P("seq"),
        P("seq", "tp"),
        P("seq", "tp"),
        P("seq", "tp"),
        P("tp", "seq"),
        P("seq"),
        P("seq", "tp"),
        P("seq", "tp"),
        P("tp", "seq"),
        P("seq", None),
    )
    return jax.shard_map(
        per_device,
        mesh=mesh,
        in_specs=placed,
        out_specs=(
            P("seq", None),
            P("seq", None),
            P("seq"),
            P("seq", "tp"),
            P("seq", "tp"),
            P("seq", "tp"),
            P("tp", "seq"),
            P("seq"),
            P("seq", "tp"),
            P("seq", "tp"),
            P("tp", "seq"),
        ),
        check_vma=False,
    )
```

```python
import functools
import math

import jax
import jax.numpy as jnp
from jax import lax
from jax.experimental import pallas as pl
from jax.experimental.pallas import tpu as pltpu
from jax.sharding import PartitionSpec as P

HD = 128
WINDOW = 1024
EPSILON = 1e-06
MASKED = -1e30
MESH = pl.DeviceIdType.MESH
HALF = jnp.bfloat16
SINGLE = jnp.float32
VMEM_LIMIT = 63 * 2**20

D = 2048
TOK = 256
HW = 512
FF = 1408
FFA, FFB = 1536, 1280
QB = 256
KB = QB + WINDOW
SCALE = 1.0 / math.sqrt(HD)
ROWS = 16
LANES = 128
PART = 512
PARTS = D // PART

ANYWHERE = pl.BlockSpec(memory_space=pl.ANY)
IN_VMEM = pl.BlockSpec(memory_space=pltpu.VMEM)
SHAPE = jax.ShapeDtypeStruct


def coords():
    s = lax.axis_index("seq")
    t = lax.axis_index("tp")
    return lax.rem(lax.div(s, 2), 4), lax.div(s, 16), lax.rem(lax.div(s, 8), 2), lax.rem(s, 2), t


def device(x, y, z, c, t):
    return (((y * 2 + z) * 4 + x) * 2 + c, t)


def moved(v, steps):
    return lax.rem(v + steps + 4, 4)


def chip_shift(steps):
    s = lax.axis_index("seq")
    return (lax.rem(s + 2 * steps + 64, 64), lax.axis_index("tp"))


def neighbours():
    x, y, z, c, t = coords()
    return [
        device(moved(x, 1), y, z, c, t),
        device(moved(x, -1), y, z, c, t),
        device(x, moved(y, 1), z, c, t),
        device(x, moved(y, -1), z, c, t),
        device(x, y, 1 - z, c, t),
        device(x, y, z, 1 - c, t),
    ]


def greet(partners):
    barrier = pltpu.get_barrier_semaphore()
    for partner in partners:
        pl.semaphore_signal(barrier, inc=1, device_id=partner, device_id_type=MESH)
    pl.semaphore_wait(barrier, len(partners))


class Sems:
    def __init__(self, send, recv):
        self.send, self.recv, self.used, self.started = send, recv, 0, []

    def copy(self, src, dst, dev):
        i = self.used
        self.used += 1
        return pltpu.make_async_remote_copy(
            src, dst, self.send.at[i], self.recv.at[i], device_id=dev, device_id_type=MESH
        )

    def start(self, *copies):
        for copy in copies:
            copy.start()
            self.started.append(copy)

    def sent(self, copies):
        for copy in copies:
            copy.wait_send()
            self.started = [other for other in self.started if other is not copy]

    def finish(self):
        self.sent(list(self.started))


class Locals:
    def __init__(self, sems):
        self.sems, self.used = sems, 0

    def sem(self):
        self.used += 1
        return self.sems.at[self.used - 1]

    def copy(self, src, dst):
        return pltpu.make_async_copy(src, dst, self.sem())

    def load(self, src, dst):
        copy = self.copy(src, dst)
        copy.start()
        return copy


class Tasks:
    def __init__(self):
        self.tasks = {}

    def add(self, name, task):
        self.tasks[name] = task

    def run(self, order):
        tasks = list(self.tasks.values())
        assert sorted(order) == list(range(len(tasks)))
        for i in order:
            tasks[i]()


def grid_piece(along_x):
    x, y, z, c, t = coords()
    if along_x:
        return x, y, lambda v: device(v, y, z, c, t), lambda v: device(x, v, z, c, t)
    return y, x, lambda v: device(x, v, z, c, t), lambda v: device(v, y, z, c, t)


def blocks(ref, along_x, h, a, zs, b):
    return ref.at[b, zs, a, h] if along_x else ref.at[a, zs, b, h]


ALL = slice(None)


GATHER_COPIES = 1 + 4 * 6 + 8


def gather_streams(along, out, sems, planes, rows):
    streams = []
    for h in range(2):
        a, b, to_a, to_b = grid_piece(along[h])
        for s, d in ((0, 1), (1, -1)):

            def copy(aa, bb, dev, h=h, s=s):
                src = blocks(out, along[h], h, aa, planes[s], bb)
                src = src.at[rows[s]] if aa is not ALL else src.at[:, rows[s]]
                return sems.copy(src, src, dev)

            streams.append(
                dict(
                    a1f=copy(a, b, to_a(moved(a, d))),
                    a1r=copy(a, b, to_a(moved(a, -d))),
                    a2=copy(moved(a, -d), b, to_a(moved(a, d))),
                    b1f=copy(ALL, b, to_b(moved(b, d))),
                    b1r=copy(ALL, b, to_b(moved(b, -d))),
                    b2=copy(ALL, moved(b, -d), to_b(moved(b, d))),
                )
            )
    return streams


def add_gather(tasks, label, along, w_in, out, target, sems, local):
    x, y, z, c, t = coords()
    mine = local.copy(w_in.at[c], out.at[y, z, x, c])
    swap = sems.copy(w_in.at[1 - c], out.at[y, z, x, c], device(x, y, z, 1 - c, t))
    load = local.copy(out, target)
    over_z = []
    for h in range(2):
        src = out.at[y, z, x, h]
        over_z.append(sems.copy(src, src, device(x, y, 1 - z, c, t)))
    streams = gather_streams(along, out, sems, (z, 1 - z), (ALL, ALL))
    add = lambda name, task: tasks.add(f"{label}.{name}", task)

    def init():
        mine.start()
        sems.start(swap)

    def own():
        mine.wait()
        swap.wait_recv()
        sems.start(*over_z)
        for p in streams[0::2]:
            sems.start(p["a1f"], p["a1r"])

    def other():
        for copy in over_z:
            copy.wait_recv()
        for p in streams[1::2]:
            sems.start(p["a1f"], p["a1r"])

    def a2(ps):
        for p in ps:
            p["a1f"].wait_recv()
            sems.start(p["a2"])

    def b1(ps):
        for p in ps:
            p["a1r"].wait_recv()
            p["a2"].wait_recv()
            sems.start(p["b1f"], p["b1r"])

    def b2(ps):
        for p in ps:
            p["b1f"].wait_recv()
            sems.start(p["b2"])

    def end():
        for p in streams:
            p["b1r"].wait_recv()
            p["b2"].wait_recv()
        load.start()

    add("init", init)
    add("own", own)
    add("other", other)
    for s in range(2):
        add(f"a2{s}", lambda s=s: a2(streams[s::2]))
        add(f"b1{s}", lambda s=s: b1(streams[s::2]))
        add(f"b2{s}", lambda s=s: b2(streams[s::2]))
    add("end", end)
    return load


def add_plane_gather(tasks, label, along, w_in, out, target, sems, local):
    x, y, z, c, t = coords()
    mine = local.copy(w_in.at[c], out.at[y, z, x, c])
    swap = sems.copy(w_in.at[1 - c], out.at[y, z, x, c], device(x, y, z, 1 - c, t))
    load = local.copy(out, target)
    streams = gather_streams(along, out, sems, (z, z), (slice(0, 16), slice(16, 32)))
    over_z = {}
    for h in range(2):
        a, b, to_a, to_b = grid_piece(along[h])
        for k in range(4):
            src = blocks(out, along[h], h, ALL, z, moved(b, k))
            over_z[h, k] = sems.copy(src, src, device(x, y, 1 - z, c, t))
    add = lambda name, task: tasks.add(f"{label}.{name}", task)

    def cross(*steps):
        for k in steps:
            sems.start(over_z[0, k], over_z[1, k])

    def init():
        mine.start()
        sems.start(swap)

    def own():
        mine.wait()
        swap.wait_recv()
        for p in streams:
            sems.start(p["a1f"], p["a1r"])

    def a2():
        for p in streams:
            p["a1f"].wait_recv()
            sems.start(p["a2"])

    def b1():
        for p in streams:
            p["a1r"].wait_recv()
            p["a2"].wait_recv()
            sems.start(p["b1f"], p["b1r"])
        cross(0)

    def b2():
        for p in streams:
            p["b1f"].wait_recv()
            sems.start(p["b2"])

    def zs():
        for p in streams:
            p["b1r"].wait_recv()
        cross(1, 3)

    def ze():
        for p in streams:
            p["b2"].wait_recv()
        cross(2)

    def end():
        for copy in over_z.values():
            copy.wait_recv()
        load.start()

    for task in (init, own, a2, b1, b2, zs, ze, end):
        add(task.__name__, task)
    return load


SCATTER_COPIES = 4 * 6 + 3
SCATTER_LOADS = 16


def scatter_slots(w):
    return [SHAPE((2, 2, 4, 32, w), HALF), SHAPE((2, 2, 2, 4, 32, w), HALF)]


def scatter_scratch(w):
    return [
        pltpu.VMEM((2, 2, 32, w), HALF),
        pltpu.VMEM((2, 2, 2, 32, w), HALF),
        pltpu.VMEM((2, 32, w), HALF),
        pltpu.VMEM((2, 32, w), SINGLE),
    ]


def scatter_shared(w):
    return [
        pltpu.VMEM((2, 2, 2, 4, 32, w), HALF),
        pltpu.VMEM((2, 2, 2, 4, 32, w), HALF),
        pltpu.VMEM((2, 2, 4, 32, w), HALF),
        pltpu.VMEM((2, 2, 2, 4, 32, w), HALF),
        pltpu.VMEM((2, 32, w), SINGLE),
    ]


def plus(ref, *others):
    total = ref[...].astype(SINGLE)
    for other in others:
        total = total + other[...].astype(SINGLE)
    ref[...] = total.astype(HALF)


class Scatter:
    def __init__(self, tasks, shared, sems, local):
        self.tasks, self.sems, self.local = tasks, sems, local
        self.sending, self.owned, self.temp_b, self.temp_a, self.final = shared
        self.count = 0
        self.busy = {}

    def take(self, key, copies):
        self.sems.sent(self.busy.get(key, []))
        self.busy[key] = copies

    def add(self, label, along, g, place, slots, scratch):
        sems, local = self.sems, self.local
        x, y, z, c, t = coords()
        slot = self.count % 2
        self.count += 1
        r2, r1 = slots
        q2, q1, rz, kept = scratch
        wide = slice(0, g.shape[-1])
        tt = self.sending.at[slot, :, :, :, :, wide]
        ss = self.owned.at[slot, :, :, :, :, wide]
        final = self.final.at[:, :, wide]
        streams = []
        for h in range(2):
            a, b, to_a, to_b = grid_piece(along[h])
            for s, zs, d in ((0, z, 1), (1, 1 - z, -1)):
                at_g = lambda bb, h=h, zs=zs: blocks(g, along[h], h, ALL, zs, bb)
                tmp_b, tmp_a = self.temp_b.at[h, s, :, :, wide], self.temp_a.at[h, s, :, :, :, wide]
                forward, back = to_b(moved(b, d)), to_b(moved(b, -d))
                own = ss.at[h, s]
                streams.append(
                    dict(
                        h=h,
                        s=s,
                        a=a,
                        d=d,
                        tt=tt.at[h, s],
                        ss=own,
                        tmp_b=tmp_b,
                        tmp_a=tmp_a,
                        load_t=local.copy(at_g(moved(b, d)), tt.at[h, s]),
                        load_s=local.copy(at_g(b), own),
                        load_2=local.copy(r2.at[h, s], tmp_b),
                        load_1=local.copy(r1.at[h, s], tmp_a),
                        x2=sems.copy(at_g(moved(b, 2)), r2.at[h, s], forward),
                        x1r=sems.copy(at_g(moved(b, -d)), r1.at[h, s, 1], back),
                        x1f=sems.copy(tt.at[h, s], r1.at[h, s, 0], forward),
                        y2=sems.copy(own.at[moved(a, 2)], q2.at[h, s], to_a(moved(a, d))),
                        y1r=sems.copy(own.at[moved(a, -d)], q1.at[h, s, 1], to_a(moved(a, -d))),
                        y1f=sems.copy(own.at[moved(a, d)], q1.at[h, s, 0], to_a(moved(a, d))),
                    )
                )
        over_z = [
            sems.copy(ss.at[h, 1, grid_piece(along[h])[0]], rz.at[h], device(x, y, 1 - z, c, t))
            for h in range(2)
        ]
        swap = sems.copy(final.at[1 - c], kept.at[1], device(x, y, z, 1 - c, t))

        def start():
            for p in streams:
                sems.start(p["x2"], p["x1r"])

        def x1a():
            self.take(("sending", slot), [p["x1f"] for p in streams])
            for p in streams:
                p["load_t"].start()
            for p in streams:
                p["x2"].wait_recv()
                p["load_2"].start()

        def x1b():
            for p in streams:
                p["load_t"].wait()
                p["load_2"].wait()

                def body(i, carry, p=p):
                    plus(p["tt"].at[i], p["tmp_b"].at[i])
                    return carry

                lax.fori_loop(0, 4, body, 0)
                sems.start(p["x1f"])

        def x0a():
            used = [p[name] for p in streams for name in ("y2", "y1r", "y1f")]
            self.take(("owned", slot), used + over_z)
            for p in streams:
                p["load_s"].start()
            for p in streams:
                p["x1r"].wait_recv()
                p["x1f"].wait_recv()
                p["load_1"].start()

        def x0b():
            for p in streams:
                p["load_s"].wait()
                p["load_1"].wait()

                def body(i, carry, p=p):
                    plus(p["ss"].at[i], p["tmp_a"].at[0, i], p["tmp_a"].at[1, i])
                    return carry

                lax.fori_loop(0, 4, body, 0)
                sems.start(p["y2"], p["y1r"])

        def y1():
            for p in streams:
                p["y2"].wait_recv()
                plus(p["ss"].at[moved(p["a"], p["d"])], q2.at[p["h"], p["s"]])
                sems.start(p["y1f"])

        def y0():
            for p in streams:
                h, s = p["h"], p["s"]
                p["y1f"].wait_recv()
                p["y1r"].wait_recv()
                plus(p["ss"].at[p["a"]], q1.at[h, s, 0], q1.at[h, s, 1])
                if s == 1:
                    sems.start(over_z[h])

        def last():
            self.take("final", [swap])
            for p in streams:
                h = p["h"]
                if p["s"] == 0:
                    over_z[h].wait_recv()
                    own = p["ss"].at[p["a"]]
                    final[h] = own[...].astype(SINGLE) + rz[h].astype(SINGLE)
            kept[0] = final[c]
            sems.start(swap)

        def done():
            swap.wait_recv()

            def read(j, start):
                lanes = slice(start, start + LANES)
                return jnp.where(c == j, kept[0, :, lanes], kept[1, :, lanes])

            place(read)

        for task in (start, x1a, x1b, x0a, x0b, y1, y0, last, done):
            self.tasks.add(f"{label}.{task.__name__}", task)


def make_grads(lhs, rhs, staging, g, local, first=0, width=None):
    sems = [local.sem() for _ in range(2)]
    width = width or g.shape[-1]
    wide = slice(0, width)

    def write(i, slot):
        return pltpu.make_async_copy(
            staging.at[slot, :, :, :, wide],
            g.at[i, slot, :, :, :, first : first + width],
            sems[slot],
        )

    def body(i, carry):
        for slot in range(2):
            n = pl.multiple_of(i * 512 + slot * 256, 256)
            left = lhs[:, :, pl.ds(n, 256)].reshape(512, 256)
            tile = product(left, rhs(), ((0,), (0,))).astype(HALF)

            @pl.when(i > 0)
            def _():
                write(i, slot).wait()

            staging[slot, :, :, :, wide] = tile.reshape(4, 2, 32, width)
            write(i, slot).start()
        return carry

    lax.fori_loop(0, 4, body, 0)
    for slot in range(2):
        write(0, slot).wait()


class FourSum:
    def __init__(self, bufs, sems):
        x, y, z, c, t = coords()
        self.to_core, self.from_core, self.from_pair, self.own = bufs
        self.sems = sems
        self.cols = [slice(i * PART, (i + 1) * PART) for i in range(PARTS)]
        core, pair = device(x, y, z, 1 - c, t), device(x, y, z, c, 1 - t)
        self.core = [sems.copy(self.to_core.at[:, n], self.from_core.at[:, n], core) for n in self.cols]
        self.pair = [sems.copy(self.from_core.at[:, n], self.from_pair.at[:, n], pair) for n in self.cols]

    def put(self, i, theirs, ours):
        self.to_core[:, self.cols[i]] = theirs.astype(HALF)
        self.own[:, self.cols[i]] = ours
        self.sems.start(self.core[i])

    def relay(self, i):
        n = self.cols[i]
        self.core[i].wait_recv()

        def add(r):
            self.from_core[r, n] = (self.own[r, n] + self.from_core[r, n].astype(SINGLE)).astype(HALF)

        row_loop(0, TOK, add, 64)
        self.sems.start(self.pair[i])

    def wait(self):
        for copy in self.pair:
            copy.wait_recv()

    def add_relays(self, tasks, label):
        for i in range(PARTS):
            tasks.add(f"{label}.relay{i}", lambda i=i: self.relay(i))

    def total(self, r):
        return self.from_core[r, :].astype(SINGLE) + self.from_pair[r, :].astype(SINGLE)


SUM_COPIES = 2 * PARTS
SUM_SCRATCH = [pltpu.VMEM((TOK, D), HALF) for _ in range(3)] + [pltpu.VMEM((TOK, D), SINGLE)]


def product(a, b, dims):
    return lax.dot_general(a, b, (dims, ((), ())), preferred_element_type=SINGLE)


def allowed_pairs(base):
    row = lax.broadcasted_iota(jnp.int32, (QB, KB), 0)
    col = lax.broadcasted_iota(jnp.int32, (QB, KB), 1)
    return (col > row) & (col <= row + WINDOW) & (col + base >= 0)


def attend_block(q, k, v, base):
    scores = product(q, k, ((1,), (1,))) * SCALE
    scores = jnp.where(allowed_pairs(base), scores, MASKED)
    row_max = jnp.max(scores, axis=-1, keepdims=True)
    expon = jnp.exp(scores - row_max)
    row_total = jnp.sum(expon, axis=-1, keepdims=True)
    probs = (expon * (1.0 / row_total)).astype(HALF)
    mixed = product(probs, v, ((1,), (0,))).astype(HALF)
    return mixed, row_max + jnp.log(row_total)


def attend_block_back(q, k, v, go, lse, base):
    scores = product(q, k, ((1,), (1,))) * SCALE
    scores = jnp.where(allowed_pairs(base), scores, MASKED)
    probs = jnp.exp(scores - lse)
    gp = product(go, v, ((1,), (1,)))
    inner = jnp.sum(probs * gp, axis=-1, keepdims=True)
    gs = (probs * (gp - inner)).astype(HALF)
    gq = product(gs, k, ((1,), (0,))) * SCALE
    gk = product(gs, q, ((0,), (0,))) * SCALE
    gv = product(probs.astype(HALF), go, ((0,), (0,)))
    return gq, gk, gv


def rms_inverse(values):
    return lax.rsqrt(jnp.mean(values * values, axis=-1, keepdims=True) + EPSILON)


def norm_back(grad, values, gain):
    inverse = rms_inverse(values)
    scaled = grad * gain
    slope = jnp.mean(scaled * values, axis=-1, keepdims=True)
    gain_term = jnp.sum(grad * values * inverse, axis=0, keepdims=True)
    return inverse * scaled - values * (inverse * inverse * inverse * slope), gain_term


def row_loop(start, count, fn, step=ROWS):
    def body(i, carry):
        fn(pl.ds(pl.multiple_of(start + i * step, step), step))
        return carry

    lax.fori_loop(0, count // step, body, 0)


def columns(w, n, size):
    return w[:, :, :, :, :, pl.ds(n, size)].reshape(D, size)


def pick_lanes():
    return lax.broadcasted_iota(jnp.int32, (8, LANES), 0) == lax.broadcasted_iota(
        jnp.int32, (8, LANES), 1
    )


def grid_of(w):
    return (4, 2, 4, 2, 32, w)


def params(collective_id):
    return pltpu.CompilerParams(
        collective_id=collective_id, has_side_effects=True, vmem_limit_bytes=VMEM_LIMIT
    )


CHUNKS = ("kv", "q", "out", "ffa", "ffb", "down")
W_KV, W_Q, W_OUT, W_FFA, W_FFB, W_DOWN = range(6)
W_WIDTHS = (2 * HW + LANES, HW, HW, FFA, FFB, FF)
ALONG = (0, 1)
ALONG_X = (1, 1)
FORWARD_ORDER = (
    30, 0, 10, 20, 50, 40, 63, 1, 21, 11, 51, 41, 2, 52, 3, 12, 6, 53, 16, 4, 7, 13, 43, 54, 55,
    5, 31, 23, 8, 56, 14, 9, 58, 17, 24, 22, 64, 65, 15, 26, 18, 66, 67, 68, 69, 33, 27, 25, 19,
    70, 32, 28, 71, 34, 29, 59, 57, 62, 84, 85, 44, 72, 73, 42, 36, 35, 74, 75, 76, 77, 46, 45,
    78, 79, 37, 80, 81, 47, 38, 48, 82, 83, 39, 60, 86, 49, 61, 87,
)


class Exchange:
    def __init__(self, sems, mine, copies):
        self.sems, self.mine, self.copies = sems, mine, copies

    def start(self):
        self.mine.start()
        self.sems.start(*self.copies)

    def wait(self):
        self.mine.wait()
        for copy in self.copies:
            copy.wait_recv()


def exchange(sems, local, part, place):
    x, y, z, c, t = coords()
    copies = []
    for d in (2, 1, -1):
        to = moved(x, d)
        copies.append(sems.copy(part(to), place(x), device(to, y, z, c, t)))
    return Exchange(sems, local.copy(part(x), place(x)), copies)


def own_rows(start, v):
    return pl.ds(pl.multiple_of(start + v * 2 * TOK, 2 * TOK), 2 * TOK)


def head_lanes(v, width):
    return pl.ds(pl.multiple_of(v * width, width), width)


def block_rows(i):
    start = pl.multiple_of(i * QB, QB)
    return pl.ds(start, QB), pl.ds(start, KB)


def first_key(i):
    return lax.div(lax.axis_index("seq"), 8) * 2 * WINDOW - WINDOW + i * QB


def arrange(raw, chunks):
    gain_one, gain_two, query, key, value, out, gate, up, down = raw
    to_kv, to_q, to_out, to_ffa, to_ffb, to_down = chunks
    lane = lax.broadcasted_iota(jnp.int32, (32, LANES), 1)
    one, two = [jnp.broadcast_to(g[...], (LANES, 32)).T for g in (gain_one, gain_two)]
    gains = jnp.where(lane == 0, one, jnp.where(lane == 1, two, 0.0)).astype(HALF)
    for j in range(2):
        to_kv[j, :, 2 * HW :] = gains
        to_q[j] = query[:, j * HW : (j + 1) * HW].astype(HALF)
        for h in range(4):
            lanes = slice((4 * j + h) * HD, (4 * j + h + 1) * HD)
            to_kv[j, :, 2 * h * HD : (2 * h + 1) * HD] = key[:, lanes].astype(HALF)
            to_kv[j, :, (2 * h + 1) * HD : (2 * h + 2) * HD] = value[:, lanes].astype(HALF)
            to_out[j, :, h * HD : (h + 1) * HD] = out[:, lanes].astype(HALF)
    blocks_count = FF // LANES
    for j in range(2):
        for i in range(blocks_count):
            n = (j * blocks_count + i) * LANES
            last = min(n + LANES, gate.shape[1])
            parts = [w[:, n:last] for w in (gate, up, down)]
            if last < n + LANES:
                zeros = jnp.zeros((32, n + LANES - last), SINGLE)
                parts = [jnp.concatenate([part, zeros], axis=1) for part in parts]
            chunk, m = (to_ffa, 2 * i * LANES) if 2 * i * LANES < FFA else (to_ffb, 2 * i * LANES - FFA)
            chunk[j, :, m : m + LANES] = parts[0].astype(HALF)
            chunk[j, :, m + LANES : m + 2 * LANES] = parts[1].astype(HALF)
            to_down[j, :, i * LANES : (i + 1) * LANES] = parts[2].astype(HALF)


def forward_kernel(*refs):
    n_w = len(CHUNKS)
    raw_in, (hid, cot), rest = refs[:9], refs[9:11], refs[11:]
    w_out, kept, gains, rest = rest[:n_w], rest[n_w : n_w + 10], rest[n_w + 10], rest[n_w + 11 :]
    results, rest = rest[:10], rest[10:]
    a1, cots, q, kv, o, lse, mid, a2, hid_ff, grad_ff = results
    raw, w_in, rest = rest[:9], rest[9 : 9 + n_w], rest[9 + n_w :]
    weights, rest = rest[:n_w], rest[n_w:]
    w_kv, w_q, w_o, w_ffa, w_ffb, w_down = weights
    rows, ghid, kv_own, q_own, o_all = rest[:5]
    sum_bufs, (send, recv, local_sems) = rest[5:9], rest[9:]
    x, y, z, c, t = coords()
    core, pair = device(x, y, z, 1 - c, t), device(x, y, z, c, 1 - t)
    theirs, ours = [pl.ds(pl.multiple_of(k * TOK, TOK), TOK) for k in (1 - c, c)]
    sems, local = Sems(send, recv), Locals(local_sems)
    raw_loads = [local.load(src, dst) for src, dst in zip(raw_in, raw, strict=True)]
    stores = [local.copy(src, dst) for src, dst in zip(results, kept, strict=True)]
    for load in raw_loads:
        load.wait()
    arrange(raw, w_in)
    greet(neighbours() + [pair, device(moved(x, 2), y, z, c, t), chip_shift(4), chip_shift(-4)])

    def store(*which):
        for i in which:
            stores[i].start()

    tasks = Tasks()
    loads = []
    for i, label in enumerate(CHUNKS):
        add = add_plane_gather if i == W_DOWN else add_gather
        along = ALONG_X if i == W_OUT else ALONG
        loads.append(add(tasks, label, along, w_in[i], w_out[i], weights[i], sems, local))
    for i, label in ((W_KV, "ldkv"), (W_OUT, "ldo"), (W_FFA, "ldffa"), (W_FFB, "ldffb"), (W_DOWN, "lddown")):
        tasks.add(label, loads[i].wait)

    row_copy, cot_copy = local.copy(hid, rows.at[c]), local.copy(cot, cots.at[c])
    row_swap, cot_swap = sems.copy(hid, rows.at[c], core), sems.copy(cot, cots.at[c], core)

    def swaps():
        row_copy.start()
        cot_copy.start()
        sems.start(row_swap, cot_swap)

    tasks.add("swaps", swaps)

    def norm():
        row_copy.wait()
        row_swap.wait_recv()
        pick = pick_lanes().astype(HALF)
        gains[...] = product(pick, columns(w_kv, 2 * HW, LANES), ((1,), (1,)))
        for half in range(2):

            def norm_one(r, half=half):
                values = rows[half, r, :].astype(SINGLE)
                a1[half, r, :] = (values * rms_inverse(values) * gains[0:1, :]).astype(HALF)

            row_loop(0, TOK, norm_one)
        store(0)

    tasks.add("norm", norm)

    def project(w, n):
        w_cols = columns(w, n, 2 * HD)
        return [product(a1[half], w_cols, ((1,), (0,))).astype(HALF) for half in range(2)]

    kv_swap = exchange(sems, local, lambda v: kv_own.at[v], lambda v: kv.at[own_rows(WINDOW, v)])
    q_swap = exchange(sems, local, lambda v: q_own.at[v], lambda v: q.at[own_rows(0, v)])
    o_swap = exchange(sems, local, lambda v: o_all.at[own_rows(0, v)], lambda v: o.at[:, head_lanes(v, HD)])
    halo = sems.copy(kv.at[2 * WINDOW : 3 * WINDOW], kv.at[0:WINDOW], chip_shift(4))
    for h in range(4):

        def project_kv(h=h):
            for half, out in enumerate(project(w_kv, h * 2 * HD)):
                kv_own[h, half * TOK : (half + 1) * TOK, :] = out

        tasks.add(f"proj{h}", project_kv)
    tasks.add("kva", kv_swap.start)

    def project_q():
        loads[W_Q].wait()
        for n in range(2):
            for half, out in enumerate(project(w_q, n * 2 * HD)):
                for k in range(2):
                    q_own[2 * n + k, half * TOK : (half + 1) * TOK, :] = out[
                        :, k * HD : (k + 1) * HD
                    ]
        q_swap.start()

    tasks.add("projq", project_q)

    def send_halo():
        kv_swap.wait()
        sems.start(halo)

    tasks.add("halo", send_halo)

    def attend_one(i, carry):
        mine, keys = block_rows(i)
        mixed, total = attend_block(
            q[mine, :], kv[keys, :HD], kv[keys, HD:], first_key(i)
        )
        o_all[mine, :] = mixed
        lse[mine, :] = jnp.broadcast_to(total, (QB, HD))
        return carry

    def attend_late():
        q_swap.wait()
        lax.fori_loop(4, 8, attend_one, 0)

    def attend_early():
        halo.wait_recv()
        lax.fori_loop(0, 4, attend_one, 0)
        o_swap.start()
        store(2, 3, 5)

    tasks.add("attA", attend_late)
    tasks.add("attB", attend_early)

    attended = FourSum(sum_bufs, sems)
    for i in range(PARTS):

        def put(i=i):
            if i == 0:
                o_swap.wait()
                store(4)
            w_rows = w_o[i].reshape(PART, HW)
            attended.put(i, *[product(o[r, :], w_rows, ((1,), (1,))) for r in (theirs, ours)])

        tasks.add(f"att.put{i}", put)
    attended.add_relays(tasks, "att")
    spreads = []
    for half in range(2):
        part = a2.at[c, half * 128 : (half + 1) * 128]
        spreads.append(sems.copy(part, part, core))

        def norm_two_half(half=half):
            if half == 0:
                attended.wait()

            def norm_two(r):
                values = rows[c, r, :].astype(SINGLE) + attended.total(r)
                mid[r, :] = values
                a2[c, r, :] = (values * rms_inverse(values) * gains[1:2, :]).astype(HALF)

            row_loop(half * 128, 128, norm_two)
            sems.start(spreads[half])

        tasks.add(f"norm2{half}", norm_two_half)

    def hidden_grads(first, count):
        def task():
            w_cols = columns(w_down, first, count)
            for half in range(2):
                r = slice(half * TOK, (half + 1) * TOK)
                ghid[r, first : first + count] = product(cots[half], w_cols, ((1,), (0,)))

        return task

    def hidden_grads_a():
        cot_copy.wait()
        cot_swap.wait_recv()
        store(1)
        for n in range(0, FFA // 2, 2 * LANES):
            hidden_grads(n, 2 * LANES)()

    def hidden_grads_b():
        for n in range(FFA // 2, FF, 2 * LANES):
            hidden_grads(n, min(2 * LANES, FF - n))()

    tasks.add("ghida", hidden_grads_a)
    tasks.add("ghidb", hidden_grads_b)

    def feed_forward(w_ff, first, i, carry):
        n = pl.multiple_of(i * 2 * LANES, 2 * LANES)
        w_cols = columns(w_ff, n, 2 * LANES)
        gate_lanes = pl.ds(pl.multiple_of(first + n, 2 * LANES), LANES)
        up_lanes = pl.ds(pl.multiple_of(first + n + LANES, LANES), LANES)
        lanes = pl.ds(pl.multiple_of(first // 2 + i * LANES, LANES), LANES)
        for half in range(2):
            r = slice(half * TOK, (half + 1) * TOK)
            both = product(a2[half], w_cols, ((1,), (0,)))
            gate, up_part = both[:, :LANES], both[:, LANES:]
            sig = 1.0 / (1.0 + jnp.exp(-gate))
            hid_ff[r, lanes] = (gate * sig * up_part).astype(HALF)
            grad = ghid[r, lanes]
            grad_ff[r, gate_lanes] = (
                grad * up_part * sig * (1.0 + gate * (1.0 - sig))
            ).astype(HALF)
            grad_ff[r, up_lanes] = (grad * gate * sig).astype(HALF)
        return carry

    pairs_a, pairs = FFA // (2 * LANES), FF // LANES

    def feed_forward_a():
        for copy in spreads:
            copy.wait_recv()
        store(6, 7)
        lax.fori_loop(0, pairs_a, lambda i, carry: feed_forward(w_ffa, 0, i, carry), 0)

    def feed_forward_b():
        lax.fori_loop(
            0, pairs - pairs_a, lambda i, carry: feed_forward(w_ffb, FFA, i, carry), 0
        )
        store(8, 9)

    tasks.add("gua", feed_forward_a)
    tasks.add("gub", feed_forward_b)
    tasks.run(FORWARD_ORDER)
    for copy in stores:
        copy.wait()
    sems.finish()


def forward(raw, hid, cot):
    n = len(CHUNKS)
    copies = GATHER_COPIES * n + 2 + 3 * 3 + 1 + SUM_COPIES + 2
    kept = [
        ((2, TOK, D), HALF),
        ((2, TOK, D), HALF),
        ((2 * WINDOW, HD), HALF),
        ((3 * WINDOW, 2 * HD), HALF),
        ((2 * TOK, HW), HALF),
        ((2 * WINDOW, HD), SINGLE),
        ((TOK, D), SINGLE),
        ((2, TOK, D), HALF),
        ((2 * TOK, FF), HALF),
        ((2 * TOK, 2 * FF), HALF),
    ]
    return pl.pallas_call(
        forward_kernel,
        out_shape=[SHAPE(grid_of(w), HALF) for w in W_WIDTHS]
        + [SHAPE(*k) for k in kept]
        + [SHAPE((8, D), SINGLE)],
        in_specs=[ANYWHERE] * (len(raw) + 2),
        out_specs=[ANYWHERE] * (n + len(kept)) + [IN_VMEM],
        scratch_shapes=[pltpu.VMEM(*k) for k in kept]
        + [pltpu.VMEM(w.shape, SINGLE) for w in raw]
        + [pltpu.VMEM((2, 32, w), HALF) for w in W_WIDTHS]
        + [pltpu.VMEM(grid_of(w), HALF) for w in W_WIDTHS]
        + [
            pltpu.VMEM((2, TOK, D), HALF),
            pltpu.VMEM((2 * TOK, FF), SINGLE),
            pltpu.VMEM((4, 2 * TOK, 2 * HD), HALF),
            pltpu.VMEM((4, 2 * TOK, HD), HALF),
            pltpu.VMEM((2 * WINDOW, HD), HALF),
        ]
        + SUM_SCRATCH
        + [
            pltpu.SemaphoreType.DMA((copies,)),
            pltpu.SemaphoreType.DMA((copies,)),
            pltpu.SemaphoreType.DMA((2 * n + 2 + 3 + len(raw) + len(kept),)),
        ],
        compiler_params=params(0),
    )(*raw, hid, cot)


GRADS = ("down", "ffa", "ffb", "oq", "kv", "gain")
G_DOWN, G_FFA, G_FFB, G_OQ, G_KV, G_GAIN = range(6)
G_WIDTHS = (FF, FFA, FFB, 2 * HW, 2 * HW, LANES)
BACKWARD_ORDER = (
    54, 0, 55, 56, 57, 58, 63, 9, 59, 60, 1, 2, 64, 61, 62, 10, 11, 65, 66, 3, 4, 67, 18, 12,
    13, 5, 68, 69, 19, 20, 73, 14, 74, 75, 76, 6, 77, 78, 79, 80, 71, 7, 70, 21, 22, 15, 8, 27,
    81, 82, 83, 23, 84, 85, 86, 72, 16, 28, 29, 36, 89, 17, 87, 88, 24, 30, 31, 37, 38, 90, 91,
    32, 25, 45, 26, 39, 40, 33, 46, 47, 41, 34, 48, 49, 42, 35, 50, 51, 43, 52, 44, 53,
)


def backward_kernel(*refs):
    n_w, n_g = len(CHUNKS), len(GRADS)
    w_kv, w_q, w_out, w_ffa, w_ffb, w_down = refs[:n_w]
    rest = refs[n_w:]
    a1_in, cots, q_in, kv_in, o_in, lse_in, mid_in, a2_in, hid_in, grad_ff_in, rows_in, gains = rest[:12]
    rest = rest[12:]
    s_query, s_key, s_value, s_out, s_gate, s_up, s_down, s_gain, in_grad, hidden_out = rest[:10]
    rest = rest[10:]
    g_refs, slots, rest = rest[:n_g], rest[n_g : 3 * n_g], rest[3 * n_g :]
    scratch, rest = rest[: 4 * n_g], rest[4 * n_g :]
    shared, rest = rest[:5], rest[5:]
    to_core, own_sum, rest = rest[0], rest[1], rest[2:]
    gn2_bufs, gn1_bufs, out_bufs, rest = rest[:2], rest[2:4], rest[4:6], rest[6:]
    (
        staging,
        cot_v,
        gatt,
        rows_v,
        hid_ff,
        grad_ff,
        mid,
        q,
        kv,
        lse,
        o,
        tiles,
        go,
        go_all,
        acc,
        far,
        got,
        gq_all,
        gkv_all,
        gq,
        gkv,
        gain_acc,
        send,
        recv,
        local_sems,
    ) = rest
    x, y, z, c, t = coords()
    core, pair = device(x, y, z, 1 - c, t), device(x, y, z, c, 1 - t)
    sems, local = Sems(send, recv), Locals(local_sems)
    theirs, ours = [pl.ds(pl.multiple_of(k * TOK, TOK), TOK) for k in (1 - c, c)]
    tasks = Tasks()

    def tile_loads(*sources):
        loads = []
        for i in range(8):
            copies, n = [], 0
            for source, width in sources:
                copies.append(
                    local.copy(
                        source.at[i // 2, i % 2, :, :, :, 0:width],
                        tiles.at[i % 2, :, :, :, n : n + width],
                    )
                )
                n += width
            loads.append(copies)
        return loads

    def begin(*loads):
        for copies in loads:
            for copy in copies:
                copy.start()

    def tile(k, start, width):
        return tiles[k, :, :, :, start : start + width].reshape(256, width)

    def add_sum(label, bufs, loads, multiply, last=None, then=None):
        total = FourSum([to_core, *bufs, own_sum], sems)
        for i in range(PARTS):

            def put(i=i):
                if i == 0 and last is not None:
                    sems.sent(last.core)
                parts = []
                for k in range(2):
                    for copy in loads[2 * i + k]:
                        copy.wait()
                    parts.append([multiply(r, k) for r in (theirs, ours)])
                    if 2 * i + k + 2 < 8:
                        begin(loads[2 * i + k + 2])
                total.put(
                    i, *[jnp.concatenate([parts[0][j], parts[1][j]], axis=1) for j in range(2)]
                )
                if i == PARTS - 1 and then is not None:
                    then()

            tasks.add(f"{label}.put{i}", put)
        total.add_relays(tasks, label)
        return total

    load_cot, load_hid = local.load(cots, cot_v), local.load(hid_in, hid_ff)
    load_grad = local.load(grad_ff_in, grad_ff)
    ff_loads = tile_loads((w_ffa, FFA), (w_ffb, FFB))
    begin(ff_loads[0], ff_loads[1])
    load_a2 = local.load(a2_in, rows_v)
    later = [
        local.load(src, dst)
        for src, dst in (
            (mid_in, mid),
            (q_in, q),
            (kv_in, kv),
            (lse_in, lse),
            (o_in, o),
        )
    ]
    load_a1 = local.copy(a1_in, rows_v)
    out_loads = [
        local.copy(
            w_out.at[i // 2, i % 2], tiles.at[i // 4, :, :, :, (i % 4) * HW : (i % 4 + 1) * HW]
        )
        for i in range(8)
    ]
    down_loads = tile_loads((w_down, FF))
    qkv_loads = tile_loads((w_q, HW), (w_kv, 2 * HW))
    greet(neighbours() + [pair, device(moved(x, 2), y, z, c, t), chip_shift(4), chip_shift(-4)])

    def place_plain(target, width, read):
        for j in range(2):
            for n in range(0, width, LANES):
                start = j * width + n
                lanes = min(LANES, target.shape[1] - start)
                target[:, start : start + lanes] = read(j, n)[:, :lanes]

    def place_ff(first, width, read):
        for j in range(2):
            for n in range(0, width, 2 * LANES):
                start = j * FF + (first + n) // 2
                lanes = min(LANES, s_gate.shape[1] - start)
                s_gate[:, start : start + lanes] = read(j, n)[:, :lanes]
                s_up[:, start : start + lanes] = read(j, n + LANES)[:, :lanes]

    def place_oq(read):
        place_plain(s_out, HW, read)
        place_plain(s_query, HW, lambda j, n: read(j, HW + n))

    def place_kv(read):
        for j in range(2):
            for h in range(4):
                lanes = slice((4 * j + h) * HD, (4 * j + h + 1) * HD)
                s_key[:, lanes] = read(j, 2 * h * HD)
                s_value[:, lanes] = read(j, (2 * h + 1) * HD)

    def place_gain(read):
        s_gain[...] = (read(0, 0) + read(1, 0)).T[:8]

    place = (
        lambda read: place_plain(s_down, FF, read),
        lambda read: place_ff(0, FFA, read),
        lambda read: place_ff(FFA, FFB, read),
        place_oq,
        place_kv,
        place_gain,
    )
    scatter = Scatter(tasks, shared, sems, local)
    for i, label in enumerate(GRADS):
        scatter.add(
            label,
            ALONG,
            g_refs[i],
            place[i],
            slots[2 * i : 2 * i + 2],
            scratch[4 * i : 4 * i + 4],
        )
    waited = set()

    def once(load):
        if id(load) not in waited:
            waited.add(id(load))
            load.wait()

    def grad_down():
        once(load_cot)
        once(load_hid)
        make_grads(cot_v, lambda: hid_ff[...], staging, g_refs[G_DOWN], local)

    tasks.add("gdown", grad_down)

    def multiply_ff(r, k):
        once(load_grad)
        return product(grad_ff[r, :], tile(k, 0, 2 * FF), ((1,), (1,)))

    gn2 = add_sum("gn2", gn2_bufs, ff_loads, multiply_ff, None, lambda: begin(out_loads))

    def grad_ffa():
        once(load_a2)
        make_grads(rows_v, lambda: grad_ff[:, :FFA], staging, g_refs[G_FFA], local)

    def grad_ffb():
        once(load_a2)
        make_grads(rows_v, lambda: grad_ff[:, FFA:], staging, g_refs[G_FFB], local)

    tasks.add("gffa", grad_ffa)
    tasks.add("gffb", grad_ffb)
    spreads = []
    for half in range(2):
        part = gatt.at[c, half * 128 : (half + 1) * 128]
        spreads.append(sems.copy(part, part, core))

        def mid_back_half(half=half):
            if half == 0:
                gn2.wait()
                for load in later:
                    load.wait()
                gain_acc[...] = jnp.zeros_like(gain_acc)

            def mid_back(r):
                part, term = norm_back(gn2.total(r), mid[r, :], gains[1:2, :])
                grad = cot_v[c, r, :].astype(SINGLE) + part
                in_grad[r, :] = grad
                gatt[c, r, :] = grad.astype(HALF)
                gain_acc[1:2, :] += term

            row_loop(half * 128, 128, mid_back)
            sems.start(spreads[half])

        tasks.add(f"mid{half}", mid_back_half)

    def attended_back():
        for copy in out_loads:
            copy.wait()
        for copy in spreads:
            copy.wait_recv()
        for half in range(2):
            total = jnp.zeros((TOK, HW), SINGLE)
            for i in range(8):
                total += product(
                    gatt[half, :, i * 256 : (i + 1) * 256],
                    tile(i // 4, (i % 4) * HW, HW),
                    ((1,), (0,)),
                )
            go[half * TOK : (half + 1) * TOK, :] = total.astype(HALF)
        go_swap.start()
        begin(down_loads[0], down_loads[1])

    tasks.add("go", attended_back)

    go_swap = exchange(
        sems, local, lambda v: go.at[:, head_lanes(v, HD)], lambda v: go_all.at[own_rows(0, v)]
    )
    gq_swap = exchange(
        sems, local, lambda v: gq_all.at[own_rows(0, v)], lambda v: gq.at[:, head_lanes(v, HD)]
    )
    gkv_swap = exchange(
        sems,
        local,
        lambda v: gkv_all.at[own_rows(0, v)],
        lambda v: gkv.at[:, head_lanes(v, 2 * HD)],
    )
    back = sems.copy(far, got, chip_shift(-4))

    def attend_one(i, carry):
        mine, keys = block_rows(i)
        grad_q, grad_k, grad_v = attend_block_back(
            q[mine, :], kv[keys, :HD], kv[keys, HD:], go_all[mine, :], lse[mine, 0:1], first_key(i)
        )
        gq_all[mine, :] = grad_q.astype(HALF)
        acc[keys, :HD] += grad_k
        acc[keys, HD:] += grad_v
        return carry

    def attend_early():
        load_a1.start()
        acc[...] = jnp.zeros_like(acc)
        go_swap.wait()
        lax.fori_loop(0, 4, attend_one, 0)
        far[...] = acc[0:WINDOW, :].astype(HALF)
        sems.start(back)

    def attend_late():
        lax.fori_loop(4, 8, attend_one, 0)
        gq_swap.start()

    def add_back():
        back.wait_recv()

        def keep(r):
            gkv_all[r, :] = acc[pl.ds(pl.multiple_of(WINDOW + r.start, 64), 64), :].astype(HALF)

        def add(r):
            total = acc[pl.ds(pl.multiple_of(2 * WINDOW + r.start, 64), 64), :]
            total = total + got[r, :].astype(SINGLE)
            gkv_all[pl.ds(pl.multiple_of(WINDOW + r.start, 64), 64), :] = total.astype(HALF)

        row_loop(0, WINDOW, keep, 64)
        row_loop(0, WINDOW, add, 64)
        gkv_swap.start()

    tasks.add("attbA", attend_early)
    tasks.add("attbB", attend_late)
    tasks.add("gadd", add_back)

    def once_arrived(swap):
        if id(swap) not in waited:
            waited.add(id(swap))
            swap.wait()

    def grad_oq():
        once(load_a1)
        once_arrived(gq_swap)
        make_grads(gatt, lambda: o[...], staging, g_refs[G_OQ], local, 0, HW)
        make_grads(rows_v, lambda: gq[...], staging, g_refs[G_OQ], local, HW, HW)

    def grad_kv():
        once(load_a1)
        once_arrived(gkv_swap)
        make_grads(rows_v, lambda: gkv[...], staging, g_refs[G_KV], local)

    tasks.add("goq", grad_oq)
    tasks.add("gkv", grad_kv)
    out_sum = add_sum(
        "out",
        out_bufs,
        down_loads,
        lambda r, k: product(hid_ff[r, :], tile(k, 0, FF), ((1,), (1,))),
        gn2,
        lambda: begin(qkv_loads[0], qkv_loads[1]),
    )

    def multiply_qkv(r, k):
        once_arrived(gq_swap)
        once_arrived(gkv_swap)
        from_q = product(gq[r, :], tile(k, 0, HW), ((1,), (1,)))
        return from_q + product(gkv[r, :], tile(k, HW, 2 * HW), ((1,), (1,)))

    gn1 = add_sum(
        "gn1",
        gn1_bufs,
        qkv_loads,
        multiply_qkv,
        out_sum,
    )

    def rows_out():
        out_sum.wait()

        def add(r):
            hidden_out[r, :] = (mid[r, :] + out_sum.total(r)).astype(HALF)

        row_loop(0, TOK, add)

    load_rows = local.copy(rows_in, to_core)

    def rows_back():
        sems.sent(gn1.core)
        load_rows.start()
        gn1.wait()
        load_rows.wait()

        def add(r):
            part, term = norm_back(gn1.total(r), to_core[r, :].astype(SINGLE), gains[0:1, :])
            in_grad[r, :] = in_grad[r, :] + part
            gain_acc[0:1, :] += term

        row_loop(0, TOK, add)

    tasks.add("rowsout", rows_out)
    tasks.add("rowsback", rows_back)

    def grad_gain():
        pick = pick_lanes().astype(HALF)
        writes = []
        for n in range(8):
            lanes = slice(n * LANES, (n + 1) * LANES)
            cols = product(gain_acc[:, n * 256 : (n + 1) * 256].astype(HALF), pick, ((0,), (0,)))
            staging[0, :, :, :, lanes] = cols.astype(HALF).reshape(4, 2, 32, LANES)
            writes.append(
                local.load(staging.at[0, :, :, :, lanes], g_refs[G_GAIN].at[n // 2, n % 2])
            )
        for copy in writes:
            copy.wait()

    tasks.add("ggain", grad_gain)
    tasks.run(BACKWARD_ORDER)
    sems.finish()


def backward(hidden_units, *operands):
    n = len(GRADS)
    copies = SCATTER_COPIES * n + SUM_COPIES * 3 + 2 + 3 * 3 + 1
    loads = 11 + 8 * (2 + 1 + 1 + 2) + SCATTER_LOADS * n + 2 * 6 + 8 + 3
    slots = [slot for w in G_WIDTHS for slot in scatter_slots(w)]
    widest = max(G_WIDTHS)
    results = [(32, 2 * HW)] * 4 + [(32, hidden_units)] * 3 + [(8, 32)]
    rows_half = pltpu.VMEM((TOK, D), HALF)
    return pl.pallas_call(
        backward_kernel,
        out_shape=[SHAPE(s, SINGLE) for s in results]
        + [SHAPE((TOK, D), SINGLE), SHAPE((TOK, D), HALF)]
        + [SHAPE(grid_of(w), HALF) for w in G_WIDTHS]
        + slots,
        in_specs=[ANYWHERE] * (len(operands) - 1) + [IN_VMEM],
        out_specs=[IN_VMEM] * (len(results) + 2) + [ANYWHERE] * (n + len(slots)),
        scratch_shapes=[buf for w in G_WIDTHS for buf in scatter_scratch(w)]
        + scatter_shared(widest)
        + [rows_half, pltpu.VMEM((TOK, D), SINGLE)]
        + [rows_half] * 6
        + [
            pltpu.VMEM((2, 4, 2, 32, widest), HALF),
            pltpu.VMEM((2, TOK, D), HALF),
            pltpu.VMEM((2, TOK, D), HALF),
            pltpu.VMEM((2, TOK, D), HALF),
            pltpu.VMEM((2 * TOK, FF), HALF),
            pltpu.VMEM((2 * TOK, 2 * FF), HALF),
            pltpu.VMEM((TOK, D), SINGLE),
            pltpu.VMEM((2 * WINDOW, HD), HALF),
            pltpu.VMEM((3 * WINDOW, 2 * HD), HALF),
            pltpu.VMEM((2 * WINDOW, HD), SINGLE),
            pltpu.VMEM((2 * TOK, HW), HALF),
            pltpu.VMEM((2, 4, 2, 32, 2 * FF), HALF),
            pltpu.VMEM((2 * TOK, HW), HALF),
            pltpu.VMEM((2 * WINDOW, HD), HALF),
            pltpu.VMEM((3 * WINDOW, 2 * HD), SINGLE),
            pltpu.VMEM((WINDOW, 2 * HD), HALF),
            pltpu.VMEM((WINDOW, 2 * HD), HALF),
            pltpu.VMEM((2 * WINDOW, HD), HALF),
            pltpu.VMEM((2 * WINDOW, 2 * HD), HALF),
            pltpu.VMEM((2 * TOK, HW), HALF),
            pltpu.VMEM((2 * TOK, 2 * HW), HALF),
            pltpu.VMEM((8, D), SINGLE),
            pltpu.SemaphoreType.DMA((copies,)),
            pltpu.SemaphoreType.DMA((copies,)),
            pltpu.SemaphoreType.DMA((loads,)),
        ],
        compiler_params=params(1),
    )(*operands)


def hand_over_kernel(count, *refs):
    sems = refs[2 * count]
    copies = [
        pltpu.make_async_copy(refs[i], refs[count + i], sems.at[i]) for i in range(count)
    ]
    for copy in copies:
        copy.start()
    for copy in copies:
        copy.wait()


def hand_over(*arrays):
    n = len(arrays)
    return pl.pallas_call(
        functools.partial(hand_over_kernel, n),
        out_shape=[SHAPE(a.shape, a.dtype) for a in arrays],
        in_specs=[IN_VMEM] * n,
        out_specs=[ANYWHERE] * n,
        scratch_shapes=[pltpu.SemaphoreType.DMA((n,))],
        compiler_params=pltpu.CompilerParams(vmem_limit_bytes=VMEM_LIMIT),
    )(*arrays)


def per_device(
    hidden_in, attn_gain, w_query, w_key, w_value, w_out, ffn_gain, w_gate, w_up, w_down, out_grad
):
    weights = (w_query, w_key, w_value, w_out.T, w_gate, w_up, w_down.T)
    gains = (attn_gain.reshape(1, -1), ffn_gain.reshape(1, -1))
    *kept, gain_rows = forward((*gains, *weights), hidden_in, out_grad)
    results = backward(w_gate.shape[1], *kept, hidden_in, gain_rows)[:10]
    s_query, s_key, s_value, s_out, s_gate, s_up, s_down, s_gain, in_grad, hidden_out = hand_over(
        *results
    )
    return (
        hidden_out,
        in_grad,
        s_gain[0],
        s_query,
        s_key,
        s_value,
        s_out.T,
        s_gain[1],
        s_gate,
        s_up,
        s_down.T,
    )


def solution(mesh):
    placed = (
        P("seq", None),
        P("seq"),
        P("seq", "tp"),
        P("seq", "tp"),
        P("seq", "tp"),
        P("tp", "seq"),
        P("seq"),
        P("seq", "tp"),
        P("seq", "tp"),
        P("tp", "seq"),
        P("seq", None),
    )
    return jax.shard_map(
        per_device,
        mesh=mesh,
        in_specs=placed,
        out_specs=(
            P("seq", None),
            P("seq", None),
            P("seq"),
            P("seq", "tp"),
            P("seq", "tp"),
            P("seq", "tp"),
            P("tp", "seq"),
            P("seq"),
            P("seq", "tp"),
            P("seq", "tp"),
            P("tp", "seq"),
        ),
        check_vma=False,
    )
```

```python
import functools
import math

import jax
import jax.numpy as jnp
from jax import lax
from jax.experimental import pallas as pl
from jax.experimental.pallas import tpu as pltpu
from jax.sharding import PartitionSpec as P

HD = 128
WINDOW = 1024
EPSILON = 1e-06
MASKED = -1e30
MESH = pl.DeviceIdType.MESH
HALF = jnp.bfloat16
SINGLE = jnp.float32
VMEM_LIMIT = 63 * 2**20

D = 2048
TOK = 256
HW = 512
FF = 1408
FFA, FFB = 1536, 1280
QB = 256
KB = QB + WINDOW
SCALE = 1.0 / math.sqrt(HD)
ROWS = 16
LANES = 128
PART = 512
PARTS = D // PART

ANYWHERE = pl.BlockSpec(memory_space=pl.ANY)
IN_VMEM = pl.BlockSpec(memory_space=pltpu.VMEM)
SHAPE = jax.ShapeDtypeStruct


def coords():
    s = lax.axis_index("seq")
    t = lax.axis_index("tp")
    return lax.rem(lax.div(s, 2), 4), lax.div(s, 16), lax.rem(lax.div(s, 8), 2), lax.rem(s, 2), t


def device(x, y, z, c, t):
    return (((y * 2 + z) * 4 + x) * 2 + c, t)


def moved(v, steps):
    return lax.rem(v + steps + 4, 4)


def chip_shift(steps):
    s = lax.axis_index("seq")
    return (lax.rem(s + 2 * steps + 64, 64), lax.axis_index("tp"))


def neighbours():
    x, y, z, c, t = coords()
    return [
        device(moved(x, 1), y, z, c, t),
        device(moved(x, -1), y, z, c, t),
        device(x, moved(y, 1), z, c, t),
        device(x, moved(y, -1), z, c, t),
        device(x, y, 1 - z, c, t),
        device(x, y, z, 1 - c, t),
    ]


def say_hello(partners):
    barrier = pltpu.get_barrier_semaphore()
    for partner in partners:
        pl.semaphore_signal(barrier, inc=1, device_id=partner, device_id_type=MESH)


def hear_hello(partners):
    pl.semaphore_wait(pltpu.get_barrier_semaphore(), len(partners))


class Sems:
    def __init__(self, send, recv):
        self.send, self.recv, self.used, self.started = send, recv, 0, []

    def copy(self, src, dst, dev):
        i = self.used
        self.used += 1
        return pltpu.make_async_remote_copy(
            src, dst, self.send.at[i], self.recv.at[i], device_id=dev, device_id_type=MESH
        )

    def start(self, *copies):
        for copy in copies:
            copy.start()
            self.started.append(copy)

    def sent(self, copies):
        for copy in copies:
            copy.wait_send()
            self.started = [other for other in self.started if other is not copy]

    def finish(self):
        self.sent(list(self.started))


class Locals:
    def __init__(self, sems):
        self.sems, self.used = sems, 0

    def sem(self):
        self.used += 1
        return self.sems.at[self.used - 1]

    def copy(self, src, dst):
        return pltpu.make_async_copy(src, dst, self.sem())

    def load(self, src, dst):
        copy = self.copy(src, dst)
        copy.start()
        return copy


class Tasks:
    def __init__(self):
        self.tasks = {}

    def add(self, name, task):
        self.tasks[name] = task

    def run(self, order):
        tasks = list(self.tasks.values())
        assert sorted(order) == list(range(len(tasks)))
        for i in order:
            tasks[i]()


def grid_piece(along_x):
    x, y, z, c, t = coords()
    if along_x:
        return x, y, lambda v: device(v, y, z, c, t), lambda v: device(x, v, z, c, t)
    return y, x, lambda v: device(x, v, z, c, t), lambda v: device(v, y, z, c, t)


def blocks(ref, along_x, h, a, zs, b):
    return ref.at[b, zs, a, h] if along_x else ref.at[a, zs, b, h]


ALL = slice(None)


GATHER_COPIES = 1 + 4 * 6 + 8


def gather_streams(along, out, sems, planes, rows):
    streams = []
    for h in range(2):
        a, b, to_a, to_b = grid_piece(along[h])
        for s, d in ((0, 1), (1, -1)):

            def copy(aa, bb, dev, h=h, s=s):
                src = blocks(out, along[h], h, aa, planes[s], bb)
                src = src.at[rows[s]] if aa is not ALL else src.at[:, rows[s]]
                return sems.copy(src, src, dev)

            streams.append(
                dict(
                    a1f=copy(a, b, to_a(moved(a, d))),
                    a1r=copy(a, b, to_a(moved(a, -d))),
                    a2=copy(moved(a, -d), b, to_a(moved(a, d))),
                    b1f=copy(ALL, b, to_b(moved(b, d))),
                    b1r=copy(ALL, b, to_b(moved(b, -d))),
                    b2=copy(ALL, moved(b, -d), to_b(moved(b, d))),
                )
            )
    return streams


def add_gather(tasks, label, along, w_in, out, load, sems, local):
    x, y, z, c, t = coords()
    mine = local.copy(w_in.at[c], out.at[y, z, x, c])
    swap = sems.copy(w_in.at[1 - c], out.at[y, z, x, c], device(x, y, z, 1 - c, t))
    over_z = []
    for h in range(2):
        src = out.at[y, z, x, h]
        over_z.append(sems.copy(src, src, device(x, y, 1 - z, c, t)))
    streams = gather_streams(along, out, sems, (z, 1 - z), (ALL, ALL))
    add = lambda name, task: tasks.add(f"{label}.{name}", task)

    def init():
        mine.start()
        sems.start(swap)

    def own():
        mine.wait()
        swap.wait_recv()
        sems.start(*over_z)
        for p in streams[0::2]:
            sems.start(p["a1f"], p["a1r"])

    def other():
        for copy in over_z:
            copy.wait_recv()
        for p in streams[1::2]:
            sems.start(p["a1f"], p["a1r"])

    def a2(ps):
        for p in ps:
            p["a1f"].wait_recv()
            sems.start(p["a2"])

    def b1(ps):
        for p in ps:
            p["a1r"].wait_recv()
            p["a2"].wait_recv()
            sems.start(p["b1f"], p["b1r"])

    def b2(ps):
        for p in ps:
            p["b1f"].wait_recv()
            sems.start(p["b2"])

    def end():
        for p in streams:
            p["b1r"].wait_recv()
            p["b2"].wait_recv()
        load.start()

    add("init", init)
    add("own", own)
    add("other", other)
    for s in range(2):
        add(f"a2{s}", lambda s=s: a2(streams[s::2]))
        add(f"b1{s}", lambda s=s: b1(streams[s::2]))
        add(f"b2{s}", lambda s=s: b2(streams[s::2]))
    add("end", end)


def add_plane_gather(tasks, label, along, w_in, out, load, sems, local):
    x, y, z, c, t = coords()
    mine = local.copy(w_in.at[c], out.at[y, z, x, c])
    swap = sems.copy(w_in.at[1 - c], out.at[y, z, x, c], device(x, y, z, 1 - c, t))
    streams = gather_streams(along, out, sems, (z, z), (slice(0, 16), slice(16, 32)))
    over_z = {}
    for h in range(2):
        a, b, to_a, to_b = grid_piece(along[h])
        for k in range(4):
            src = blocks(out, along[h], h, ALL, z, moved(b, k))
            over_z[h, k] = sems.copy(src, src, device(x, y, 1 - z, c, t))
    add = lambda name, task: tasks.add(f"{label}.{name}", task)

    def cross(*steps):
        for k in steps:
            sems.start(over_z[0, k], over_z[1, k])

    def init():
        mine.start()
        sems.start(swap)

    def own():
        mine.wait()
        swap.wait_recv()
        for p in streams:
            sems.start(p["a1f"], p["a1r"])

    def a2():
        for p in streams:
            p["a1f"].wait_recv()
            sems.start(p["a2"])

    def b1():
        for p in streams:
            p["a1r"].wait_recv()
            p["a2"].wait_recv()
            sems.start(p["b1f"], p["b1r"])
        cross(0)

    def b2():
        for p in streams:
            p["b1f"].wait_recv()
            sems.start(p["b2"])

    def zs():
        for p in streams:
            p["b1r"].wait_recv()
        cross(1, 3)

    def ze():
        for p in streams:
            p["b2"].wait_recv()
        cross(2)

    def end():
        for copy in over_z.values():
            copy.wait_recv()
        load.start()

    for task in (init, own, a2, b1, b2, zs, ze, end):
        add(task.__name__, task)


SCATTER_COPIES = 4 * 6 + 3
SCATTER_LOADS = 16


def scatter_slots(w):
    return [SHAPE((2, 2, 4, 32, w), HALF), SHAPE((2, 2, 2, 4, 32, w), HALF)]


def scatter_scratch(w):
    return [
        pltpu.VMEM((2, 2, 32, w), HALF),
        pltpu.VMEM((2, 2, 2, 32, w), HALF),
        pltpu.VMEM((2, 32, w), HALF),
        pltpu.VMEM((2, 32, w), SINGLE),
    ]


def scatter_shared(w):
    return [
        pltpu.VMEM((2, 2, 2, 4, 32, w), HALF),
        pltpu.VMEM((2, 2, 2, 4, 32, w), HALF),
        pltpu.VMEM((2, 2, 4, 32, w), HALF),
        pltpu.VMEM((2, 2, 2, 4, 32, w), HALF),
        pltpu.VMEM((2, 32, w), SINGLE),
    ]


def plus(ref, *others):
    total = ref[...].astype(SINGLE)
    for other in others:
        total = total + other[...].astype(SINGLE)
    ref[...] = total.astype(HALF)


class Scatter:
    def __init__(self, tasks, shared, sems, local):
        self.tasks, self.sems, self.local = tasks, sems, local
        self.sending, self.owned, self.temp_b, self.temp_a, self.final = shared
        self.count = 0
        self.busy = {}

    def take(self, key, copies):
        self.sems.sent(self.busy.get(key, []))
        self.busy[key] = copies

    def add(self, label, along, g, place, slots, scratch):
        sems, local = self.sems, self.local
        x, y, z, c, t = coords()
        slot = self.count % 2
        self.count += 1
        r2, r1 = slots
        q2, q1, rz, kept = scratch
        wide = slice(0, g.shape[-1])
        tt = self.sending.at[slot, :, :, :, :, wide]
        ss = self.owned.at[slot, :, :, :, :, wide]
        final = self.final.at[:, :, wide]
        streams = []
        for h in range(2):
            a, b, to_a, to_b = grid_piece(along[h])
            for s, zs, d in ((0, z, 1), (1, 1 - z, -1)):
                at_g = lambda bb, h=h, zs=zs: blocks(g, along[h], h, ALL, zs, bb)
                tmp_b, tmp_a = self.temp_b.at[h, s, :, :, wide], self.temp_a.at[h, s, :, :, :, wide]
                forward, back = to_b(moved(b, d)), to_b(moved(b, -d))
                own = ss.at[h, s]
                streams.append(
                    dict(
                        h=h,
                        s=s,
                        a=a,
                        d=d,
                        tt=tt.at[h, s],
                        ss=own,
                        tmp_b=tmp_b,
                        tmp_a=tmp_a,
                        load_t=local.copy(at_g(moved(b, d)), tt.at[h, s]),
                        load_s=local.copy(at_g(b), own),
                        load_2=local.copy(r2.at[h, s], tmp_b),
                        load_1=local.copy(r1.at[h, s], tmp_a),
                        x2=sems.copy(at_g(moved(b, 2)), r2.at[h, s], forward),
                        x1r=sems.copy(at_g(moved(b, -d)), r1.at[h, s, 1], back),
                        x1f=sems.copy(tt.at[h, s], r1.at[h, s, 0], forward),
                        y2=sems.copy(own.at[moved(a, 2)], q2.at[h, s], to_a(moved(a, d))),
                        y1r=sems.copy(own.at[moved(a, -d)], q1.at[h, s, 1], to_a(moved(a, -d))),
                        y1f=sems.copy(own.at[moved(a, d)], q1.at[h, s, 0], to_a(moved(a, d))),
                    )
                )
        over_z = [
            sems.copy(ss.at[h, 1, grid_piece(along[h])[0]], rz.at[h], device(x, y, 1 - z, c, t))
            for h in range(2)
        ]
        swap = sems.copy(final.at[1 - c], kept.at[1], device(x, y, z, 1 - c, t))

        def start():
            for p in streams:
                sems.start(p["x2"], p["x1r"])

        def x1a():
            self.take(("sending", slot), [p["x1f"] for p in streams])
            for p in streams:
                p["load_t"].start()
            for p in streams:
                p["x2"].wait_recv()
                p["load_2"].start()

        def x1b():
            for p in streams:
                p["load_t"].wait()
                p["load_2"].wait()

                def body(i, carry, p=p):
                    plus(p["tt"].at[i], p["tmp_b"].at[i])
                    return carry

                lax.fori_loop(0, 4, body, 0)
                sems.start(p["x1f"])

        def x0a():
            used = [p[name] for p in streams for name in ("y2", "y1r", "y1f")]
            self.take(("owned", slot), used + over_z)
            for p in streams:
                p["load_s"].start()
            for p in streams:
                p["x1r"].wait_recv()
                p["x1f"].wait_recv()
                p["load_1"].start()

        def x0b():
            for p in streams:
                p["load_s"].wait()
                p["load_1"].wait()

                def body(i, carry, p=p):
                    plus(p["ss"].at[i], p["tmp_a"].at[0, i], p["tmp_a"].at[1, i])
                    return carry

                lax.fori_loop(0, 4, body, 0)
                sems.start(p["y2"], p["y1r"])

        def y1():
            for p in streams:
                p["y2"].wait_recv()
                plus(p["ss"].at[moved(p["a"], p["d"])], q2.at[p["h"], p["s"]])
                sems.start(p["y1f"])

        def y0():
            for p in streams:
                h, s = p["h"], p["s"]
                p["y1f"].wait_recv()
                p["y1r"].wait_recv()
                plus(p["ss"].at[p["a"]], q1.at[h, s, 0], q1.at[h, s, 1])
                if s == 1:
                    sems.start(over_z[h])

        def last():
            self.take("final", [swap])
            for p in streams:
                h = p["h"]
                if p["s"] == 0:
                    over_z[h].wait_recv()
                    own = p["ss"].at[p["a"]]
                    final[h] = own[...].astype(SINGLE) + rz[h].astype(SINGLE)
            kept[0] = final[c]
            sems.start(swap)

        def done():
            swap.wait_recv()

            def read(j, start):
                lanes = slice(start, start + LANES)
                return jnp.where(c == j, kept[0, :, lanes], kept[1, :, lanes])

            place(read)

        for task in (start, x1a, x1b, x0a, x0b, y1, y0, last, done):
            self.tasks.add(f"{label}.{task.__name__}", task)


def make_grads(lhs, rhs, staging, g, local, first=0, width=None):
    sems = [local.sem() for _ in range(2)]
    width = width or g.shape[-1]
    wide = slice(0, width)

    def write(i, slot):
        return pltpu.make_async_copy(
            staging.at[slot, :, :, :, wide],
            g.at[i, slot, :, :, :, first : first + width],
            sems[slot],
        )

    def body(i, carry):
        for slot in range(2):
            n = pl.multiple_of(i * 512 + slot * 256, 256)
            left = lhs[:, :, pl.ds(n, 256)].reshape(512, 256)
            tile = product(left, rhs(), ((0,), (0,))).astype(HALF)

            @pl.when(i > 0)
            def _():
                write(i, slot).wait()

            staging[slot, :, :, :, wide] = tile.reshape(4, 2, 32, width)
            write(i, slot).start()
        return carry

    lax.fori_loop(0, 4, body, 0)
    for slot in range(2):
        write(0, slot).wait()


class FourSum:
    def __init__(self, bufs, sems):
        x, y, z, c, t = coords()
        self.to_core, self.from_core, self.from_pair, self.own = bufs
        self.sems = sems
        self.cols = [slice(i * PART, (i + 1) * PART) for i in range(PARTS)]
        core, pair = device(x, y, z, 1 - c, t), device(x, y, z, c, 1 - t)
        self.core = [sems.copy(self.to_core.at[:, n], self.from_core.at[:, n], core) for n in self.cols]
        self.pair = [sems.copy(self.from_core.at[:, n], self.from_pair.at[:, n], pair) for n in self.cols]

    def put(self, i, theirs, ours):
        self.to_core[:, self.cols[i]] = theirs.astype(HALF)
        self.own[:, self.cols[i]] = ours
        self.sems.start(self.core[i])

    def relay(self, i):
        n = self.cols[i]
        self.core[i].wait_recv()

        def add(r):
            self.from_core[r, n] = (self.own[r, n] + self.from_core[r, n].astype(SINGLE)).astype(HALF)

        row_loop(0, TOK, add, 64)
        self.sems.start(self.pair[i])

    def wait(self):
        for copy in self.pair:
            copy.wait_recv()

    def add_relays(self, tasks, label):
        for i in range(PARTS):
            tasks.add(f"{label}.relay{i}", lambda i=i: self.relay(i))

    def total(self, r):
        return self.from_core[r, :].astype(SINGLE) + self.from_pair[r, :].astype(SINGLE)


SUM_COPIES = 2 * PARTS
SUM_SCRATCH = [pltpu.VMEM((TOK, D), HALF) for _ in range(3)] + [pltpu.VMEM((TOK, D), SINGLE)]


def product(a, b, dims):
    return lax.dot_general(a, b, (dims, ((), ())), preferred_element_type=SINGLE)


def allowed_pairs(base):
    row = lax.broadcasted_iota(jnp.int32, (QB, KB), 0)
    col = lax.broadcasted_iota(jnp.int32, (QB, KB), 1)
    return (col > row) & (col <= row + WINDOW) & (col + base >= 0)


def attend_block(q, k, v, base):
    scores = product(q, k, ((1,), (1,))) * SCALE
    scores = jnp.where(allowed_pairs(base), scores, MASKED)
    row_max = jnp.max(scores, axis=-1, keepdims=True)
    expon = jnp.exp(scores - row_max)
    row_total = jnp.sum(expon, axis=-1, keepdims=True)
    probs = (expon * (1.0 / row_total)).astype(HALF)
    mixed = product(probs, v, ((1,), (0,))).astype(HALF)
    return mixed, row_max + jnp.log(row_total)


def attend_block_back(q, k, v, go, lse, base):
    scores = product(q, k, ((1,), (1,))) * SCALE
    scores = jnp.where(allowed_pairs(base), scores, MASKED)
    probs = jnp.exp(scores - lse)
    gp = product(go, v, ((1,), (1,)))
    inner = jnp.sum(probs * gp, axis=-1, keepdims=True)
    gs = (probs * (gp - inner)).astype(HALF)
    gq = product(gs, k, ((1,), (0,))) * SCALE
    gk = product(gs, q, ((0,), (0,))) * SCALE
    gv = product(probs.astype(HALF), go, ((0,), (0,)))
    return gq, gk, gv


def rms_inverse(values):
    return lax.rsqrt(jnp.mean(values * values, axis=-1, keepdims=True) + EPSILON)


def norm_back(grad, values, gain):
    inverse = rms_inverse(values)
    scaled = grad * gain
    slope = jnp.mean(scaled * values, axis=-1, keepdims=True)
    gain_term = jnp.sum(grad * values * inverse, axis=0, keepdims=True)
    return inverse * scaled - values * (inverse * inverse * inverse * slope), gain_term


def row_loop(start, count, fn, step=ROWS):
    def body(i, carry):
        fn(pl.ds(pl.multiple_of(start + i * step, step), step))
        return carry

    lax.fori_loop(0, count // step, body, 0)


def columns(w, n, size):
    return w[:, :, :, :, :, pl.ds(n, size)].reshape(D, size)


def pick_lanes():
    return lax.broadcasted_iota(jnp.int32, (8, LANES), 0) == lax.broadcasted_iota(
        jnp.int32, (8, LANES), 1
    )


def grid_of(w):
    return (4, 2, 4, 2, 32, w)


def params(collective_id):
    return pltpu.CompilerParams(
        collective_id=collective_id, has_side_effects=True, vmem_limit_bytes=VMEM_LIMIT
    )


CHUNKS = ("kv", "q", "out", "ffa", "ffb", "down")
W_KV, W_Q, W_OUT, W_FFA, W_FFB, W_DOWN = range(6)
WFA, WFB = 2048, 768
W_WIDTHS = (2 * HW + LANES, HW, HW, WFA, WFB, FF)
PIECES = {
    W_KV: [(2 * HW, LANES)] + [(n, 2 * HD) for n in range(0, 2 * HW, 2 * HD)],
    W_FFA: [(n, 2 * LANES) for n in range(0, WFA, 2 * LANES)],
    W_FFB: [(n, 2 * LANES) for n in range(0, WFB, 2 * LANES)],
}
ALONG = (0, 1)
ALONG_X = (1, 1)
FORWARD_ORDER = (
    0, 30, 20, 40, 10, 50, 61, 1, 11, 51, 3, 2, 52, 31, 4, 6, 53, 5, 12, 33, 54, 21, 13, 55, 16,
    22, 7, 17, 26, 56, 23, 8, 14, 18, 27, 32, 9, 58, 62, 24, 15, 63, 64, 65, 66, 28, 67, 36, 25,
    19, 68, 69, 29, 59, 34, 57, 60, 41, 82, 83, 70, 71, 42, 37, 35, 43, 72, 73, 74, 46, 75, 76,
    77, 78, 79, 38, 47, 44, 39, 80, 81, 48, 45, 84, 49, 85,
)


class Load:
    def __init__(self, src, dst, pieces, local):
        self.src, self.dst, self.pieces = src, dst, pieces
        self.first = local.used
        self.sems = local.sems
        for _ in pieces:
            local.sem()

    def copy(self, i, n, width):
        lanes = pl.ds(n, width)
        return pltpu.make_async_copy(
            self.src.at[:, :, :, :, :, lanes],
            self.dst.at[:, :, :, :, :, lanes],
            self.sems.at[self.first + i],
        )

    def start(self):
        for i, (n, width) in enumerate(self.pieces):
            self.copy(i, n, width).start()

    def wait(self, i, n=None):
        start, width = self.pieces[0] if n is not None else self.pieces[i]
        self.copy(i, start if n is None else n, width).wait()


class Exchange:
    def __init__(self, sems, mine, copies):
        self.sems, self.mine, self.copies = sems, mine, copies

    def start(self):
        self.mine.start()
        self.sems.start(*self.copies)

    def wait(self):
        self.mine.wait()
        for copy in self.copies:
            copy.wait_recv()


def exchange(sems, local, part, place):
    x, y, z, c, t = coords()
    copies = []
    for d in (2, 1, -1):
        to = moved(x, d)
        copies.append(sems.copy(part(to), place(x), device(to, y, z, c, t)))
    return Exchange(sems, local.copy(part(x), place(x)), copies)


def own_rows(start, v):
    return pl.ds(pl.multiple_of(start + v * 2 * TOK, 2 * TOK), 2 * TOK)


def head_lanes(v, width):
    return pl.ds(pl.multiple_of(v * width, width), width)


def block_rows(i):
    start = pl.multiple_of(i * QB, QB)
    return pl.ds(start, QB), pl.ds(start, KB)


def first_key(i):
    return lax.div(lax.axis_index("seq"), 8) * 2 * WINDOW - WINDOW + i * QB


def arrange(raw, chunks):
    gain_one, gain_two, query, key, value, out, gate, up, down = raw
    to_kv, to_q, to_out, to_ffa, to_ffb, to_down = chunks
    lane = lax.broadcasted_iota(jnp.int32, (32, LANES), 1)
    one, two = [jnp.broadcast_to(g[...], (LANES, 32)).T for g in (gain_one, gain_two)]
    gains = jnp.where(lane == 0, one, jnp.where(lane == 1, two, 0.0)).astype(HALF)
    for j in range(2):
        to_kv[j, :, 2 * HW :] = gains
        to_q[j] = query[:, j * HW : (j + 1) * HW].astype(HALF)
        for h in range(4):
            lanes = slice((4 * j + h) * HD, (4 * j + h + 1) * HD)
            to_kv[j, :, 2 * h * HD : (2 * h + 1) * HD] = key[:, lanes].astype(HALF)
            to_kv[j, :, (2 * h + 1) * HD : (2 * h + 2) * HD] = value[:, lanes].astype(HALF)
            to_out[j, :, h * HD : (h + 1) * HD] = out[:, lanes].astype(HALF)
    blocks_count = FF // LANES
    for j in range(2):
        for i in range(blocks_count):
            n = (j * blocks_count + i) * LANES
            last = min(n + LANES, gate.shape[1])
            parts = [w[:, n:last] for w in (gate, up, down)]
            if last < n + LANES:
                zeros = jnp.zeros((32, n + LANES - last), SINGLE)
                parts = [jnp.concatenate([part, zeros], axis=1) for part in parts]
            chunk, m = (to_ffa, 2 * i * LANES) if 2 * i * LANES < WFA else (to_ffb, 2 * i * LANES - WFA)
            chunk[j, :, m : m + LANES] = parts[0].astype(HALF)
            chunk[j, :, m + LANES : m + 2 * LANES] = parts[1].astype(HALF)
            to_down[j, :, i * LANES : (i + 1) * LANES] = parts[2].astype(HALF)


def forward_kernel(*refs):
    n_w = len(CHUNKS)
    raw_in, (hid, cot), rest = refs[:9], refs[9:11], refs[11:]
    w_out, kept, gains, rest = rest[:n_w], rest[n_w : n_w + 10], rest[n_w + 10], rest[n_w + 11 :]
    results, rest = rest[:10], rest[10:]
    a1, cots, q, kv, o, lse, mid, a2, hid_ff, grad_ff = results
    raw, w_in, rest = rest[:9], rest[9 : 9 + n_w], rest[9 + n_w :]
    weights, rest = rest[:n_w], rest[n_w:]
    w_kv, w_q, w_o, _, _, w_down = weights
    rows, ghid, kv_own, q_own, o_all = rest[:5]
    sum_bufs, (send, recv, local_sems) = rest[5:9], rest[9:]
    x, y, z, c, t = coords()
    core, pair = device(x, y, z, 1 - c, t), device(x, y, z, c, 1 - t)
    theirs, ours = [pl.ds(pl.multiple_of(k * TOK, TOK), TOK) for k in (1 - c, c)]
    sems, local = Sems(send, recv), Locals(local_sems)
    raw_loads = [local.load(src, dst) for src, dst in zip(raw_in, raw, strict=True)]
    stores = [local.copy(src, dst) for src, dst in zip(results, kept, strict=True)]
    partners = neighbours() + [pair, device(moved(x, 2), y, z, c, t), chip_shift(4), chip_shift(-4)]
    say_hello(partners)
    for load in raw_loads:
        load.wait()
    arrange(raw, w_in)
    hear_hello(partners)

    def store(*which):
        for i in which:
            stores[i].start()

    tasks = Tasks()
    loads = []
    for i, label in enumerate(CHUNKS):
        add = add_plane_gather if i == W_DOWN else add_gather
        along = ALONG_X if i == W_OUT else ALONG
        load = Load(w_out[i], weights[i], PIECES.get(i, [(0, W_WIDTHS[i])]), local)
        add(tasks, label, along, w_in[i], w_out[i], load, sems, local)
        loads.append(load)
    tasks.add("ldkv", lambda: loads[W_KV].wait(0))
    tasks.add("ldo", lambda: loads[W_OUT].wait(0))
    tasks.add("lddown", lambda: loads[W_DOWN].wait(0))

    row_copy, cot_copy = local.copy(hid, rows.at[c]), local.copy(cot, cots.at[c])
    row_swap, cot_swap = sems.copy(hid, rows.at[c], core), sems.copy(cot, cots.at[c], core)

    def swaps():
        row_copy.start()
        cot_copy.start()
        sems.start(row_swap, cot_swap)

    tasks.add("swaps", swaps)

    def norm():
        row_copy.wait()
        row_swap.wait_recv()
        pick = pick_lanes().astype(HALF)
        gains[...] = product(pick, columns(w_kv, 2 * HW, LANES), ((1,), (1,)))
        for half in range(2):

            def norm_one(r, half=half):
                values = rows[half, r, :].astype(SINGLE)
                a1[half, r, :] = (values * rms_inverse(values) * gains[0:1, :]).astype(HALF)

            row_loop(0, TOK, norm_one)
        store(0)

    tasks.add("norm", norm)

    def project(w, n):
        w_cols = columns(w, n, 2 * HD)
        return [product(a1[half], w_cols, ((1,), (0,))).astype(HALF) for half in range(2)]

    kv_swap = exchange(sems, local, lambda v: kv_own.at[v], lambda v: kv.at[own_rows(WINDOW, v)])
    q_swap = exchange(sems, local, lambda v: q_own.at[v], lambda v: q.at[own_rows(0, v)])
    o_swap = exchange(sems, local, lambda v: o_all.at[own_rows(0, v)], lambda v: o.at[:, head_lanes(v, HD)])
    halo = sems.copy(kv.at[2 * WINDOW : 3 * WINDOW], kv.at[0:WINDOW], chip_shift(4))
    for h in range(4):

        def project_kv(h=h):
            loads[W_KV].wait(1 + h)
            for half, out in enumerate(project(w_kv, h * 2 * HD)):
                kv_own[h, half * TOK : (half + 1) * TOK, :] = out

        tasks.add(f"proj{h}", project_kv)
    tasks.add("kva", kv_swap.start)

    def project_q():
        loads[W_Q].wait(0)
        for n in range(2):
            for half, out in enumerate(project(w_q, n * 2 * HD)):
                for k in range(2):
                    q_own[2 * n + k, half * TOK : (half + 1) * TOK, :] = out[
                        :, k * HD : (k + 1) * HD
                    ]
        q_swap.start()

    tasks.add("projq", project_q)

    def send_halo():
        kv_swap.wait()
        sems.start(halo)

    tasks.add("halo", send_halo)

    def attend_one(i, carry):
        mine, keys = block_rows(i)
        mixed, total = attend_block(
            q[mine, :], kv[keys, :HD], kv[keys, HD:], first_key(i)
        )
        o_all[mine, :] = mixed
        lse[mine, :] = jnp.broadcast_to(total, (QB, HD))
        return carry

    def attend_late():
        q_swap.wait()
        lax.fori_loop(4, 8, attend_one, 0)

    def attend_early():
        halo.wait_recv()
        lax.fori_loop(0, 4, attend_one, 0)
        o_swap.start()
        store(2, 3, 5)

    tasks.add("attA", attend_late)
    tasks.add("attB", attend_early)

    attended = FourSum(sum_bufs, sems)
    for i in range(PARTS):

        def put(i=i):
            if i == 0:
                o_swap.wait()
                store(4)
            w_rows = w_o[i].reshape(PART, HW)
            attended.put(i, *[product(o[r, :], w_rows, ((1,), (1,))) for r in (theirs, ours)])

        tasks.add(f"att.put{i}", put)
    attended.add_relays(tasks, "att")
    spreads = []
    for half in range(2):
        part = a2.at[c, half * 128 : (half + 1) * 128]
        spreads.append(sems.copy(part, part, core))

        def norm_two_half(half=half):
            if half == 0:
                attended.wait()

            def norm_two(r):
                values = rows[c, r, :].astype(SINGLE) + attended.total(r)
                mid[r, :] = values
                a2[c, r, :] = (values * rms_inverse(values) * gains[1:2, :]).astype(HALF)

            row_loop(half * 128, 128, norm_two)
            sems.start(spreads[half])

        tasks.add(f"norm2{half}", norm_two_half)

    def hidden_grads(first, count):
        def task():
            w_cols = columns(w_down, first, count)
            for half in range(2):
                r = slice(half * TOK, (half + 1) * TOK)
                ghid[r, first : first + count] = product(cots[half], w_cols, ((1,), (0,)))

        return task

    def hidden_grads_a():
        cot_copy.wait()
        cot_swap.wait_recv()
        store(1)
        for n in range(0, FFA // 2, 2 * LANES):
            hidden_grads(n, 2 * LANES)()

    def hidden_grads_b():
        for n in range(FFA // 2, FF, 2 * LANES):
            hidden_grads(n, min(2 * LANES, FF - n))()

    tasks.add("ghida", hidden_grads_a)
    tasks.add("ghidb", hidden_grads_b)

    def feed_forward(chunk, first, i, carry):
        n = pl.multiple_of(i * 2 * LANES, 2 * LANES)
        loads[chunk].wait(i, n)
        w_cols = columns(weights[chunk], n, 2 * LANES)
        gate_lanes = pl.ds(pl.multiple_of(first + n, 2 * LANES), LANES)
        up_lanes = pl.ds(pl.multiple_of(first + n + LANES, LANES), LANES)
        lanes = pl.ds(pl.multiple_of(first // 2 + i * LANES, LANES), LANES)
        for half in range(2):
            r = slice(half * TOK, (half + 1) * TOK)
            both = product(a2[half], w_cols, ((1,), (0,)))
            gate, up_part = both[:, :LANES], both[:, LANES:]
            sig = 1.0 / (1.0 + jnp.exp(-gate))
            hid_ff[r, lanes] = (gate * sig * up_part).astype(HALF)
            grad = ghid[r, lanes]
            grad_ff[r, gate_lanes] = (
                grad * up_part * sig * (1.0 + gate * (1.0 - sig))
            ).astype(HALF)
            grad_ff[r, up_lanes] = (grad * gate * sig).astype(HALF)
        return carry

    pairs_a, pairs = WFA // (2 * LANES), FF // LANES

    def feed_forward_a():
        for copy in spreads:
            copy.wait_recv()
        store(6, 7)
        lax.fori_loop(0, pairs_a, lambda i, carry: feed_forward(W_FFA, 0, i, carry), 0)

    def feed_forward_b():
        lax.fori_loop(
            0, pairs - pairs_a, lambda i, carry: feed_forward(W_FFB, WFA, i, carry), 0
        )
        store(8, 9)

    tasks.add("gua", feed_forward_a)
    tasks.add("gub", feed_forward_b)
    tasks.run(FORWARD_ORDER)
    for copy in stores:
        copy.wait()
    sems.finish()


def forward(raw, hid, cot):
    n = len(CHUNKS)
    copies = GATHER_COPIES * n + 2 + 3 * 3 + 1 + SUM_COPIES + 2
    kept = [
        ((2, TOK, D), HALF),
        ((2, TOK, D), HALF),
        ((2 * WINDOW, HD), HALF),
        ((3 * WINDOW, 2 * HD), HALF),
        ((2 * TOK, HW), HALF),
        ((2 * WINDOW, HD), SINGLE),
        ((TOK, D), SINGLE),
        ((2, TOK, D), HALF),
        ((2 * TOK, FF), HALF),
        ((2 * TOK, 2 * FF), HALF),
    ]
    return pl.pallas_call(
        forward_kernel,
        out_shape=[SHAPE(grid_of(w), HALF) for w in W_WIDTHS]
        + [SHAPE(*k) for k in kept]
        + [SHAPE((8, D), SINGLE)],
        in_specs=[ANYWHERE] * (len(raw) + 2),
        out_specs=[ANYWHERE] * (n + len(kept)) + [IN_VMEM],
        scratch_shapes=[pltpu.VMEM(*k) for k in kept]
        + [pltpu.VMEM(w.shape, SINGLE) for w in raw]
        + [pltpu.VMEM((2, 32, w), HALF) for w in W_WIDTHS]
        + [pltpu.VMEM(grid_of(w), HALF) for w in W_WIDTHS]
        + [
            pltpu.VMEM((2, TOK, D), HALF),
            pltpu.VMEM((2 * TOK, FF), SINGLE),
            pltpu.VMEM((4, 2 * TOK, 2 * HD), HALF),
            pltpu.VMEM((4, 2 * TOK, HD), HALF),
            pltpu.VMEM((2 * WINDOW, HD), HALF),
        ]
        + SUM_SCRATCH
        + [
            pltpu.SemaphoreType.DMA((copies,)),
            pltpu.SemaphoreType.DMA((copies,)),
            pltpu.SemaphoreType.DMA((2 * n + sum(len(p) for p in PIECES.values()) + 5 + len(raw) + len(kept),)),
        ],
        compiler_params=params(0),
    )(*raw, hid, cot)


GRADS = ("down", "ffa", "ffb", "oq", "kv", "gain")
G_DOWN, G_FFA, G_FFB, G_OQ, G_KV, G_GAIN = range(6)
G_WIDTHS = (FF, FFA, FFB, 2 * HW, 2 * HW, LANES)
BACKWARD_ORDER = (
    54, 0, 55, 56, 57, 58, 64, 1, 2, 59, 60, 63, 61, 62, 9, 3, 4, 10, 11, 65, 66, 5, 67, 18, 12,
    13, 6, 68, 7, 69, 19, 20, 73, 14, 8, 74, 75, 76, 77, 78, 79, 80, 71, 70, 27, 21, 22, 15, 81,
    82, 83, 89, 84, 85, 16, 28, 29, 86, 87, 88, 17, 72, 23, 36, 30, 31, 24, 37, 38, 90, 91, 25,
    32, 26, 45, 39, 40, 33, 46, 47, 41, 34, 48, 49, 42, 35, 50, 51, 43, 52, 44, 53,
)


def backward_kernel(*refs):
    n_w, n_g = len(CHUNKS), len(GRADS)
    w_kv, w_q, w_out, w_ffa, w_ffb, w_down = refs[:n_w]
    rest = refs[n_w:]
    a1_in, cots, q_in, kv_in, o_in, lse_in, mid_in, a2_in, hid_in, grad_ff_in, rows_in, gains = rest[:12]
    rest = rest[12:]
    s_query, s_key, s_value, s_out, s_gate, s_up, s_down, s_gain, in_grad, hidden_out = rest[:10]
    rest = rest[10:]
    g_refs, slots, rest = rest[:n_g], rest[n_g : 3 * n_g], rest[3 * n_g :]
    scratch, rest = rest[: 4 * n_g], rest[4 * n_g :]
    shared, rest = rest[:5], rest[5:]
    to_core, own_sum, rest = rest[0], rest[1], rest[2:]
    gn2_bufs, gn1_bufs, out_bufs, rest = rest[:2], rest[2:4], rest[4:6], rest[6:]
    (
        staging,
        cot_v,
        gatt,
        rows_v,
        hid_ff,
        grad_ff,
        mid,
        q,
        kv,
        lse,
        o,
        tiles,
        go,
        go_all,
        acc,
        far,
        got,
        gq_all,
        gkv_all,
        gq,
        gkv,
        gain_acc,
        send,
        recv,
        local_sems,
    ) = rest
    x, y, z, c, t = coords()
    core, pair = device(x, y, z, 1 - c, t), device(x, y, z, c, 1 - t)
    sems, local = Sems(send, recv), Locals(local_sems)
    theirs, ours = [pl.ds(pl.multiple_of(k * TOK, TOK), TOK) for k in (1 - c, c)]
    tasks = Tasks()

    def tile_loads(*sources):
        loads = []
        for i in range(8):
            copies, n = [], 0
            for source, width in sources:
                copies.append(
                    local.copy(
                        source.at[i // 2, i % 2, :, :, :, 0:width],
                        tiles.at[i % 2, :, :, :, n : n + width],
                    )
                )
                n += width
            loads.append(copies)
        return loads

    def begin(*loads):
        for copies in loads:
            for copy in copies:
                copy.start()

    def tile(k, start, width):
        return tiles[k, :, :, :, start : start + width].reshape(256, width)

    def add_sum(label, bufs, loads, multiply, last=None, then=None):
        total = FourSum([to_core, *bufs, own_sum], sems)
        for i in range(PARTS):

            def put(i=i):
                if i == 0 and last is not None:
                    sems.sent(last.core)
                parts = []
                for k in range(2):
                    for copy in loads[2 * i + k]:
                        copy.wait()
                    parts.append([multiply(r, k) for r in (theirs, ours)])
                    if 2 * i + k + 2 < 8:
                        begin(loads[2 * i + k + 2])
                total.put(
                    i, *[jnp.concatenate([parts[0][j], parts[1][j]], axis=1) for j in range(2)]
                )
                if i == PARTS - 1 and then is not None:
                    then()

            tasks.add(f"{label}.put{i}", put)
        total.add_relays(tasks, label)
        return total

    partners = neighbours() + [pair, device(moved(x, 2), y, z, c, t), chip_shift(4), chip_shift(-4)]
    say_hello(partners)
    load_cot, load_hid = local.load(cots, cot_v), local.load(hid_in, hid_ff)
    load_grad = local.load(grad_ff_in, grad_ff)
    ff_loads = tile_loads((w_ffa, WFA), (w_ffb, WFB))
    begin(ff_loads[0], ff_loads[1])
    load_a2 = local.load(a2_in, rows_v)
    later = [
        local.load(src, dst)
        for src, dst in (
            (mid_in, mid),
            (q_in, q),
            (kv_in, kv),
            (lse_in, lse),
            (o_in, o),
        )
    ]
    load_a1 = local.copy(a1_in, rows_v)
    out_loads = [
        local.copy(
            w_out.at[i // 2, i % 2], tiles.at[i // 4, :, :, :, (i % 4) * HW : (i % 4 + 1) * HW]
        )
        for i in range(8)
    ]
    down_loads = tile_loads((w_down, FF))
    qkv_loads = tile_loads((w_q, HW), (w_kv, 2 * HW))

    def place_plain(target, width, read):
        for j in range(2):
            for n in range(0, width, LANES):
                start = j * width + n
                lanes = min(LANES, target.shape[1] - start)
                target[:, start : start + lanes] = read(j, n)[:, :lanes]

    def place_ff(first, width, read):
        for j in range(2):
            for n in range(0, width, 2 * LANES):
                start = j * FF + (first + n) // 2
                lanes = min(LANES, s_gate.shape[1] - start)
                s_gate[:, start : start + lanes] = read(j, n)[:, :lanes]
                s_up[:, start : start + lanes] = read(j, n + LANES)[:, :lanes]

    def place_oq(read):
        place_plain(s_out, HW, read)
        place_plain(s_query, HW, lambda j, n: read(j, HW + n))

    def place_kv(read):
        for j in range(2):
            for h in range(4):
                lanes = slice((4 * j + h) * HD, (4 * j + h + 1) * HD)
                s_key[:, lanes] = read(j, 2 * h * HD)
                s_value[:, lanes] = read(j, (2 * h + 1) * HD)

    def place_gain(read):
        s_gain[...] = (read(0, 0) + read(1, 0)).T[:8]

    place = (
        lambda read: place_plain(s_down, FF, read),
        lambda read: place_ff(0, FFA, read),
        lambda read: place_ff(FFA, FFB, read),
        place_oq,
        place_kv,
        place_gain,
    )
    scatter = Scatter(tasks, shared, sems, local)
    for i, label in enumerate(GRADS):
        scatter.add(
            label,
            ALONG,
            g_refs[i],
            place[i],
            slots[2 * i : 2 * i + 2],
            scratch[4 * i : 4 * i + 4],
        )
    waited = set()

    def once(load):
        if id(load) not in waited:
            waited.add(id(load))
            load.wait()

    def grad_down():
        once(load_cot)
        once(load_hid)
        make_grads(cot_v, lambda: hid_ff[...], staging, g_refs[G_DOWN], local)
        hear_hello(partners)

    tasks.add("gdown", grad_down)

    def multiply_ff(r, k):
        once(load_grad)
        return product(grad_ff[r, :], tile(k, 0, 2 * FF), ((1,), (1,)))

    gn2 = add_sum("gn2", gn2_bufs, ff_loads, multiply_ff, None, lambda: begin(out_loads))

    def grad_ffa():
        once(load_a2)
        make_grads(rows_v, lambda: grad_ff[:, :FFA], staging, g_refs[G_FFA], local)

    def grad_ffb():
        once(load_a2)
        make_grads(rows_v, lambda: grad_ff[:, FFA:], staging, g_refs[G_FFB], local)

    tasks.add("gffa", grad_ffa)
    tasks.add("gffb", grad_ffb)
    spreads = []
    for half in range(2):
        part = gatt.at[c, half * 128 : (half + 1) * 128]
        spreads.append(sems.copy(part, part, core))

        def mid_back_half(half=half):
            if half == 0:
                gn2.wait()
                for load in later:
                    load.wait()
                gain_acc[...] = jnp.zeros_like(gain_acc)

            def mid_back(r):
                part, term = norm_back(gn2.total(r), mid[r, :], gains[1:2, :])
                grad = cot_v[c, r, :].astype(SINGLE) + part
                in_grad[r, :] = grad
                gatt[c, r, :] = grad.astype(HALF)
                gain_acc[1:2, :] += term

            row_loop(half * 128, 128, mid_back)
            sems.start(spreads[half])

        tasks.add(f"mid{half}", mid_back_half)

    def attended_back():
        for copy in out_loads:
            copy.wait()
        for copy in spreads:
            copy.wait_recv()
        for half in range(2):
            total = jnp.zeros((TOK, HW), SINGLE)
            for i in range(8):
                total += product(
                    gatt[half, :, i * 256 : (i + 1) * 256],
                    tile(i // 4, (i % 4) * HW, HW),
                    ((1,), (0,)),
                )
            go[half * TOK : (half + 1) * TOK, :] = total.astype(HALF)
        go_swap.start()
        begin(down_loads[0], down_loads[1])

    tasks.add("go", attended_back)

    go_swap = exchange(
        sems, local, lambda v: go.at[:, head_lanes(v, HD)], lambda v: go_all.at[own_rows(0, v)]
    )
    gq_swap = exchange(
        sems, local, lambda v: gq_all.at[own_rows(0, v)], lambda v: gq.at[:, head_lanes(v, HD)]
    )
    gkv_swap = exchange(
        sems,
        local,
        lambda v: gkv_all.at[own_rows(0, v)],
        lambda v: gkv.at[:, head_lanes(v, 2 * HD)],
    )
    back = sems.copy(far, got, chip_shift(-4))

    def attend_one(i, carry):
        mine, keys = block_rows(i)
        grad_q, grad_k, grad_v = attend_block_back(
            q[mine, :], kv[keys, :HD], kv[keys, HD:], go_all[mine, :], lse[mine, 0:1], first_key(i)
        )
        gq_all[mine, :] = grad_q.astype(HALF)
        acc[keys, :HD] += grad_k
        acc[keys, HD:] += grad_v
        return carry

    def attend_early():
        load_a1.start()
        acc[...] = jnp.zeros_like(acc)
        go_swap.wait()
        lax.fori_loop(0, 4, attend_one, 0)
        far[...] = acc[0:WINDOW, :].astype(HALF)
        sems.start(back)

    def attend_late():
        lax.fori_loop(4, 8, attend_one, 0)
        gq_swap.start()

    def add_back():
        back.wait_recv()

        def keep(r):
            gkv_all[r, :] = acc[pl.ds(pl.multiple_of(WINDOW + r.start, 64), 64), :].astype(HALF)

        def add(r):
            total = acc[pl.ds(pl.multiple_of(2 * WINDOW + r.start, 64), 64), :]
            total = total + got[r, :].astype(SINGLE)
            gkv_all[pl.ds(pl.multiple_of(WINDOW + r.start, 64), 64), :] = total.astype(HALF)

        row_loop(0, WINDOW, keep, 64)
        row_loop(0, WINDOW, add, 64)
        gkv_swap.start()

    tasks.add("attbA", attend_early)
    tasks.add("attbB", attend_late)
    tasks.add("gadd", add_back)

    def once_arrived(swap):
        if id(swap) not in waited:
            waited.add(id(swap))
            swap.wait()

    def grad_oq():
        once(load_a1)
        once_arrived(gq_swap)
        make_grads(gatt, lambda: o[...], staging, g_refs[G_OQ], local, 0, HW)
        make_grads(rows_v, lambda: gq[...], staging, g_refs[G_OQ], local, HW, HW)

    def grad_kv():
        once(load_a1)
        once_arrived(gkv_swap)
        make_grads(rows_v, lambda: gkv[...], staging, g_refs[G_KV], local)

    tasks.add("goq", grad_oq)
    tasks.add("gkv", grad_kv)
    out_sum = add_sum(
        "out",
        out_bufs,
        down_loads,
        lambda r, k: product(hid_ff[r, :], tile(k, 0, FF), ((1,), (1,))),
        gn2,
        lambda: begin(qkv_loads[0], qkv_loads[1]),
    )

    def multiply_qkv(r, k):
        once_arrived(gq_swap)
        once_arrived(gkv_swap)
        from_q = product(gq[r, :], tile(k, 0, HW), ((1,), (1,)))
        return from_q + product(gkv[r, :], tile(k, HW, 2 * HW), ((1,), (1,)))

    gn1 = add_sum(
        "gn1",
        gn1_bufs,
        qkv_loads,
        multiply_qkv,
        out_sum,
    )

    def rows_out():
        out_sum.wait()

        def add(r):
            hidden_out[r, :] = (mid[r, :] + out_sum.total(r)).astype(HALF)

        row_loop(0, TOK, add)

    load_rows = local.copy(rows_in, to_core)

    def rows_back():
        sems.sent(gn1.core)
        load_rows.start()
        gn1.wait()
        load_rows.wait()

        def add(r):
            part, term = norm_back(gn1.total(r), to_core[r, :].astype(SINGLE), gains[0:1, :])
            in_grad[r, :] = in_grad[r, :] + part
            gain_acc[0:1, :] += term

        row_loop(0, TOK, add)

    tasks.add("rowsout", rows_out)
    tasks.add("rowsback", rows_back)

    def grad_gain():
        pick = pick_lanes().astype(HALF)
        writes = []
        for n in range(8):
            lanes = slice(n * LANES, (n + 1) * LANES)
            cols = product(gain_acc[:, n * 256 : (n + 1) * 256].astype(HALF), pick, ((0,), (0,)))
            staging[0, :, :, :, lanes] = cols.astype(HALF).reshape(4, 2, 32, LANES)
            writes.append(
                local.load(staging.at[0, :, :, :, lanes], g_refs[G_GAIN].at[n // 2, n % 2])
            )
        for copy in writes:
            copy.wait()

    tasks.add("ggain", grad_gain)
    tasks.run(BACKWARD_ORDER)
    sems.finish()


def backward(hidden_units, *operands):
    n = len(GRADS)
    copies = SCATTER_COPIES * n + SUM_COPIES * 3 + 2 + 3 * 3 + 1
    loads = 11 + 8 * (2 + 1 + 1 + 2) + SCATTER_LOADS * n + 2 * 6 + 8 + 3
    slots = [slot for w in G_WIDTHS for slot in scatter_slots(w)]
    widest = max(G_WIDTHS)
    results = [(32, 2 * HW)] * 4 + [(32, hidden_units)] * 3 + [(8, 32)]
    rows_half = pltpu.VMEM((TOK, D), HALF)
    return pl.pallas_call(
        backward_kernel,
        out_shape=[SHAPE(s, SINGLE) for s in results]
        + [SHAPE((TOK, D), SINGLE), SHAPE((TOK, D), HALF)]
        + [SHAPE(grid_of(w), HALF) for w in G_WIDTHS]
        + slots,
        in_specs=[ANYWHERE] * (len(operands) - 1) + [IN_VMEM],
        out_specs=[IN_VMEM] * (len(results) + 2) + [ANYWHERE] * (n + len(slots)),
        scratch_shapes=[buf for w in G_WIDTHS for buf in scatter_scratch(w)]
        + scatter_shared(widest)
        + [rows_half, pltpu.VMEM((TOK, D), SINGLE)]
        + [rows_half] * 6
        + [
            pltpu.VMEM((2, 4, 2, 32, widest), HALF),
            pltpu.VMEM((2, TOK, D), HALF),
            pltpu.VMEM((2, TOK, D), HALF),
            pltpu.VMEM((2, TOK, D), HALF),
            pltpu.VMEM((2 * TOK, FF), HALF),
            pltpu.VMEM((2 * TOK, 2 * FF), HALF),
            pltpu.VMEM((TOK, D), SINGLE),
            pltpu.VMEM((2 * WINDOW, HD), HALF),
            pltpu.VMEM((3 * WINDOW, 2 * HD), HALF),
            pltpu.VMEM((2 * WINDOW, HD), SINGLE),
            pltpu.VMEM((2 * TOK, HW), HALF),
            pltpu.VMEM((2, 4, 2, 32, 2 * FF), HALF),
            pltpu.VMEM((2 * TOK, HW), HALF),
            pltpu.VMEM((2 * WINDOW, HD), HALF),
            pltpu.VMEM((3 * WINDOW, 2 * HD), SINGLE),
            pltpu.VMEM((WINDOW, 2 * HD), HALF),
            pltpu.VMEM((WINDOW, 2 * HD), HALF),
            pltpu.VMEM((2 * WINDOW, HD), HALF),
            pltpu.VMEM((2 * WINDOW, 2 * HD), HALF),
            pltpu.VMEM((2 * TOK, HW), HALF),
            pltpu.VMEM((2 * TOK, 2 * HW), HALF),
            pltpu.VMEM((8, D), SINGLE),
            pltpu.SemaphoreType.DMA((copies,)),
            pltpu.SemaphoreType.DMA((copies,)),
            pltpu.SemaphoreType.DMA((loads,)),
        ],
        compiler_params=params(1),
    )(*operands)


def hand_over_kernel(count, *refs):
    ins, outs, refs = refs[:count], refs[count : 2 * count], refs[2 * count :]
    held, sems = refs[:count], refs[count]
    load = [pltpu.make_async_copy(ins[i], held[i], sems.at[0, i]) for i in range(count)]
    store = [pltpu.make_async_copy(held[i], outs[i], sems.at[1, i]) for i in range(count)]
    for copy in load:
        copy.start()
    for i in range(count):
        load[i].wait()
        store[i].start()
    for copy in store:
        copy.wait()


def hand_over(*arrays):
    n = len(arrays)
    return pl.pallas_call(
        functools.partial(hand_over_kernel, n),
        out_shape=[SHAPE(a.shape, a.dtype) for a in arrays],
        in_specs=[ANYWHERE] * n,
        out_specs=[ANYWHERE] * n,
        scratch_shapes=[pltpu.VMEM(a.shape, a.dtype) for a in arrays]
        + [pltpu.SemaphoreType.DMA((2, n))],
        compiler_params=pltpu.CompilerParams(vmem_limit_bytes=VMEM_LIMIT),
    )(*arrays)


def per_device(
    hidden_in, attn_gain, w_query, w_key, w_value, w_out, ffn_gain, w_gate, w_up, w_down, out_grad
):
    weights = (w_query, w_key, w_value, w_out.T, w_gate, w_up, w_down.T)
    gains = (attn_gain.reshape(1, -1), ffn_gain.reshape(1, -1))
    *kept, gain_rows = forward((*gains, *weights), hidden_in, out_grad)
    results = backward(w_gate.shape[1], *kept, hidden_in, gain_rows)[:10]
    s_query, s_key, s_value, s_out, s_gate, s_up, s_down, s_gain, in_grad, hidden_out = hand_over(
        *results
    )
    return (
        hidden_out,
        in_grad,
        s_gain[0],
        s_query,
        s_key,
        s_value,
        s_out.T,
        s_gain[1],
        s_gate,
        s_up,
        s_down.T,
    )


def solution(mesh):
    placed = (
        P("seq", None),
        P("seq"),
        P("seq", "tp"),
        P("seq", "tp"),
        P("seq", "tp"),
        P("tp", "seq"),
        P("seq"),
        P("seq", "tp"),
        P("seq", "tp"),
        P("tp", "seq"),
        P("seq", None),
    )
    return jax.shard_map(
        per_device,
        mesh=mesh,
        in_specs=placed,
        out_specs=(
            P("seq", None),
            P("seq", None),
            P("seq"),
            P("seq", "tp"),
            P("seq", "tp"),
            P("seq", "tp"),
            P("tp", "seq"),
            P("seq"),
            P("seq", "tp"),
            P("seq", "tp"),
            P("tp", "seq"),
        ),
        check_vma=False,
    )
```

```python
import functools
import math

import jax
import jax.numpy as jnp
from jax import lax
from jax.experimental import pallas as pl
from jax.experimental.pallas import tpu as pltpu
from jax.sharding import PartitionSpec as P

HD = 128
WINDOW = 1024
EPSILON = 1e-06
MASKED = -1e30
MESH = pl.DeviceIdType.MESH
HALF = jnp.bfloat16
SINGLE = jnp.float32
VMEM_LIMIT = 63 * 2**20

D = 2048
TOK = 256
HW = 512
FF = 1408
FFA, FFB = 1536, 1280
QB = 256
KB = QB + WINDOW
SCALE = 1.0 / math.sqrt(HD)
ROWS = 16
LANES = 128
PART = 512
PARTS = D // PART

ANYWHERE = pl.BlockSpec(memory_space=pl.ANY)
IN_VMEM = pl.BlockSpec(memory_space=pltpu.VMEM)
SHAPE = jax.ShapeDtypeStruct


def coords():
    s = lax.axis_index("seq")
    t = lax.axis_index("tp")
    return lax.rem(lax.div(s, 2), 4), lax.div(s, 16), lax.rem(lax.div(s, 8), 2), lax.rem(s, 2), t


def device(x, y, z, c, t):
    return (((y * 2 + z) * 4 + x) * 2 + c, t)


def moved(v, steps):
    return lax.rem(v + steps + 4, 4)


def chip_shift(steps):
    s = lax.axis_index("seq")
    return (lax.rem(s + 2 * steps + 64, 64), lax.axis_index("tp"))


def neighbours():
    x, y, z, c, t = coords()
    return [
        device(moved(x, 1), y, z, c, t),
        device(moved(x, -1), y, z, c, t),
        device(x, moved(y, 1), z, c, t),
        device(x, moved(y, -1), z, c, t),
        device(x, y, 1 - z, c, t),
        device(x, y, z, 1 - c, t),
    ]


def say_hello(partners):
    barrier = pltpu.get_barrier_semaphore()
    for partner in partners:
        pl.semaphore_signal(barrier, inc=1, device_id=partner, device_id_type=MESH)


def hear_hello(partners):
    pl.semaphore_wait(pltpu.get_barrier_semaphore(), len(partners))


class Sems:
    def __init__(self, send, recv):
        self.send, self.recv, self.used, self.started = send, recv, 0, []

    def copy(self, src, dst, dev):
        i = self.used
        self.used += 1
        return pltpu.make_async_remote_copy(
            src, dst, self.send.at[i], self.recv.at[i], device_id=dev, device_id_type=MESH
        )

    def start(self, *copies):
        for copy in copies:
            copy.start()
            self.started.append(copy)

    def sent(self, copies):
        for copy in copies:
            copy.wait_send()
            self.started = [other for other in self.started if other is not copy]

    def finish(self):
        self.sent(list(self.started))


class Locals:
    def __init__(self, sems):
        self.sems, self.used = sems, 0

    def sem(self):
        self.used += 1
        return self.sems.at[self.used - 1]

    def copy(self, src, dst):
        return pltpu.make_async_copy(src, dst, self.sem())

    def load(self, src, dst):
        copy = self.copy(src, dst)
        copy.start()
        return copy


class Tasks:
    def __init__(self):
        self.tasks = {}

    def add(self, name, task):
        self.tasks[name] = task

    def run(self, order):
        tasks = list(self.tasks.values())
        assert sorted(order) == list(range(len(tasks)))
        for i in order:
            tasks[i]()


def grid_piece(along_x):
    x, y, z, c, t = coords()
    if along_x:
        return x, y, lambda v: device(v, y, z, c, t), lambda v: device(x, v, z, c, t)
    return y, x, lambda v: device(x, v, z, c, t), lambda v: device(v, y, z, c, t)


def blocks(ref, along_x, h, a, zs, b):
    return ref.at[b, zs, a, h] if along_x else ref.at[a, zs, b, h]


ALL = slice(None)


GATHER_COPIES = 1 + 4 * 6 + 8


def gather_streams(along, out, sems, planes, rows):
    streams = []
    for h in range(2):
        a, b, to_a, to_b = grid_piece(along[h])
        for s, d in ((0, 1), (1, -1)):

            def copy(aa, bb, dev, h=h, s=s):
                src = blocks(out, along[h], h, aa, planes[s], bb)
                src = src.at[rows[s]] if aa is not ALL else src.at[:, rows[s]]
                return sems.copy(src, src, dev)

            streams.append(
                dict(
                    a1f=copy(a, b, to_a(moved(a, d))),
                    a1r=copy(a, b, to_a(moved(a, -d))),
                    a2=copy(moved(a, -d), b, to_a(moved(a, d))),
                    b1f=copy(ALL, b, to_b(moved(b, d))),
                    b1r=copy(ALL, b, to_b(moved(b, -d))),
                    b2=copy(ALL, moved(b, -d), to_b(moved(b, d))),
                )
            )
    return streams


def add_gather(tasks, label, along, w_in, out, load, sems, local):
    x, y, z, c, t = coords()
    mine = local.copy(w_in.at[c], out.at[y, z, x, c])
    swap = sems.copy(w_in.at[1 - c], out.at[y, z, x, c], device(x, y, z, 1 - c, t))
    over_z = []
    for h in range(2):
        src = out.at[y, z, x, h]
        over_z.append(sems.copy(src, src, device(x, y, 1 - z, c, t)))
    streams = gather_streams(along, out, sems, (z, 1 - z), (ALL, ALL))
    add = lambda name, task: tasks.add(f"{label}.{name}", task)

    def init():
        mine.start()
        sems.start(swap)

    def own():
        mine.wait()
        swap.wait_recv()
        sems.start(*over_z)
        for p in streams[0::2]:
            sems.start(p["a1f"], p["a1r"])

    def other():
        for copy in over_z:
            copy.wait_recv()
        for p in streams[1::2]:
            sems.start(p["a1f"], p["a1r"])

    def a2(ps):
        for p in ps:
            p["a1f"].wait_recv()
            sems.start(p["a2"])

    def b1(ps):
        for p in ps:
            p["a1r"].wait_recv()
            p["a2"].wait_recv()
            sems.start(p["b1f"], p["b1r"])

    def b2(ps):
        for p in ps:
            p["b1f"].wait_recv()
            sems.start(p["b2"])

    def end():
        for p in streams:
            p["b1r"].wait_recv()
            p["b2"].wait_recv()
        load.start()

    add("init", init)
    add("own", own)
    add("other", other)
    for s in range(2):
        add(f"a2{s}", lambda s=s: a2(streams[s::2]))
        add(f"b1{s}", lambda s=s: b1(streams[s::2]))
        add(f"b2{s}", lambda s=s: b2(streams[s::2]))
    add("end", end)


def add_plane_gather(tasks, label, along, w_in, out, load, sems, local):
    x, y, z, c, t = coords()
    mine = local.copy(w_in.at[c], out.at[y, z, x, c])
    swap = sems.copy(w_in.at[1 - c], out.at[y, z, x, c], device(x, y, z, 1 - c, t))
    streams = gather_streams(along, out, sems, (z, z), (slice(0, 16), slice(16, 32)))
    over_z = {}
    for h in range(2):
        a, b, to_a, to_b = grid_piece(along[h])
        for k in range(4):
            src = blocks(out, along[h], h, ALL, z, moved(b, k))
            over_z[h, k] = sems.copy(src, src, device(x, y, 1 - z, c, t))
    add = lambda name, task: tasks.add(f"{label}.{name}", task)

    def cross(*steps):
        for k in steps:
            sems.start(over_z[0, k], over_z[1, k])

    def init():
        mine.start()
        sems.start(swap)

    def own():
        mine.wait()
        swap.wait_recv()
        for p in streams:
            sems.start(p["a1f"], p["a1r"])

    def a2():
        for p in streams:
            p["a1f"].wait_recv()
            sems.start(p["a2"])

    def b1():
        for p in streams:
            p["a1r"].wait_recv()
            p["a2"].wait_recv()
            sems.start(p["b1f"], p["b1r"])
        cross(0)

    def b2():
        for p in streams:
            p["b1f"].wait_recv()
            sems.start(p["b2"])

    def zs():
        for p in streams:
            p["b1r"].wait_recv()
        cross(1, 3)

    def ze():
        for p in streams:
            p["b2"].wait_recv()
        cross(2)

    def end():
        for copy in over_z.values():
            copy.wait_recv()
        load.start()

    for task in (init, own, a2, b1, b2, zs, ze, end):
        add(task.__name__, task)


SCATTER_COPIES = 4 * 6 + 3
SCATTER_LOADS = 16


def scatter_slots(w):
    return [SHAPE((2, 2, 4, 32, w), HALF), SHAPE((2, 2, 2, 4, 32, w), HALF)]


def scatter_scratch(w):
    return [
        pltpu.VMEM((2, 2, 32, w), HALF),
        pltpu.VMEM((2, 2, 2, 32, w), HALF),
        pltpu.VMEM((2, 32, w), HALF),
        pltpu.VMEM((2, 32, w), SINGLE),
    ]


def scatter_shared(w):
    return [
        pltpu.VMEM((2, 2, 2, 4, 32, w), HALF),
        pltpu.VMEM((2, 2, 2, 4, 32, w), HALF),
        pltpu.VMEM((2, 2, 4, 32, w), HALF),
        pltpu.VMEM((2, 2, 2, 4, 32, w), HALF),
        pltpu.VMEM((2, 32, w), SINGLE),
    ]


def plus(ref, *others):
    total = ref[...].astype(SINGLE)
    for other in others:
        total = total + other[...].astype(SINGLE)
    ref[...] = total.astype(HALF)


class Scatter:
    def __init__(self, tasks, shared, sems, local):
        self.tasks, self.sems, self.local = tasks, sems, local
        self.sending, self.owned, self.temp_b, self.temp_a, self.final = shared
        self.count = 0
        self.busy = {}

    def take(self, key, copies):
        self.sems.sent(self.busy.get(key, []))
        self.busy[key] = copies

    def add(self, label, along, g, place, slots, scratch):
        sems, local = self.sems, self.local
        x, y, z, c, t = coords()
        slot = self.count % 2
        self.count += 1
        r2, r1 = slots
        q2, q1, rz, kept = scratch
        wide = slice(0, g.shape[-1])
        tt = self.sending.at[slot, :, :, :, :, wide]
        ss = self.owned.at[slot, :, :, :, :, wide]
        final = self.final.at[:, :, wide]
        streams = []
        for h in range(2):
            a, b, to_a, to_b = grid_piece(along[h])
            for s, zs, d in ((0, z, 1), (1, 1 - z, -1)):
                at_g = lambda bb, h=h, zs=zs: blocks(g, along[h], h, ALL, zs, bb)
                tmp_b, tmp_a = self.temp_b.at[h, s, :, :, wide], self.temp_a.at[h, s, :, :, :, wide]
                forward, back = to_b(moved(b, d)), to_b(moved(b, -d))
                own = ss.at[h, s]
                streams.append(
                    dict(
                        h=h,
                        s=s,
                        a=a,
                        d=d,
                        tt=tt.at[h, s],
                        ss=own,
                        tmp_b=tmp_b,
                        tmp_a=tmp_a,
                        load_t=local.copy(at_g(moved(b, d)), tt.at[h, s]),
                        load_s=local.copy(at_g(b), own),
                        load_2=local.copy(r2.at[h, s], tmp_b),
                        load_1=local.copy(r1.at[h, s], tmp_a),
                        x2=sems.copy(at_g(moved(b, 2)), r2.at[h, s], forward),
                        x1r=sems.copy(at_g(moved(b, -d)), r1.at[h, s, 1], back),
                        x1f=sems.copy(tt.at[h, s], r1.at[h, s, 0], forward),
                        y2=sems.copy(own.at[moved(a, 2)], q2.at[h, s], to_a(moved(a, d))),
                        y1r=sems.copy(own.at[moved(a, -d)], q1.at[h, s, 1], to_a(moved(a, -d))),
                        y1f=sems.copy(own.at[moved(a, d)], q1.at[h, s, 0], to_a(moved(a, d))),
                    )
                )
        over_z = [
            sems.copy(ss.at[h, 1, grid_piece(along[h])[0]], rz.at[h], device(x, y, 1 - z, c, t))
            for h in range(2)
        ]
        swap = sems.copy(final.at[1 - c], kept.at[1], device(x, y, z, 1 - c, t))

        def start():
            for p in streams:
                sems.start(p["x2"], p["x1r"])

        def x1a():
            self.take(("sending", slot), [p["x1f"] for p in streams])
            for p in streams:
                p["load_t"].start()
            for p in streams:
                p["x2"].wait_recv()
                p["load_2"].start()

        def x1b():
            for p in streams:
                p["load_t"].wait()
                p["load_2"].wait()

                def body(i, carry, p=p):
                    plus(p["tt"].at[i], p["tmp_b"].at[i])
                    return carry

                lax.fori_loop(0, 4, body, 0)
                sems.start(p["x1f"])

        def x0a():
            used = [p[name] for p in streams for name in ("y2", "y1r", "y1f")]
            self.take(("owned", slot), used + over_z)
            for p in streams:
                p["load_s"].start()
            for p in streams:
                p["x1r"].wait_recv()
                p["x1f"].wait_recv()
                p["load_1"].start()

        def x0b():
            for p in streams:
                p["load_s"].wait()
                p["load_1"].wait()

                def body(i, carry, p=p):
                    plus(p["ss"].at[i], p["tmp_a"].at[0, i], p["tmp_a"].at[1, i])
                    return carry

                lax.fori_loop(0, 4, body, 0)
                sems.start(p["y2"], p["y1r"])

        def y1():
            for p in streams:
                p["y2"].wait_recv()
                plus(p["ss"].at[moved(p["a"], p["d"])], q2.at[p["h"], p["s"]])
                sems.start(p["y1f"])

        def y0():
            for p in streams:
                h, s = p["h"], p["s"]
                p["y1f"].wait_recv()
                p["y1r"].wait_recv()
                plus(p["ss"].at[p["a"]], q1.at[h, s, 0], q1.at[h, s, 1])
                if s == 1:
                    sems.start(over_z[h])

        def last():
            self.take("final", [swap])
            for p in streams:
                h = p["h"]
                if p["s"] == 0:
                    over_z[h].wait_recv()
                    own = p["ss"].at[p["a"]]
                    final[h] = own[...].astype(SINGLE) + rz[h].astype(SINGLE)
            kept[0] = final[c]
            sems.start(swap)

        def done():
            swap.wait_recv()

            def read(j, start):
                lanes = slice(start, start + LANES)
                return jnp.where(c == j, kept[0, :, lanes], kept[1, :, lanes])

            place(read)

        for task in (start, x1a, x1b, x0a, x0b, y1, y0, last, done):
            self.tasks.add(f"{label}.{task.__name__}", task)


def make_grads(lhs, rhs, staging, g, local, first=0, width=None):
    sems = [local.sem() for _ in range(2)]
    width = width or g.shape[-1]
    wide = slice(0, width)

    def write(i, slot):
        return pltpu.make_async_copy(
            staging.at[slot, :, :, :, wide],
            g.at[i, slot, :, :, :, first : first + width],
            sems[slot],
        )

    def body(i, carry):
        for slot in range(2):
            n = pl.multiple_of(i * 512 + slot * 256, 256)
            left = lhs[:, :, pl.ds(n, 256)].reshape(512, 256)
            tile = product(left, rhs(), ((0,), (0,))).astype(HALF)

            @pl.when(i > 0)
            def _():
                write(i, slot).wait()

            staging[slot, :, :, :, wide] = tile.reshape(4, 2, 32, width)
            write(i, slot).start()
        return carry

    lax.fori_loop(0, 4, body, 0)
    for slot in range(2):
        write(0, slot).wait()


class FourSum:
    def __init__(self, bufs, sems):
        x, y, z, c, t = coords()
        self.to_core, self.from_core, self.from_pair, self.own = bufs
        self.sems = sems
        self.cols = [slice(i * PART, (i + 1) * PART) for i in range(PARTS)]
        core, pair = device(x, y, z, 1 - c, t), device(x, y, z, c, 1 - t)
        self.core = [sems.copy(self.to_core.at[:, n], self.from_core.at[:, n], core) for n in self.cols]
        self.pair = [sems.copy(self.from_core.at[:, n], self.from_pair.at[:, n], pair) for n in self.cols]

    def put(self, i, theirs, ours):
        self.to_core[:, self.cols[i]] = theirs.astype(HALF)
        self.own[:, self.cols[i]] = ours
        self.sems.start(self.core[i])

    def relay(self, i):
        n = self.cols[i]
        self.core[i].wait_recv()

        def add(r):
            self.from_core[r, n] = (self.own[r, n] + self.from_core[r, n].astype(SINGLE)).astype(HALF)

        row_loop(0, TOK, add, 64)
        self.sems.start(self.pair[i])

    def wait(self):
        for copy in self.pair:
            copy.wait_recv()

    def add_relays(self, tasks, label):
        for i in range(PARTS):
            tasks.add(f"{label}.relay{i}", lambda i=i: self.relay(i))

    def total(self, r):
        return self.from_core[r, :].astype(SINGLE) + self.from_pair[r, :].astype(SINGLE)


SUM_COPIES = 2 * PARTS
SUM_SCRATCH = [pltpu.VMEM((TOK, D), HALF) for _ in range(3)] + [pltpu.VMEM((TOK, D), SINGLE)]


def product(a, b, dims):
    return lax.dot_general(a, b, (dims, ((), ())), preferred_element_type=SINGLE)


def allowed_pairs(base):
    row = lax.broadcasted_iota(jnp.int32, (QB, KB), 0)
    col = lax.broadcasted_iota(jnp.int32, (QB, KB), 1)
    return (col > row) & (col <= row + WINDOW) & (col + base >= 0)


def attend_block(q, k, v, base):
    scores = product(q, k, ((1,), (1,))) * SCALE
    scores = jnp.where(allowed_pairs(base), scores, MASKED)
    row_max = jnp.max(scores, axis=-1, keepdims=True)
    expon = jnp.exp(scores - row_max)
    row_total = jnp.sum(expon, axis=-1, keepdims=True)
    probs = (expon * (1.0 / row_total)).astype(HALF)
    mixed = product(probs, v, ((1,), (0,))).astype(HALF)
    return mixed, row_max + jnp.log(row_total)


def attend_block_back(q, k, v, go, lse, base):
    scores = product(q, k, ((1,), (1,))) * SCALE
    scores = jnp.where(allowed_pairs(base), scores, MASKED)
    probs = jnp.exp(scores - lse)
    gp = product(go, v, ((1,), (1,)))
    inner = jnp.sum(probs * gp, axis=-1, keepdims=True)
    gs = (probs * (gp - inner)).astype(HALF)
    gq = product(gs, k, ((1,), (0,))) * SCALE
    gk = product(gs, q, ((0,), (0,))) * SCALE
    gv = product(probs.astype(HALF), go, ((0,), (0,)))
    return gq, gk, gv


def rms_inverse(values):
    return lax.rsqrt(jnp.mean(values * values, axis=-1, keepdims=True) + EPSILON)


def norm_back(grad, values, gain):
    inverse = rms_inverse(values)
    scaled = grad * gain
    slope = jnp.mean(scaled * values, axis=-1, keepdims=True)
    gain_term = jnp.sum(grad * values * inverse, axis=0, keepdims=True)
    return inverse * scaled - values * (inverse * inverse * inverse * slope), gain_term


def row_loop(start, count, fn, step=ROWS):
    def body(i, carry):
        fn(pl.ds(pl.multiple_of(start + i * step, step), step))
        return carry

    lax.fori_loop(0, count // step, body, 0)


def columns(w, n, size):
    return w[:, :, :, :, :, pl.ds(n, size)].reshape(D, size)


def pick_lanes():
    return lax.broadcasted_iota(jnp.int32, (8, LANES), 0) == lax.broadcasted_iota(
        jnp.int32, (8, LANES), 1
    )


def grid_of(w):
    return (4, 2, 4, 2, 32, w)


def params(collective_id):
    return pltpu.CompilerParams(
        collective_id=collective_id, has_side_effects=True, vmem_limit_bytes=VMEM_LIMIT
    )


CHUNKS = ("kv", "q", "out", "ffa", "ffb", "down")
W_KV, W_Q, W_OUT, W_FFA, W_FFB, W_DOWN = range(6)
WFA, WFB = 2048, 768
W_WIDTHS = (2 * HW + LANES, HW, HW, WFA, WFB, FF)
PIECES = {
    W_KV: [(2 * HW, LANES)] + [(n, 2 * HD) for n in range(0, 2 * HW, 2 * HD)],
    W_FFA: [(n, 2 * LANES) for n in range(0, WFA, 2 * LANES)],
    W_FFB: [(n, 2 * LANES) for n in range(0, WFB, 2 * LANES)],
}
ALONG = (0, 1)
ALONG_X = (1, 1)
FORWARD_ORDER = (
    0, 30, 20, 40, 10, 50, 61, 1, 11, 51, 3, 2, 52, 31, 4, 6, 53, 5, 12, 33, 54, 21, 13, 55, 16,
    22, 7, 17, 26, 56, 23, 8, 14, 18, 27, 32, 9, 58, 62, 24, 15, 63, 64, 65, 66, 28, 67, 36, 25,
    19, 68, 69, 29, 59, 34, 57, 60, 41, 82, 83, 70, 71, 42, 37, 35, 43, 72, 73, 74, 46, 75, 76,
    77, 78, 79, 38, 47, 44, 39, 80, 81, 48, 45, 84, 49, 85,
)


class Load:
    def __init__(self, src, dst, pieces, local):
        self.src, self.dst, self.pieces = src, dst, pieces
        self.first = local.used
        self.sems = local.sems
        for _ in pieces:
            local.sem()

    def copy(self, i, n, width):
        lanes = pl.ds(n, width)
        return pltpu.make_async_copy(
            self.src.at[:, :, :, :, :, lanes],
            self.dst.at[:, :, :, :, :, lanes],
            self.sems.at[self.first + i],
        )

    def start(self):
        for i, (n, width) in enumerate(self.pieces):
            self.copy(i, n, width).start()

    def wait(self, i, n=None):
        start, width = self.pieces[0] if n is not None else self.pieces[i]
        self.copy(i, start if n is None else n, width).wait()


class Exchange:
    def __init__(self, sems, mine, copies):
        self.sems, self.mine, self.copies = sems, mine, copies

    def start(self):
        self.mine.start()
        self.sems.start(*self.copies)

    def wait(self):
        self.mine.wait()
        for copy in self.copies:
            copy.wait_recv()


def exchange(sems, local, part, place):
    x, y, z, c, t = coords()
    copies = []
    for d in (2, 1, -1):
        to = moved(x, d)
        copies.append(sems.copy(part(to), place(x), device(to, y, z, c, t)))
    return Exchange(sems, local.copy(part(x), place(x)), copies)


def own_rows(start, v):
    return pl.ds(pl.multiple_of(start + v * 2 * TOK, 2 * TOK), 2 * TOK)


def head_lanes(v, width):
    return pl.ds(pl.multiple_of(v * width, width), width)


def block_rows(i):
    start = pl.multiple_of(i * QB, QB)
    return pl.ds(start, QB), pl.ds(start, KB)


def first_key(i):
    return lax.div(lax.axis_index("seq"), 8) * 2 * WINDOW - WINDOW + i * QB


def arrange(raw, chunks):
    gain_one, gain_two, query, key, value, out, gate, up, down = raw
    to_kv, to_q, to_out, to_ffa, to_ffb, to_down = chunks
    lane = lax.broadcasted_iota(jnp.int32, (32, LANES), 1)
    one, two = [jnp.broadcast_to(g[...], (LANES, 32)).T for g in (gain_one, gain_two)]
    gains = jnp.where(lane == 0, one, jnp.where(lane == 1, two, 0.0)).astype(HALF)
    for j in range(2):
        to_kv[j, :, 2 * HW :] = gains
        to_q[j] = query[:, j * HW : (j + 1) * HW].astype(HALF)
        for h in range(4):
            lanes = slice((4 * j + h) * HD, (4 * j + h + 1) * HD)
            to_kv[j, :, 2 * h * HD : (2 * h + 1) * HD] = key[:, lanes].astype(HALF)
            to_kv[j, :, (2 * h + 1) * HD : (2 * h + 2) * HD] = value[:, lanes].astype(HALF)
            to_out[j, :, h * HD : (h + 1) * HD] = out[:, lanes].astype(HALF)
    blocks_count = FF // LANES
    for j in range(2):
        for i in range(blocks_count):
            n = (j * blocks_count + i) * LANES
            last = min(n + LANES, gate.shape[1])
            parts = [w[:, n:last] for w in (gate, up, down)]
            if last < n + LANES:
                zeros = jnp.zeros((32, n + LANES - last), SINGLE)
                parts = [jnp.concatenate([part, zeros], axis=1) for part in parts]
            chunk, m = (to_ffa, 2 * i * LANES) if 2 * i * LANES < WFA else (to_ffb, 2 * i * LANES - WFA)
            chunk[j, :, m : m + LANES] = parts[0].astype(HALF)
            chunk[j, :, m + LANES : m + 2 * LANES] = parts[1].astype(HALF)
            to_down[j, :, i * LANES : (i + 1) * LANES] = parts[2].astype(HALF)


def forward_kernel(*refs):
    n_w = len(CHUNKS)
    raw_in, (hid, cot), rest = refs[:9], refs[9:11], refs[11:]
    w_out, kept, gains, rest = rest[:n_w], rest[n_w : n_w + 10], rest[n_w + 10], rest[n_w + 11 :]
    results, rest = rest[:10], rest[10:]
    a1, cots, q, kv, o, lse, mid, a2, hid_ff, grad_ff = results
    raw, w_in, rest = rest[:9], rest[9 : 9 + n_w], rest[9 + n_w :]
    weights, rest = rest[:n_w], rest[n_w:]
    w_kv, w_q, w_o, _, _, w_down = weights
    rows, ghid, kv_own, q_own, o_all = rest[:5]
    sum_bufs, (send, recv, local_sems) = rest[5:9], rest[9:]
    x, y, z, c, t = coords()
    core, pair = device(x, y, z, 1 - c, t), device(x, y, z, c, 1 - t)
    theirs, ours = [pl.ds(pl.multiple_of(k * TOK, TOK), TOK) for k in (1 - c, c)]
    sems, local = Sems(send, recv), Locals(local_sems)
    raw_loads = [local.load(src, dst) for src, dst in zip(raw_in, raw, strict=True)]
    stores = [local.copy(src, dst) for src, dst in zip(results, kept, strict=True)]
    partners = neighbours() + [pair, device(moved(x, 2), y, z, c, t), chip_shift(4), chip_shift(-4)]
    say_hello(partners)
    for load in raw_loads:
        load.wait()
    arrange(raw, w_in)
    hear_hello(partners)

    def store(*which):
        for i in which:
            stores[i].start()

    tasks = Tasks()
    loads = []
    for i, label in enumerate(CHUNKS):
        add = add_plane_gather if i == W_DOWN else add_gather
        along = ALONG_X if i == W_OUT else ALONG
        load = Load(w_out[i], weights[i], PIECES.get(i, [(0, W_WIDTHS[i])]), local)
        add(tasks, label, along, w_in[i], w_out[i], load, sems, local)
        loads.append(load)
    tasks.add("ldkv", lambda: loads[W_KV].wait(0))
    tasks.add("ldo", lambda: loads[W_OUT].wait(0))
    tasks.add("lddown", lambda: loads[W_DOWN].wait(0))

    row_copy, cot_copy = local.copy(hid, rows.at[c]), local.copy(cot, cots.at[c])
    row_swap, cot_swap = sems.copy(hid, rows.at[c], core), sems.copy(cot, cots.at[c], core)

    def swaps():
        row_copy.start()
        cot_copy.start()
        sems.start(row_swap, cot_swap)

    tasks.add("swaps", swaps)

    def norm():
        row_copy.wait()
        row_swap.wait_recv()
        pick = pick_lanes().astype(HALF)
        gains[...] = product(pick, columns(w_kv, 2 * HW, LANES), ((1,), (1,)))
        for half in range(2):

            def norm_one(r, half=half):
                values = rows[half, r, :].astype(SINGLE)
                a1[half, r, :] = (values * rms_inverse(values) * gains[0:1, :]).astype(HALF)

            row_loop(0, TOK, norm_one)
        store(0)

    tasks.add("norm", norm)

    def project(w, n):
        w_cols = columns(w, n, 2 * HD)
        return [product(a1[half], w_cols, ((1,), (0,))).astype(HALF) for half in range(2)]

    kv_swap = exchange(sems, local, lambda v: kv_own.at[v], lambda v: kv.at[own_rows(WINDOW, v)])
    q_swap = exchange(sems, local, lambda v: q_own.at[v], lambda v: q.at[own_rows(0, v)])
    o_swap = exchange(sems, local, lambda v: o_all.at[own_rows(0, v)], lambda v: o.at[:, head_lanes(v, HD)])
    halo = sems.copy(kv.at[2 * WINDOW : 3 * WINDOW], kv.at[0:WINDOW], chip_shift(4))
    for h in range(4):

        def project_kv(h=h):
            loads[W_KV].wait(1 + h)
            for half, out in enumerate(project(w_kv, h * 2 * HD)):
                kv_own[h, half * TOK : (half + 1) * TOK, :] = out

        tasks.add(f"proj{h}", project_kv)
    tasks.add("kva", kv_swap.start)

    def project_q():
        loads[W_Q].wait(0)
        for n in range(2):
            for half, out in enumerate(project(w_q, n * 2 * HD)):
                for k in range(2):
                    q_own[2 * n + k, half * TOK : (half + 1) * TOK, :] = out[
                        :, k * HD : (k + 1) * HD
                    ]
        q_swap.start()

    tasks.add("projq", project_q)

    def send_halo():
        kv_swap.wait()
        sems.start(halo)

    tasks.add("halo", send_halo)

    def attend_one(i, carry):
        mine, keys = block_rows(i)
        mixed, total = attend_block(
            q[mine, :], kv[keys, :HD], kv[keys, HD:], first_key(i)
        )
        o_all[mine, :] = mixed
        lse[mine, :] = jnp.broadcast_to(total, (QB, HD))
        return carry

    def attend_late():
        q_swap.wait()
        lax.fori_loop(4, 8, attend_one, 0)

    def attend_early():
        halo.wait_recv()
        lax.fori_loop(0, 4, attend_one, 0)
        o_swap.start()
        store(2, 3, 5)

    tasks.add("attA", attend_late)
    tasks.add("attB", attend_early)

    attended = FourSum(sum_bufs, sems)
    for i in range(PARTS):

        def put(i=i):
            if i == 0:
                o_swap.wait()
                store(4)
            w_rows = w_o[i].reshape(PART, HW)
            attended.put(i, *[product(o[r, :], w_rows, ((1,), (1,))) for r in (theirs, ours)])

        tasks.add(f"att.put{i}", put)
    attended.add_relays(tasks, "att")
    spreads = []
    for half in range(2):
        part = a2.at[c, half * 128 : (half + 1) * 128]
        spreads.append(sems.copy(part, part, core))

        def norm_two_half(half=half):
            if half == 0:
                attended.wait()

            def norm_two(r):
                values = rows[c, r, :].astype(SINGLE) + attended.total(r)
                mid[r, :] = values
                a2[c, r, :] = (values * rms_inverse(values) * gains[1:2, :]).astype(HALF)

            row_loop(half * 128, 128, norm_two)
            sems.start(spreads[half])

        tasks.add(f"norm2{half}", norm_two_half)

    def hidden_grads(first, count):
        def task():
            w_cols = columns(w_down, first, count)
            for half in range(2):
                r = slice(half * TOK, (half + 1) * TOK)
                ghid[r, first : first + count] = product(cots[half], w_cols, ((1,), (0,)))

        return task

    def hidden_grads_a():
        cot_copy.wait()
        cot_swap.wait_recv()
        store(1)
        for n in range(0, FFA // 2, 2 * LANES):
            hidden_grads(n, 2 * LANES)()

    def hidden_grads_b():
        for n in range(FFA // 2, FF, 2 * LANES):
            hidden_grads(n, min(2 * LANES, FF - n))()

    tasks.add("ghida", hidden_grads_a)
    tasks.add("ghidb", hidden_grads_b)

    def feed_forward(chunk, first, i, carry):
        n = pl.multiple_of(i * 2 * LANES, 2 * LANES)
        loads[chunk].wait(i, n)
        w_cols = columns(weights[chunk], n, 2 * LANES)
        gate_lanes = pl.ds(pl.multiple_of(first + n, 2 * LANES), LANES)
        up_lanes = pl.ds(pl.multiple_of(first + n + LANES, LANES), LANES)
        lanes = pl.ds(pl.multiple_of(first // 2 + i * LANES, LANES), LANES)
        for half in range(2):
            r = slice(half * TOK, (half + 1) * TOK)
            both = product(a2[half], w_cols, ((1,), (0,)))
            gate, up_part = both[:, :LANES], both[:, LANES:]
            sig = 1.0 / (1.0 + jnp.exp(-gate))
            hid_ff[r, lanes] = (gate * sig * up_part).astype(HALF)
            grad = ghid[r, lanes]
            grad_ff[r, gate_lanes] = (
                grad * up_part * sig * (1.0 + gate * (1.0 - sig))
            ).astype(HALF)
            grad_ff[r, up_lanes] = (grad * gate * sig).astype(HALF)
        return carry

    pairs_a, pairs = WFA // (2 * LANES), FF // LANES

    def feed_forward_a():
        for copy in spreads:
            copy.wait_recv()
        store(6, 7)
        lax.fori_loop(0, pairs_a, lambda i, carry: feed_forward(W_FFA, 0, i, carry), 0)

    def feed_forward_b():
        lax.fori_loop(
            0, pairs - pairs_a, lambda i, carry: feed_forward(W_FFB, WFA, i, carry), 0
        )
        store(8, 9)

    tasks.add("gua", feed_forward_a)
    tasks.add("gub", feed_forward_b)
    tasks.run(FORWARD_ORDER)
    for copy in stores:
        copy.wait()
    sems.finish()


def forward(raw, hid, cot):
    n = len(CHUNKS)
    copies = GATHER_COPIES * n + 2 + 3 * 3 + 1 + SUM_COPIES + 2
    kept = [
        ((2, TOK, D), HALF),
        ((2, TOK, D), HALF),
        ((2 * WINDOW, HD), HALF),
        ((3 * WINDOW, 2 * HD), HALF),
        ((2 * TOK, HW), HALF),
        ((2 * WINDOW, HD), SINGLE),
        ((TOK, D), SINGLE),
        ((2, TOK, D), HALF),
        ((2 * TOK, FF), HALF),
        ((2 * TOK, 2 * FF), HALF),
    ]
    return pl.pallas_call(
        forward_kernel,
        out_shape=[SHAPE(grid_of(w), HALF) for w in W_WIDTHS]
        + [SHAPE(*k) for k in kept]
        + [SHAPE((8, D), SINGLE)],
        in_specs=[ANYWHERE] * (len(raw) + 2),
        out_specs=[ANYWHERE] * (n + len(kept)) + [IN_VMEM],
        scratch_shapes=[pltpu.VMEM(*k) for k in kept]
        + [pltpu.VMEM(w.shape, SINGLE) for w in raw]
        + [pltpu.VMEM((2, 32, w), HALF) for w in W_WIDTHS]
        + [pltpu.VMEM(grid_of(w), HALF) for w in W_WIDTHS]
        + [
            pltpu.VMEM((2, TOK, D), HALF),
            pltpu.VMEM((2 * TOK, FF), SINGLE),
            pltpu.VMEM((4, 2 * TOK, 2 * HD), HALF),
            pltpu.VMEM((4, 2 * TOK, HD), HALF),
            pltpu.VMEM((2 * WINDOW, HD), HALF),
        ]
        + SUM_SCRATCH
        + [
            pltpu.SemaphoreType.DMA((copies,)),
            pltpu.SemaphoreType.DMA((copies,)),
            pltpu.SemaphoreType.DMA((2 * n + sum(len(p) for p in PIECES.values()) + 5 + len(raw) + len(kept),)),
        ],
        compiler_params=params(0),
    )(*raw, hid, cot)


GRADS = ("down", "ffa", "ffb", "oq", "kv", "gain")
G_DOWN, G_FFA, G_FFB, G_OQ, G_KV, G_GAIN = range(6)
G_WIDTHS = (FF, FFA, FFB, 2 * HW, 2 * HW, LANES)
BACKWARD_ORDER = (
    54, 0, 55, 56, 57, 58, 64, 1, 2, 59, 60, 63, 61, 62, 9, 3, 4, 10, 11, 65, 66, 5, 67, 18, 12,
    13, 6, 68, 7, 69, 19, 20, 73, 14, 8, 74, 75, 76, 77, 78, 79, 80, 71, 70, 27, 21, 22, 15, 81,
    82, 83, 89, 84, 85, 16, 28, 29, 86, 87, 88, 17, 72, 23, 36, 30, 31, 24, 37, 38, 90, 91, 25,
    32, 26, 45, 39, 40, 33, 46, 47, 41, 34, 48, 49, 42, 35, 50, 51, 43, 52, 44, 53,
)


def backward_kernel(*refs):
    n_w, n_g = len(CHUNKS), len(GRADS)
    w_kv, w_q, w_out, w_ffa, w_ffb, w_down = refs[:n_w]
    rest = refs[n_w:]
    a1_in, cots, q_in, kv_in, o_in, lse_in, mid_in, a2_in, hid_in, grad_ff_in, rows_in, gains = rest[:12]
    rest = rest[12:]
    s_query, s_key, s_value, s_out, s_gate, s_up, s_down, s_one, s_two, in_grad, hidden_out = rest[:11]
    rest = rest[11:]
    g_refs, slots, rest = rest[:n_g], rest[n_g : 3 * n_g], rest[3 * n_g :]
    scratch, rest = rest[: 4 * n_g], rest[4 * n_g :]
    shared, rest = rest[:5], rest[5:]
    to_core, own_sum, rest = rest[0], rest[1], rest[2:]
    gn2_bufs, gn1_bufs, out_bufs, rest = rest[:2], rest[2:4], rest[4:6], rest[6:]
    (
        staging,
        cot_v,
        gatt,
        rows_v,
        hid_ff,
        grad_ff,
        mid,
        q,
        kv,
        lse,
        o,
        tiles,
        go,
        go_all,
        acc,
        far,
        got,
        gq_all,
        gkv_all,
        gq,
        gkv,
        gain_acc,
        send,
        recv,
        local_sems,
    ) = rest
    x, y, z, c, t = coords()
    core, pair = device(x, y, z, 1 - c, t), device(x, y, z, c, 1 - t)
    sems, local = Sems(send, recv), Locals(local_sems)
    theirs, ours = [pl.ds(pl.multiple_of(k * TOK, TOK), TOK) for k in (1 - c, c)]
    tasks = Tasks()

    def tile_loads(*sources):
        loads = []
        for i in range(8):
            copies, n = [], 0
            for source, width in sources:
                copies.append(
                    local.copy(
                        source.at[i // 2, i % 2, :, :, :, 0:width],
                        tiles.at[i % 2, :, :, :, n : n + width],
                    )
                )
                n += width
            loads.append(copies)
        return loads

    def begin(*loads):
        for copies in loads:
            for copy in copies:
                copy.start()

    def tile(k, start, width):
        return tiles[k, :, :, :, start : start + width].reshape(256, width)

    def add_sum(label, bufs, loads, multiply, last=None, then=None):
        total = FourSum([to_core, *bufs, own_sum], sems)
        for i in range(PARTS):

            def put(i=i):
                if i == 0 and last is not None:
                    sems.sent(last.core)
                parts = []
                for k in range(2):
                    for copy in loads[2 * i + k]:
                        copy.wait()
                    parts.append([multiply(r, k) for r in (theirs, ours)])
                    if 2 * i + k + 2 < 8:
                        begin(loads[2 * i + k + 2])
                total.put(
                    i, *[jnp.concatenate([parts[0][j], parts[1][j]], axis=1) for j in range(2)]
                )
                if i == PARTS - 1 and then is not None:
                    then()

            tasks.add(f"{label}.put{i}", put)
        total.add_relays(tasks, label)
        return total

    partners = neighbours() + [pair, device(moved(x, 2), y, z, c, t), chip_shift(4), chip_shift(-4)]
    say_hello(partners)
    load_cot, load_hid = local.load(cots, cot_v), local.load(hid_in, hid_ff)
    load_grad = local.load(grad_ff_in, grad_ff)
    ff_loads = tile_loads((w_ffa, WFA), (w_ffb, WFB))
    begin(ff_loads[0], ff_loads[1])
    load_a2 = local.load(a2_in, rows_v)
    later = [
        local.load(src, dst)
        for src, dst in (
            (mid_in, mid),
            (q_in, q),
            (kv_in, kv),
            (lse_in, lse),
            (o_in, o),
        )
    ]
    load_a1 = local.copy(a1_in, rows_v)
    out_loads = [
        local.copy(
            w_out.at[i // 2, i % 2], tiles.at[i // 4, :, :, :, (i % 4) * HW : (i % 4 + 1) * HW]
        )
        for i in range(8)
    ]
    down_loads = tile_loads((w_down, FF))
    qkv_loads = tile_loads((w_q, HW), (w_kv, 2 * HW))

    def place_plain(target, width, read):
        for j in range(2):
            for n in range(0, width, LANES):
                start = j * width + n
                lanes = min(LANES, target.shape[1] - start)
                target[:, start : start + lanes] = read(j, n)[:, :lanes]

    def place_ff(first, width, read):
        for j in range(2):
            for n in range(0, width, 2 * LANES):
                start = j * FF + (first + n) // 2
                lanes = min(LANES, s_gate.shape[1] - start)
                s_gate[:, start : start + lanes] = read(j, n)[:, :lanes]
                s_up[:, start : start + lanes] = read(j, n + LANES)[:, :lanes]

    def place_oq(read):
        place_plain(s_out, HW, read)
        place_plain(s_query, HW, lambda j, n: read(j, HW + n))

    def place_kv(read):
        for j in range(2):
            for h in range(4):
                lanes = slice((4 * j + h) * HD, (4 * j + h + 1) * HD)
                s_key[:, lanes] = read(j, 2 * h * HD)
                s_value[:, lanes] = read(j, (2 * h + 1) * HD)

    def place_gain(read):
        total = (read(0, 0) + read(1, 0)).T
        s_one[...] = total[0:1]
        s_two[...] = total[1:2]

    place = (
        lambda read: place_plain(s_down, FF, read),
        lambda read: place_ff(0, FFA, read),
        lambda read: place_ff(FFA, FFB, read),
        place_oq,
        place_kv,
        place_gain,
    )
    scatter = Scatter(tasks, shared, sems, local)
    for i, label in enumerate(GRADS):
        scatter.add(
            label,
            ALONG,
            g_refs[i],
            place[i],
            slots[2 * i : 2 * i + 2],
            scratch[4 * i : 4 * i + 4],
        )
    waited = set()

    def once(load):
        if id(load) not in waited:
            waited.add(id(load))
            load.wait()

    def grad_down():
        once(load_cot)
        once(load_hid)
        make_grads(cot_v, lambda: hid_ff[...], staging, g_refs[G_DOWN], local)
        hear_hello(partners)

    tasks.add("gdown", grad_down)

    def multiply_ff(r, k):
        once(load_grad)
        return product(grad_ff[r, :], tile(k, 0, 2 * FF), ((1,), (1,)))

    gn2 = add_sum("gn2", gn2_bufs, ff_loads, multiply_ff, None, lambda: begin(out_loads))

    def grad_ffa():
        once(load_a2)
        make_grads(rows_v, lambda: grad_ff[:, :FFA], staging, g_refs[G_FFA], local)

    def grad_ffb():
        once(load_a2)
        make_grads(rows_v, lambda: grad_ff[:, FFA:], staging, g_refs[G_FFB], local)

    tasks.add("gffa", grad_ffa)
    tasks.add("gffb", grad_ffb)
    spreads = []
    for half in range(2):
        part = gatt.at[c, half * 128 : (half + 1) * 128]
        spreads.append(sems.copy(part, part, core))

        def mid_back_half(half=half):
            if half == 0:
                gn2.wait()
                for load in later:
                    load.wait()
                gain_acc[...] = jnp.zeros_like(gain_acc)

            def mid_back(r):
                part, term = norm_back(gn2.total(r), mid[r, :], gains[1:2, :])
                grad = cot_v[c, r, :].astype(SINGLE) + part
                in_grad[r, :] = grad
                gatt[c, r, :] = grad.astype(HALF)
                gain_acc[1:2, :] += term

            row_loop(half * 128, 128, mid_back)
            sems.start(spreads[half])

        tasks.add(f"mid{half}", mid_back_half)

    def attended_back():
        for copy in out_loads:
            copy.wait()
        for copy in spreads:
            copy.wait_recv()
        for half in range(2):
            total = jnp.zeros((TOK, HW), SINGLE)
            for i in range(8):
                total += product(
                    gatt[half, :, i * 256 : (i + 1) * 256],
                    tile(i // 4, (i % 4) * HW, HW),
                    ((1,), (0,)),
                )
            go[half * TOK : (half + 1) * TOK, :] = total.astype(HALF)
        go_swap.start()
        begin(down_loads[0], down_loads[1])

    tasks.add("go", attended_back)

    go_swap = exchange(
        sems, local, lambda v: go.at[:, head_lanes(v, HD)], lambda v: go_all.at[own_rows(0, v)]
    )
    gq_swap = exchange(
        sems, local, lambda v: gq_all.at[own_rows(0, v)], lambda v: gq.at[:, head_lanes(v, HD)]
    )
    gkv_swap = exchange(
        sems,
        local,
        lambda v: gkv_all.at[own_rows(0, v)],
        lambda v: gkv.at[:, head_lanes(v, 2 * HD)],
    )
    back = sems.copy(far, got, chip_shift(-4))

    def attend_one(i, carry):
        mine, keys = block_rows(i)
        grad_q, grad_k, grad_v = attend_block_back(
            q[mine, :], kv[keys, :HD], kv[keys, HD:], go_all[mine, :], lse[mine, 0:1], first_key(i)
        )
        gq_all[mine, :] = grad_q.astype(HALF)
        acc[keys, :HD] += grad_k
        acc[keys, HD:] += grad_v
        return carry

    def attend_early():
        load_a1.start()
        acc[...] = jnp.zeros_like(acc)
        go_swap.wait()
        lax.fori_loop(0, 4, attend_one, 0)
        far[...] = acc[0:WINDOW, :].astype(HALF)
        sems.start(back)

    def attend_late():
        lax.fori_loop(4, 8, attend_one, 0)
        gq_swap.start()

    def add_back():
        back.wait_recv()

        def keep(r):
            gkv_all[r, :] = acc[pl.ds(pl.multiple_of(WINDOW + r.start, 64), 64), :].astype(HALF)

        def add(r):
            total = acc[pl.ds(pl.multiple_of(2 * WINDOW + r.start, 64), 64), :]
            total = total + got[r, :].astype(SINGLE)
            gkv_all[pl.ds(pl.multiple_of(WINDOW + r.start, 64), 64), :] = total.astype(HALF)

        row_loop(0, WINDOW, keep, 64)
        row_loop(0, WINDOW, add, 64)
        gkv_swap.start()

    tasks.add("attbA", attend_early)
    tasks.add("attbB", attend_late)
    tasks.add("gadd", add_back)

    def once_arrived(swap):
        if id(swap) not in waited:
            waited.add(id(swap))
            swap.wait()

    def grad_oq():
        once(load_a1)
        once_arrived(gq_swap)
        make_grads(gatt, lambda: o[...], staging, g_refs[G_OQ], local, 0, HW)
        make_grads(rows_v, lambda: gq[...], staging, g_refs[G_OQ], local, HW, HW)

    def grad_kv():
        once(load_a1)
        once_arrived(gkv_swap)
        make_grads(rows_v, lambda: gkv[...], staging, g_refs[G_KV], local)

    tasks.add("goq", grad_oq)
    tasks.add("gkv", grad_kv)
    out_sum = add_sum(
        "out",
        out_bufs,
        down_loads,
        lambda r, k: product(hid_ff[r, :], tile(k, 0, FF), ((1,), (1,))),
        gn2,
        lambda: begin(qkv_loads[0], qkv_loads[1]),
    )

    def multiply_qkv(r, k):
        once_arrived(gq_swap)
        once_arrived(gkv_swap)
        from_q = product(gq[r, :], tile(k, 0, HW), ((1,), (1,)))
        return from_q + product(gkv[r, :], tile(k, HW, 2 * HW), ((1,), (1,)))

    gn1 = add_sum(
        "gn1",
        gn1_bufs,
        qkv_loads,
        multiply_qkv,
        out_sum,
    )

    def rows_out():
        out_sum.wait()

        def add(r):
            hidden_out[r, :] = (mid[r, :] + out_sum.total(r)).astype(HALF)

        row_loop(0, TOK, add)

    load_rows = local.copy(rows_in, to_core)

    def rows_back():
        sems.sent(gn1.core)
        load_rows.start()
        gn1.wait()
        load_rows.wait()

        def add(r):
            part, term = norm_back(gn1.total(r), to_core[r, :].astype(SINGLE), gains[0:1, :])
            in_grad[r, :] = in_grad[r, :] + part
            gain_acc[0:1, :] += term

        row_loop(0, TOK, add)

    tasks.add("rowsout", rows_out)
    tasks.add("rowsback", rows_back)

    def grad_gain():
        pick = pick_lanes().astype(HALF)
        writes = []
        for n in range(8):
            lanes = slice(n * LANES, (n + 1) * LANES)
            cols = product(gain_acc[:, n * 256 : (n + 1) * 256].astype(HALF), pick, ((0,), (0,)))
            staging[0, :, :, :, lanes] = cols.astype(HALF).reshape(4, 2, 32, LANES)
            writes.append(
                local.load(staging.at[0, :, :, :, lanes], g_refs[G_GAIN].at[n // 2, n % 2])
            )
        for copy in writes:
            copy.wait()

    tasks.add("ggain", grad_gain)
    tasks.run(BACKWARD_ORDER)
    sems.finish()


def backward(hidden_units, *operands):
    n = len(GRADS)
    copies = SCATTER_COPIES * n + SUM_COPIES * 3 + 2 + 3 * 3 + 1
    loads = 11 + 8 * (2 + 1 + 1 + 2) + SCATTER_LOADS * n + 2 * 6 + 8 + 3
    slots = [slot for w in G_WIDTHS for slot in scatter_slots(w)]
    widest = max(G_WIDTHS)
    results = [(32, 2 * HW)] * 4 + [(32, hidden_units)] * 3 + [(1, 32)] * 2
    rows_half = pltpu.VMEM((TOK, D), HALF)
    return pl.pallas_call(
        backward_kernel,
        out_shape=[SHAPE(s, SINGLE) for s in results]
        + [SHAPE((TOK, D), SINGLE), SHAPE((TOK, D), HALF)]
        + [SHAPE(grid_of(w), HALF) for w in G_WIDTHS]
        + slots,
        in_specs=[ANYWHERE] * (len(operands) - 1) + [IN_VMEM],
        out_specs=[IN_VMEM] * (len(results) + 2) + [ANYWHERE] * (n + len(slots)),
        scratch_shapes=[buf for w in G_WIDTHS for buf in scatter_scratch(w)]
        + scatter_shared(widest)
        + [rows_half, pltpu.VMEM((TOK, D), SINGLE)]
        + [rows_half] * 6
        + [
            pltpu.VMEM((2, 4, 2, 32, widest), HALF),
            pltpu.VMEM((2, TOK, D), HALF),
            pltpu.VMEM((2, TOK, D), HALF),
            pltpu.VMEM((2, TOK, D), HALF),
            pltpu.VMEM((2 * TOK, FF), HALF),
            pltpu.VMEM((2 * TOK, 2 * FF), HALF),
            pltpu.VMEM((TOK, D), SINGLE),
            pltpu.VMEM((2 * WINDOW, HD), HALF),
            pltpu.VMEM((3 * WINDOW, 2 * HD), HALF),
            pltpu.VMEM((2 * WINDOW, HD), SINGLE),
            pltpu.VMEM((2 * TOK, HW), HALF),
            pltpu.VMEM((2, 4, 2, 32, 2 * FF), HALF),
            pltpu.VMEM((2 * TOK, HW), HALF),
            pltpu.VMEM((2 * WINDOW, HD), HALF),
            pltpu.VMEM((3 * WINDOW, 2 * HD), SINGLE),
            pltpu.VMEM((WINDOW, 2 * HD), HALF),
            pltpu.VMEM((WINDOW, 2 * HD), HALF),
            pltpu.VMEM((2 * WINDOW, HD), HALF),
            pltpu.VMEM((2 * WINDOW, 2 * HD), HALF),
            pltpu.VMEM((2 * TOK, HW), HALF),
            pltpu.VMEM((2 * TOK, 2 * HW), HALF),
            pltpu.VMEM((8, D), SINGLE),
            pltpu.SemaphoreType.DMA((copies,)),
            pltpu.SemaphoreType.DMA((copies,)),
            pltpu.SemaphoreType.DMA((loads,)),
        ],
        compiler_params=params(1),
    )(*operands)


def hand_over_kernel(count, *refs):
    ins, outs, refs = refs[:count], refs[count : 2 * count], refs[2 * count :]
    held, sems = refs[:count], refs[count]
    load = [pltpu.make_async_copy(ins[i], held[i], sems.at[0, i]) for i in range(count)]
    store = [pltpu.make_async_copy(held[i], outs[i], sems.at[1, i]) for i in range(count)]
    for copy in load:
        copy.start()
    for i in range(count):
        load[i].wait()
        store[i].start()
    for copy in store:
        copy.wait()


def hand_over(*arrays):
    n = len(arrays)
    return pl.pallas_call(
        functools.partial(hand_over_kernel, n),
        out_shape=[SHAPE(a.shape, a.dtype) for a in arrays],
        in_specs=[ANYWHERE] * n,
        out_specs=[ANYWHERE] * n,
        scratch_shapes=[pltpu.VMEM(a.shape, a.dtype) for a in arrays]
        + [pltpu.SemaphoreType.DMA((2, n))],
        compiler_params=pltpu.CompilerParams(vmem_limit_bytes=VMEM_LIMIT),
    )(*arrays)


def per_device(
    hidden_in, attn_gain, w_query, w_key, w_value, w_out, ffn_gain, w_gate, w_up, w_down, out_grad
):
    weights = (w_query, w_key, w_value, w_out.T, w_gate, w_up, w_down.T)
    gains = (attn_gain.reshape(1, -1), ffn_gain.reshape(1, -1))
    *kept, gain_rows = forward((*gains, *weights), hidden_in, out_grad)
    results = backward(w_gate.shape[1], *kept, hidden_in, gain_rows)[:11]
    s_query, s_key, s_value, s_out, s_gate, s_up, s_down, s_one, s_two, in_grad, hidden_out = hand_over(
        *results
    )
    return (
        hidden_out,
        in_grad,
        s_one.reshape(-1),
        s_query,
        s_key,
        s_value,
        s_out.T,
        s_two.reshape(-1),
        s_gate,
        s_up,
        s_down.T,
    )


def solution(mesh):
    placed = (
        P("seq", None),
        P("seq"),
        P("seq", "tp"),
        P("seq", "tp"),
        P("seq", "tp"),
        P("tp", "seq"),
        P("seq"),
        P("seq", "tp"),
        P("seq", "tp"),
        P("tp", "seq"),
        P("seq", None),
    )
    return jax.shard_map(
        per_device,
        mesh=mesh,
        in_specs=placed,
        out_specs=(
            P("seq", None),
            P("seq", None),
            P("seq"),
            P("seq", "tp"),
            P("seq", "tp"),
            P("seq", "tp"),
            P("tp", "seq"),
            P("seq"),
            P("seq", "tp"),
            P("seq", "tp"),
            P("tp", "seq"),
        ),
        check_vma=False,
    )
```
